512 devices in a mesh: gz: 16 (over z, core), xy: 32 (over x, y).
Axes of the slice: x: 4, y: 8, z: 8, core: 2. Of those that a mesh axis runs over, the one named last changes fastest.
Arguments:
- tile_image: bfloat16 [16, 32, 4, 4, 2, 128], P('gz', 'xy'), may hold values from -6 to 6
- tile_target: bfloat16 [16, 32, 4, 3, 4, 2, 128], P('gz', 'xy'), may hold values from 0 to 1
- owner_counts: int32 [16, 32], P('gz', 'xy'), may hold values from 0 to 4, as said below
- tile_list: int32 [16, 32, 4], P('gz', 'xy'), may hold values from -1 to 63, as said below
- w_in: bfloat16 [27, 32], replicated, may hold values from -1.25 to 1.25
- w_res: bfloat16 [27, 32, 32], replicated, may hold values from -0.21875 to 0.21875
- w_down: bfloat16 [8, 64, 32], replicated, may hold values from -0.375 to 0.375
- w_mid: bfloat16 [27, 64, 64], replicated, may hold values from -0.15625 to 0.15625
- w_up: bfloat16 [8, 32, 64], replicated, may hold values from -0.75 to 0.75
- head_weight: bfloat16 [3, 32], replicated, may hold values from -1 to 1
Outputs:
- err_tiles: bfloat16 [16, 32, 4, 3, 4, 2, 128], P('gz', 'xy')
- grad_in: float32 [27, 32], replicated
- grad_res: float32 [27, 32, 32], replicated
- grad_down: float32 [8, 64, 32], replicated
- grad_mid: float32 [27, 64, 64], replicated
- grad_up: float32 [8, 32, 64], replicated
- head_weight_gradient: float32 [3, 32], replicated
The draws below stay inside these ranges and needn't reach their ends.
Inputs may be any that keep to these rules, and one draw needn't show every extreme that they name: `owner_counts`: in each depth row the counts add up to 64, and some owner of every row holds exactly 4 tiles. `tile_list`: in each depth row the live slots (s < owner_counts) name every position 0 to 63 exactly once; the other slots hold -1.
All inputs are finite; a program needn't handle non-finite values.
Results may differ from the reference program's by a relative error of at most 0.0046.
Values may be sent and summed in bfloat16 or wider, within the bound.
A program may use at most 64 MiB of HBM per device.

```python
import jax
import jax.numpy as jnp
from jax import lax

CH0 = 32
CH1 = 64
CZ = 4
CY = 2
TX = 128
TPD = 2
MAXT = 4
TOT = 64
NZ = 64
NX = 8192
SLAB_VOXELS = 1048576
N_GZ = 16
N_XY = 32


def owner_plan(key):
    base = jax.random.fold_in(key, 101)
    row_keys = jax.random.split(base, N_GZ)

    def one_row(row_key):
        key_order, key_delta, key_place = jax.random.split(row_key, 3)
        order = jax.random.permutation(key_order, N_XY)
        delta = jax.random.randint(key_delta, (N_XY // 2,), -TPD, TPD + 1)
        delta = delta.at[0].set(MAXT - TPD)
        counts = jnp.zeros((N_XY,), jnp.int32)
        counts = counts.at[order[0::2]].set(TPD + delta).at[order[1::2]].set(TPD - delta)
        places = jax.random.permutation(key_place, N_XY * TPD).astype(jnp.int32)
        offsets = jnp.cumsum(counts) - counts
        slots = jnp.arange(MAXT, dtype=jnp.int32)
        index = jnp.clip(offsets[:, None] + slots[None, :], 0, N_XY * TPD - 1)
        listing = jnp.where(slots[None, :] < counts[:, None], places[index], -1)
        return (counts.astype(jnp.int32), listing.astype(jnp.int32))
    return jax.vmap(one_row)(row_keys)


def draw_owner_counts(key, part):
    return owner_plan(key)[0]


def draw_tile_list(key, part):
    return owner_plan(key)[1]


def draw_tile_target(key, part):
    key_kind, key_rough = jax.random.split(jax.random.fold_in(key, 202))
    kind = jax.random.randint(key_kind, (N_GZ, N_XY, MAXT, 3, 1, 1, 1), 0, 2).astype(jnp.float32)
    rough = jax.random.uniform(key_rough, (N_GZ, N_XY, MAXT, 3, CZ, CY, TX), jnp.float32)
    width_part = 0.1
    high = 1.0 - width_part * rough
    low = width_part * rough
    return (kind * high + (1.0 - kind) * low).astype(jnp.bfloat16)


def steps_of(rng, dims, shards, least, top_value):
    factor_of = 1.0
    for axis_at, shards_of in shards:
        steps = jax.random.uniform(jax.random.fold_in(jax.random.fold_in(rng, 6), axis_at), (shards_of,), jnp.float32, least / len(shards), top_value / len(shards))
        factor_of = factor_of * jnp.repeat(jnp.exp(steps), dims[axis_at] // shards_of).reshape((-1,) + (1,) * (len(dims) - 1 - axis_at))
    return factor_of


def bell_draw(rng, extent, scale, limit, pieces=(), held_as=jnp.bfloat16):
    factor_of = steps_of(rng, extent, pieces, -0.22, 0.18) if pieces else 1.0
    values = jax.random.normal(rng, extent, jnp.float32) * scale * factor_of
    return jnp.minimum(jnp.maximum(values, -limit), limit).astype(held_as)


def setup_inputs(seed: int = 0) -> dict:
    splits = jax.random.split(jax.random.key(seed), 11)
    return {
        "tile_image": bell_draw(splits[0], (N_GZ, N_XY, MAXT, CZ, CY, TX), 1.0, 6.0, ((0, 16), (1, 32))),
        "tile_target": draw_tile_target(jax.random.fold_in(splits[10], 71), 0),
        "owner_counts": draw_owner_counts(jax.random.fold_in(splits[10], 71), 0),
        "tile_list": draw_tile_list(jax.random.fold_in(splits[10], 71), 0),
        "w_in": bell_draw(splits[4], (27, CH0), 27 ** -0.5, 1.25),
        "w_res": bell_draw(splits[5], (27, CH0, CH0), (27 * CH0) ** -0.5, 0.21875),
        "w_down": bell_draw(splits[6], (8, CH1, CH0), (8 * CH0) ** -0.5, 0.375),
        "w_mid": bell_draw(splits[7], (27, CH1, CH1), (27 * CH1) ** -0.5, 0.15625),
        "w_up": bell_draw(splits[8], (8, CH0, CH1), CH1 ** -0.5, 0.75),
        "head_weight": bell_draw(splits[9], (3, CH0), CH0 ** -0.5, 1.0),
    }


def convolve(field, weights):
    kernel = weights.reshape(3, 3, 3, weights.shape[1], weights.shape[2]).transpose(3, 4, 0, 1, 2)
    result = lax.conv_general_dilated(field[None], kernel, (1, 1, 1), ((1, 1), (1, 1), (1, 1)),
                                      dimension_numbers=("NCDHW", "OIDHW", "NCDHW"),
                                      preferred_element_type=jnp.float32)
    return result[0]


def flipped(weights):
    return jnp.transpose(weights[::-1], (0, 2, 1))


def tap_grads(grad, field):
    padded = jnp.pad(field, ((0, 0), (1, 1), (1, 1), (1, 1)))
    depth, height, width = grad.shape[1:]
    grad_f = grad.astype(jnp.float32)
    terms = []
    for tap in range(27):
        off_z, off_y, off_x = tap // 9, (tap // 3) % 3, tap % 3
        window = padded[:, off_z:off_z + depth, off_y:off_y + height, off_x:off_x + width].astype(jnp.float32)
        terms.append(jnp.einsum("ozyx,czyx->oc", grad_f, window))
    return jnp.stack(terms)


def strided(field, tap):
    return field[:, tap // 4::2, (tap // 2) % 2::2, tap % 2::2]


def alternate(parts):
    chans, depth, height, width = parts.shape[1:]
    return parts.reshape(2, 2, 2, chans, depth, height, width).transpose(3, 4, 0, 5, 1, 6, 2).reshape(
        chans, 2 * depth, 2 * height, 2 * width)


def selector(counts_row, list_row):
    live = jnp.arange(MAXT)[None, :] < counts_row[:, None]
    match = (list_row.reshape(-1)[None, :] == jnp.arange(TOT)[:, None]) & live.reshape(-1)[None, :]
    return match.astype(jnp.float32)


def reference(tile_image, tile_target, owner_counts, tile_list, w_in, w_res, w_down, w_mid, w_up, head_weight):
    single_float = jnp.float32
    brain_float_half = jnp.bfloat16
    hi = lax.Precision.HIGHEST
    image_rows = []
    target_rows = []
    selects = []
    for row in range(N_GZ):
        select = selector(owner_counts[row], tile_list[row])
        selects.append(select)
        flat_img = tile_image[row].reshape((N_XY * MAXT, CZ, CY, TX)).astype(single_float)
        flat_tgt = tile_target[row].reshape((N_XY * MAXT, 3, CZ, CY, TX)).astype(single_float)
        image_rows.append(jnp.tensordot(select, flat_img, axes=1, precision=hi))
        target_rows.append(jnp.tensordot(select, flat_tgt, axes=1, precision=hi))
    image = jnp.stack(image_rows).transpose(0, 2, 3, 1, 4).reshape(1, NZ, CY, NX).astype(brain_float_half)
    target = jnp.stack(target_rows).transpose(2, 0, 3, 4, 1, 5).reshape(3, NZ, CY, NX).astype(brain_float_half)

    h0 = jax.nn.relu(convolve(image, w_in[:, :, None])).astype(brain_float_half)
    h1 = jax.nn.relu(h0.astype(single_float) + convolve(h0, w_res)).astype(brain_float_half)
    down_sum = sum(jnp.einsum("oc,czyx->ozyx", w_down[tap].astype(single_float), strided(h1, tap).astype(single_float)) for tap in range(8))
    dfield = jax.nn.relu(down_sum).astype(brain_float_half)
    cfield = jax.nn.relu(dfield.astype(single_float) + convolve(dfield, w_mid)).astype(brain_float_half)
    upward = alternate(jnp.stack([jnp.einsum("oc,czyx->ozyx", w_up[tap].astype(single_float), cfield.astype(single_float)) for tap in range(8)]))
    signal_field = jax.nn.relu(h1.astype(single_float) + upward).astype(brain_float_half)
    logits = jnp.einsum("ac,czyx->azyx", head_weight.astype(single_float), signal_field.astype(single_float))
    affinity_map = jax.nn.sigmoid(logits)
    error_field = affinity_map - target.astype(single_float)
    err_out = error_field.astype(brain_float_half)

    tiles = err_out.reshape(3, N_GZ, CZ, CY, TOT, TX).transpose(1, 4, 0, 2, 3, 5).astype(single_float)
    slot_rows = []
    for row in range(N_GZ):
        placed = jnp.tensordot(selects[row].T, tiles[row], axes=1, precision=hi)
        slot_rows.append(placed.reshape(N_XY, MAXT, 3, CZ, CY, TX))
    err_tiles = jnp.stack(slot_rows).astype(brain_float_half)

    logit_gradient = (error_field * affinity_map * (1.0 - affinity_map) / SLAB_VOXELS).astype(brain_float_half)
    head_weight_gradient = jnp.einsum("mtnq,btnq->mb", logit_gradient.astype(single_float), signal_field.astype(single_float))
    gradient_total = jnp.einsum("jn,jbrq->nbrq", head_weight.astype(single_float), logit_gradient.astype(single_float))
    gsf = jnp.where(signal_field > 0, gradient_total, 0.0).astype(brain_float_half)
    grad_up = jnp.stack([jnp.einsum("ozyx,czyx->oc", strided(gsf, tap).astype(single_float), cfield.astype(single_float)) for tap in range(8)])
    gcoarse = sum(jnp.einsum("oc,ozyx->czyx", w_up[tap].astype(single_float), strided(gsf, tap).astype(single_float)) for tap in range(8))
    gquad = jnp.where(cfield > 0, gcoarse, 0.0).astype(brain_float_half)
    grad_mid = tap_grads(gquad, dfield)
    gdown = gquad.astype(single_float) + convolve(gquad, flipped(w_mid))
    gdd = jnp.where(dfield > 0, gdown, 0.0).astype(brain_float_half)
    grad_down = jnp.stack([jnp.einsum("ozyx,czyx->oc", gdd.astype(single_float), strided(h1, tap).astype(single_float)) for tap in range(8)])
    spread = alternate(jnp.stack([jnp.einsum("oc,ozyx->czyx", w_down[tap].astype(single_float), gdd.astype(single_float)) for tap in range(8)]))
    gres = jnp.where(h1 > 0, gsf.astype(single_float) + spread, 0.0).astype(brain_float_half)
    grad_res = tap_grads(gres, h0)
    gfirst = gres.astype(single_float) + convolve(gres, flipped(w_res))
    gact = jnp.where(h0 > 0, gfirst, 0.0).astype(brain_float_half)
    grad_in = tap_grads(gact, image)[:, :, 0]
    return (err_tiles, grad_in, grad_res, grad_down, grad_mid, grad_up, head_weight_gradient)
```

```python
import functools

import jax
import jax.numpy as jnp
from jax import lax
from jax.experimental import pallas as pl
from jax.experimental.pallas import tpu as pltpu
from jax.sharding import PartitionSpec as P

F32 = jnp.float32
BF16 = jnp.bfloat16
MESH = pl.DeviceIdType.MESH
SLOTS = 4
CORES = 2
ROWS = 1024
VM = pl.BlockSpec(memory_space=pltpu.VMEM)

RES, MID, DOWN, UP, INP, HEAD, USED = 0, 288, 672, 800, 928, 992, 1000


def grid_of(ranks):
    height = 8 if ranks == 32 else 2
    return ranks // height, height


def remote(src, dst, send, recv, where):
    return pltpu.make_async_remote_copy(
        src_ref=src, dst_ref=dst, send_sem=send, recv_sem=recv, device_id=where, device_id_type=MESH
    )


def greet(peers):
    barrier = pltpu.get_barrier_semaphore()
    for peer in peers:
        pl.semaphore_signal(barrier, inc=1, device_id=peer, device_id_type=MESH)
    pl.semaphore_wait(barrier, len(peers))


def spread_kernel(
    nx, ny, ng, block, halo, full, meta, xg, placed, yr, mine, hr, xs, xr, ys, yw, hs, hw
):
    ranks = nx * ny
    g = lax.axis_index("gz")
    j = lax.axis_index("xy")
    xi = j // ny
    yi = lax.rem(j, ny)
    x_peer = [(g, lax.rem(xi + k, nx) * ny + yi) for k in range(nx)]
    y_peer = [(g, xi * ny + lax.rem(yi + k, ny)) for k in range(ny)]
    around = [(dz, dj) for dz in (0, -1, 1, -2, 2) for dj in (0, -1, 1) if (dz, dj) != (0, 0)]
    near = [(lax.rem(g + dz + ng, ng), lax.rem(j + dj + ranks, ranks)) for dz, dj in around]
    greet(x_peer[1:] + y_peer[1:] + near)

    steps = [remote(block, xg.at[k], xs.at[k], xr.at[k], x_peer[k]) for k in range(1, nx)]
    for copy in steps:
        copy.start()
    xg[0] = block[...]
    for copy in steps:
        copy.wait()
    for k in range(nx):
        meta[k] = xg[k, 128:144, :]

    def place(k):
        first = ((xi * ny + lax.rem(yi + k, ny)) * 2).astype(F32)
        sums = [jnp.zeros((32, 128), F32), jnp.zeros((32, 128), F32)]
        for a in range(nx):
            names = xg[a, 128:144, :].astype(F32)
            for s in range(SLOTS):
                tile = xg[a, s * 32 : (s + 1) * 32, :].astype(F32)
                name = names[s : s + 1]
                for t in range(2):
                    sums[t] = sums[t] + jnp.where(name == first + t, tile, 0.0)
        for t in range(2):
            placed[k, t] = sums[t].astype(BF16)

    def y_copy(k):
        return remote(
            placed.at[k],
            yr.at[k],
            ys.at[k],
            yw.at[k],
            (g, xi * ny + lax.rem(yi + k, ny)),
        )

    def send_one(k, carry):
        place(k)
        y_copy(k).start()
        return carry

    lax.fori_loop(1, ny, send_one, 0)
    place(0)
    total = placed[0].astype(F32)
    for k in range(1, ny):
        y_copy(k).wait()
        total = total + yr[k].astype(F32)
    mine[...] = total.astype(BF16)

    copies = []
    for n, (dz, dj) in enumerate(around):
        rows = slice(0, 16) if abs(dz) == 2 else slice(0, 32)
        if dj == 0:
            src, dst = mine.at[:, rows], hr.at[2 - dz, 1:3, rows]
        elif dj == 1:
            src, dst = mine.at[1, rows], hr.at[2 - dz, 0, rows]
        else:
            src, dst = mine.at[0, rows], hr.at[2 - dz, 3, rows]
        copies.append(remote(src, dst, hs.at[n], hw.at[n], near[n]))
    for copy in copies:
        copy.start()
    hr[2, 1:3] = mine[...]
    for copy in copies:
        copy.wait()
    for z in range(5):
        halo[z] = hr[z, :, 0:16]
    for z in range(3):
        full[z] = hr[z + 1]


def spread_tiles(nx, ny, ng, block):
    return pl.pallas_call(
        functools.partial(spread_kernel, nx, ny, ng),
        out_shape=(
            jax.ShapeDtypeStruct((5, 4, 16, 128), BF16),
            jax.ShapeDtypeStruct((3, 4, 32, 128), BF16),
            jax.ShapeDtypeStruct((nx, 16, 128), BF16),
        ),
        in_specs=[VM],
        out_specs=(VM, VM, VM),
        scratch_shapes=[
            pltpu.VMEM((nx, 144, 128), BF16),
            pltpu.VMEM((ny, 2, 32, 128), BF16),
            pltpu.VMEM((ny, 2, 32, 128), BF16),
            pltpu.VMEM((2, 32, 128), BF16),
            pltpu.VMEM((5, 4, 32, 128), BF16),
            pltpu.SemaphoreType.DMA((nx,)),
            pltpu.SemaphoreType.DMA((nx,)),
            pltpu.SemaphoreType.DMA((ny,)),
            pltpu.SemaphoreType.DMA((ny,)),
            pltpu.SemaphoreType.DMA((14,)),
            pltpu.SemaphoreType.DMA((14,)),
        ],
        compiler_params=pltpu.CompilerParams(
            collective_id=0, has_side_effects=True, vmem_limit_bytes=32 << 20
        ),
        name="spread",
    )(block)


def iota(shape, dim):
    return lax.broadcasted_iota(jnp.int32, shape, dim)


def dot(a, b):
    return jnp.dot(a, b, preferred_element_type=F32)


def dot_t(a, b):
    return lax.dot_general(a, b, (((1,), (1,)), ((), ())), preferred_element_type=F32)


def hot(cond):
    return jnp.where(cond, 1.0, 0.0).astype(BF16)


def eye(n):
    return hot(iota((n, n), 0) == iota((n, n), 1))


def before(v):
    return pltpu.roll(v, 1, 1)


def after(v):
    return pltpu.roll(v, v.shape[1] - 1, 1)


def put_fine(buf, at, v):
    prev = before(v[128:256]).astype(BF16)
    succ = after(v[0:128]).astype(BF16)
    even = v[0:128].astype(BF16)
    odd = v[128:256].astype(BF16)
    for zo in range(2):
        for yo in range(2):
            rows = slice(zo * 64 + yo * 32, zo * 64 + yo * 32 + 32)
            for n, part in enumerate((prev, even, odd, succ)):
                buf[at + zo, yo * 128 + n * 32 : yo * 128 + n * 32 + 32, :] = part[rows]


def put_coarse(buf, at, v):
    buf[at, 0:64, :] = before(v).astype(BF16)
    buf[at, 64:128, :] = v.astype(BF16)
    buf[at, 128:192, :] = after(v).astype(BF16)
    buf[at, 192:256, :] = jnp.zeros((64, v.shape[1]), BF16)


def tap_of(pos):
    return (pos >> 1 & 1) * 4 + (pos & 1) * 2 + (pos >> 2)


def step_kernel(
    nz,
    nx_cells,
    voxels,
    halo,
    full,
    w_in,
    w_res,
    w_down,
    w_mid,
    w_up,
    head,
    vec,
    err_ref,
    w0,
    w1,
    w1b,
    wm,
    wmb,
    tcol,
    tgt,
    h0s,
    c0,
    h1s,
    cd,
    qs,
    ss,
    gls,
    gss,
    cg,
    gds,
    cr,
    grs,
    gas,
    errs,
):
    g = lax.axis_index("gz")
    j = lax.axis_index("xy")
    wide = 256

    i32, i64 = eye(32), eye(64)
    for xo in range(2):
        fwd = jnp.zeros((288, 128), F32)
        for c in range(3):
            put = hot(iota((32, 128), 1) == iota((32, 128), 0) + 32 * (c + xo))
            fwd = fwd + dot(w_res[:, c].reshape(288, 32), put)
        fwd = fwd.astype(BF16)
        blank = jnp.zeros((32, 32), BF16)
        for zy in range(9):
            parts = [w_res[8 - zy, 2 - c] for c in range(3)]
            parts = [blank] + parts if xo else parts + [blank]
            bwd = dot_t(i32, jnp.concatenate(parts, axis=0)).astype(BF16)
            dz, dy = zy // 3, zy % 3
            for zo in range(2):
                for yo in range(2):
                    y_in = yo + dy - 1
                    if 0 <= y_in < 2:
                        rows = slice(xo * 128 + zo * 64 + yo * 32, xo * 128 + zo * 64 + yo * 32 + 32)
                        lanes = slice((zo + dz) * 256 + y_in * 128, (zo + dz) * 256 + y_in * 128 + 128)
                        w1[rows, lanes] = fwd[zy * 32 : zy * 32 + 32]
                        w1b[rows, lanes] = bwd
        for zo in range(2):
            for yo in range(2):
                rows = slice(xo * 128 + zo * 64 + yo * 32, xo * 128 + zo * 64 + yo * 32 + 32)
                lanes = slice((3 - 3 * zo) * 256, (3 - 3 * zo) * 256 + 256)
                w1[rows, lanes] = jnp.zeros((32, 256), BF16)
                w1b[rows, lanes] = jnp.zeros((32, 256), BF16)
    taps_t = dot_t(i32, w_in[...]).astype(BF16)
    col = iota((27, 32), 1)
    tap = iota((27, 32), 0)
    for pos in range(8):
        xo, zo, yo = pos >> 2, pos >> 1 & 1, pos & 1
        hit = jnp.zeros((27, 32), jnp.bool_)
        for t in range(27):
            dz, dy, dx = t // 9, t // 3 % 3, t % 3
            if 0 <= yo + dy - 1 < 2:
                at = (zo + dz) * 8 + (xo + dx) * 2 + yo + dy - 1
                hit = hit | ((tap == t) & (col == at))
        w0[pos * 32 : pos * 32 + 32, :] = dot(taps_t, hot(hit)).astype(BF16)
    wd_t = jnp.concatenate([dot_t(i32, w_down[tap_of(p)]) for p in range(8)], axis=0).astype(BF16)
    wd = dot_t(i64, wd_t).astype(BF16)
    wu = jnp.concatenate([w_up[tap_of(p)] for p in range(8)], axis=0)
    wu_t = dot_t(i64, wu).astype(BF16)
    blank = jnp.zeros((64, 64), BF16)
    for a in range(3):
        fwd = [dot_t(i64, w_mid[9 * a + 3 + c]).astype(BF16) for c in range(3)] + [blank]
        bwd = [w_mid[26 - (9 * a + 3 + c)] for c in range(3)] + [blank]
        wm[:, a * 256 : a * 256 + 256] = dot_t(i64, jnp.concatenate(fwd, axis=0)).astype(BF16)
        wmb[:, a * 256 : a * 256 + 256] = dot_t(i64, jnp.concatenate(bwd, axis=0)).astype(BF16)
    heads = dot(head[...], hot((iota((32, 256), 1) & 31) == iota((32, 256), 0)))
    hd = jnp.concatenate(
        [jnp.broadcast_to(heads[a : a + 1], (8, 256)) for a in range(3)]
        + [jnp.zeros((8, 256), F32)],
        axis=0,
    )
    same = (iota((32, 256), 0) & 7) == (iota((32, 256), 1) >> 5)
    hd = jnp.where(same, hd, 0.0).astype(BF16)
    hd_t = dot_t(eye(256), hd).astype(BF16)

    image = jnp.concatenate(
        [
            jnp.concatenate([halo[z, t].astype(F32)[0:8] for t in range(4)], axis=1)
            for z in range(5)
        ],
        axis=0,
    )
    z2 = iota((40, 512), 0) + 8 * g - 16
    x1 = iota((40, 512), 1) + 256 * j - 128
    inside = (z2 >= 0) & (z2 < 4 * nz) & (x1 >= 0) & (x1 < 2 * nx_cells)
    image = jnp.where(inside, image, 0.0).astype(BF16)
    place = iota((512, wide), 0)
    lane2 = 2 * iota((512, wide), 1) + 128
    pick = [hot(place == ((lane2 + k) & 511)) for k in (-1, 0, 1, 2)]
    parts = jnp.concatenate([dot(image, p) for p in pick], axis=0).astype(BF16)
    r = iota((176, 160), 0)
    zi = r >> 3
    source = ((r >> 1) & 3) * 40 + (zi - 1) * 2 + (r & 1)
    order = hot((iota((176, 160), 1) == source) & (zi >= 1) & (zi <= 20))
    tcol[...] = dot(order, parts).astype(BF16)
    target = jnp.concatenate(
        [
            jnp.concatenate([full[z, t].astype(F32)[8:32] for t in range(4)], axis=1)
            for z in range(3)
        ],
        axis=0,
    ).astype(BF16)
    parts = jnp.concatenate([dot(target, p) for p in pick[1:3]], axis=0).astype(BF16)
    r = iota((192, 144), 0)
    source = (
        ((r >> 2) & 1) * 72
        + (r >> 6) * 24
        + ((r >> 3) & 3) * 8
        + (((r >> 5) & 1) * 2 + ((r >> 1) & 1)) * 2
        + (r & 1)
    )
    order = hot((iota((192, 144), 1) == source) & (((r >> 3) & 3) < 3))
    placed = dot(order, parts)
    for n in range(6):
        tgt[n] = placed[n * 32 : n * 32 + 32]

    lane = iota((1, wide), 1)
    cell = jnp.where(lane < 192, lane, lane - 256) + 128 * j
    lane_in = jnp.where((cell >= 0) & (cell < nx_cells), 1.0, 0.0)

    def in_slab(zc):
        at = 2 * g + zc
        return lane_in * jnp.where((at >= 0) & (at < nz), 1.0, 0.0)

    def first_conv(n, carry):
        rows = tcol[pl.ds(pl.multiple_of(n * 16, 16), 32), :]
        h0 = jnp.maximum(dot(w0[...], rows), 0.0) * in_slab(n - 4)
        h0s[n] = h0.astype(BF16)
        put_fine(c0, 2 * n, h0)
        return carry

    lax.fori_loop(0, 10, first_conv, 0)

    def second_conv(n, carry):
        cols = c0[pl.ds(2 * n + 1, 4)].reshape(1024, wide)
        h1 = jnp.maximum(h0s[n + 1].astype(F32) + dot(w1[...], cols), 0.0).astype(BF16)
        h1s[n] = h1
        put_coarse(cd, n, jnp.maximum(dot(wd, h1), 0.0) * in_slab(n - 3))
        return carry

    lax.fori_loop(0, 8, second_conv, 0)

    def middle(n, carry):
        cols = cd[pl.ds(n, 3)].reshape(768, wide)
        q = jnp.maximum(cd[n + 1, 64:128].astype(F32) + dot(wm[...], cols), 0.0).astype(BF16)
        qs[n] = q
        s = jnp.maximum(h1s[n + 1].astype(F32) + dot(wu, q), 0.0).astype(BF16)
        ss[n] = s
        aff = jax.nn.sigmoid(dot(hd, s))
        err = aff - tgt[n]
        errs[n] = err.astype(BF16)
        gl = (err * aff * (1.0 - aff) / voxels).astype(BF16)
        gls[n] = gl
        gs = jnp.where(s.astype(F32) > 0, dot(hd_t, gl), 0.0).astype(BF16)
        gss[n] = gs
        gq = jnp.where(q.astype(F32) > 0, dot(wu_t, gs), 0.0) * in_slab(n - 2)
        put_coarse(cg, n, gq)
        return carry

    lax.fori_loop(0, 6, middle, 0)

    def back(n, carry):
        cols = cg[pl.ds(n, 3)].reshape(768, wide)
        gdd = cg[n + 1, 64:128].astype(F32) + dot(wmb[...], cols)
        gdd = jnp.where(cd[n + 2, 64:128].astype(F32) > 0, gdd, 0.0).astype(BF16)
        gds[n] = gdd
        gr = gss[n + 1].astype(F32) + dot(wd_t, gdd)
        gr = jnp.where(h1s[n + 2].astype(F32) > 0, gr, 0.0) * in_slab(n - 1)
        grs[n] = gr.astype(BF16)
        put_fine(cr, 2 * n, gr)
        return carry

    lax.fori_loop(0, 4, back, 0)

    for n in range(2):
        cols = cr[2 * n + 1 : 2 * n + 5, :, 0:128].reshape(1024, 128)
        ga = grs[n + 1, :, 0:128].astype(F32) + dot(w1b[...], cols)
        gas[n] = jnp.where(h0s[n + 4, :, 0:128].astype(F32) > 0, ga, 0.0).astype(BF16)

    def own(ref, first):
        return jnp.concatenate([ref[first, :, 0:128], ref[first + 1, :, 0:128]], axis=1)

    rows = jnp.concatenate([errs[2, :, 0:128], errs[3, :, 0:128]], axis=0)
    src = iota((128, 256), 0)
    dst = iota((128, 256), 1)
    parts = jnp.concatenate([dot(rows, hot(dst == 2 * src + xo)) for xo in range(2)], axis=0)
    r = iota((32, 128), 0)
    source = ((r >> 2) & 1) * 32 + (r >> 3) * 8 + ((r >> 1) & 1) * 2 + (r & 1)
    q = iota((32, 128), 1)
    order = hot((q == source) | (q == source + 68))
    tiles = dot(order, parts.astype(BF16))
    err_ref[...] = jnp.concatenate([tiles[0:24, 0:128], tiles[0:24, 128:256]], axis=0).astype(BF16)

    gr = own(grs, 1)
    for zi in range(4):
        for yi in range(2):
            lanes = slice(yi * 128, yi * 128 + 128)
            cols = jnp.concatenate([c0[7 + zi, lanes, 0:128], c0[9 + zi, lanes, 0:128]], axis=1)
            part = dot_t(gr, cols)
            for zo in range(2):
                for yo in range(2):
                    dz, dy = zi - zo, yi - yo + 1
                    if 0 <= dz < 3:
                        rows = zo * 64 + yo * 32
                        both = part[rows : rows + 32] + pltpu.roll(
                            part[128 + rows : 128 + rows + 32], 96, 1
                        )
                        at = RES + (dz * 3 + dy) * 32
                        if zi == dz and yi == max(dy - 1, 0):
                            vec[at : at + 32, :] = both
                        else:
                            vec[at : at + 32, :] += both
    gq = jnp.concatenate([cg[2, 64:128, 0:128], cg[3, 64:128, 0:128]], axis=1)
    for a in range(3):
        for half in range(2):
            lanes = slice(half * 128, half * 128 + 128)
            cols = jnp.concatenate([cd[2 + a, lanes, 0:128], cd[3 + a, lanes, 0:128]], axis=1)
            at = MID + (a * 2 + half) * 64
            vec[at : at + 64, :] = dot_t(gq, cols)
    gdd = own(gds, 1)
    down = dot_t(gdd, own(h1s, 3))
    vec[DOWN : DOWN + 64, :] = down[:, 0:128]
    vec[DOWN + 64 : DOWN + 128, :] = down[:, 128:256]
    gs = own(gss, 2)
    qq = own(qs, 2)
    none = jnp.zeros((64, 256), BF16)
    vec[UP : UP + 128, :] = dot_t(gs[0:128], jnp.concatenate([qq, none], axis=0)) + dot_t(
        gs[128:256], jnp.concatenate([none, qq], axis=0)
    )
    cols = jnp.concatenate([tcol[64:96, 0:128], tcol[80:112, 0:128]], axis=1)
    inp = dot_t(cols, own(gas, 0))
    vec[INP : INP + 32, :] = inp[:, 0:128]
    vec[INP + 32 : INP + 64, :] = inp[:, 128:256]
    heads = jnp.where(same, dot_t(own(gls, 2), own(ss, 2)), 0.0)
    vec[HEAD:ROWS, :] = jnp.zeros((ROWS - HEAD, 128), F32)
    for a in range(3):
        line = jnp.sum(heads[a * 8 : a * 8 + 8], axis=0, keepdims=True)
        line = line[:, 0:128] + line[:, 128:256]
        line = line + pltpu.roll(line, 64, 1)
        line = line + pltpu.roll(line, 32, 1)
        vec[HEAD + a : HEAD + a + 1, :] = line


def local_step(nz, nx_cells, voxels, halo, full, w_in, w_res, w_down, w_mid, w_up, head):
    wide = 256
    return pl.pallas_call(
        functools.partial(step_kernel, nz, nx_cells, float(voxels)),
        out_shape=(
            jax.ShapeDtypeStruct((ROWS, 128), F32),
            jax.ShapeDtypeStruct((48, 128), BF16),
        ),
        in_specs=[VM] * 8,
        out_specs=(VM, VM),
        scratch_shapes=[
            pltpu.VMEM((256, 32), BF16),
            pltpu.VMEM((256, 1024), BF16),
            pltpu.VMEM((256, 1024), BF16),
            pltpu.VMEM((64, 768), BF16),
            pltpu.VMEM((64, 768), BF16),
            pltpu.VMEM((176, wide), BF16),
            pltpu.VMEM((6, 32, wide), F32),
            pltpu.VMEM((10, 256, wide), BF16),
            pltpu.VMEM((20, 256, wide), BF16),
            pltpu.VMEM((8, 256, wide), BF16),
            pltpu.VMEM((8, 256, wide), BF16),
            pltpu.VMEM((6, 64, wide), BF16),
            pltpu.VMEM((6, 256, wide), BF16),
            pltpu.VMEM((6, 32, wide), BF16),
            pltpu.VMEM((6, 256, wide), BF16),
            pltpu.VMEM((6, 256, wide), BF16),
            pltpu.VMEM((4, 64, wide), BF16),
            pltpu.VMEM((8, 256, wide), BF16),
            pltpu.VMEM((4, 256, wide), BF16),
            pltpu.VMEM((2, 256, 128), BF16),
            pltpu.VMEM((6, 32, wide), BF16),
        ],
        compiler_params=pltpu.CompilerParams(vmem_limit_bytes=48 << 20),
        name="step",
    )(halo, full, w_in, w_res, w_down, w_mid, w_up, head)


def sum_kernel(
    nx,
    ny,
    nzc,
    vec,
    err,
    meta,
    out,
    tiles,
    rc,
    ac,
    rx,
    ax,
    ry,
    ay,
    rz,
    gy,
    gx,
    gc,
    ey,
    em,
    ex,
    cs,
    cw,
    xs,
    xw,
    ys,
    yw,
    zs,
    zw,
    eys,
    eyw,
    exs,
    exw,
    gys,
    gyw,
    gxs,
    gxw,
):
    g = lax.axis_index("gz")
    j = lax.axis_index("xy")
    xi = j // ny
    yi = lax.rem(j, ny)
    zi = g // CORES
    core = lax.rem(g, CORES)
    other = (zi * CORES + 1 - core, j)
    x_at = [lax.rem(xi + k, nx) for k in range(nx)]
    y_at = [lax.rem(yi + k, ny) for k in range(ny)]
    x_peer = [(g, x_at[k] * ny + yi) for k in range(nx)]
    y_peer = [(g, xi * ny + y_at[k]) for k in range(ny)]
    z_peer = [(lax.rem(zi + k, nzc) * CORES + core, j) for k in range(nzc)]
    greet([other] + x_peer[1:] + y_peer[1:] + z_peer[1:])

    swap = remote(vec.at[1 - core], rc, cs.at[0], cw.at[0], other)
    swap.start()
    to_y = [remote(err, ey.at[k], eys.at[k], eyw.at[k], y_peer[k]) for k in range(1, ny)]
    for copy in to_y:
        copy.start()
    ey[0] = err[...]
    swap.wait_recv()
    ac[...] = vec[core] + rc[...]
    over_x = [remote(ac.at[x_at[k]], rx.at[k], xs.at[k], xw.at[k], x_peer[k]) for k in range(1, nx)]
    for copy in over_x:
        copy.start()

    for copy in to_y:
        copy.wait_recv()
    def answer(a, carry):
        names = meta[a].astype(F32)
        sums = [jnp.zeros((24, 128), F32) for _ in range(SLOTS)]
        for k in range(ny):
            first = ((xi * ny + lax.rem(yi - k + ny, ny)) * 2).astype(F32)
            pair = ey[k].astype(F32)
            for t in range(2):
                for s in range(SLOTS):
                    sums[s] = sums[s] + jnp.where(
                        names[s : s + 1] == first + t, pair[t * 24 : t * 24 + 24], 0.0
                    )
        em[a] = jnp.concatenate(sums, axis=0).astype(BF16)
        return carry

    lax.fori_loop(0, nx, answer, 0)
    to_x = [
        remote(em.at[nx - k], ex.at[k], exs.at[k], exw.at[k], x_peer[k]) for k in range(1, nx)
    ]
    for copy in to_x:
        copy.start()

    for copy in over_x:
        copy.wait_recv()
    total = ac[xi]
    for k in range(1, nx):
        total = total + rx[k]
    ax[...] = total
    over_y = [remote(ax.at[y_at[k]], ry.at[k], ys.at[k], yw.at[k], y_peer[k]) for k in range(1, ny)]
    for copy in over_y:
        copy.start()
    for copy in over_y:
        copy.wait_recv()
    total = ax[yi]
    for k in range(1, ny):
        total = total + ry[k]
    ay[...] = total
    over_z = [remote(ay, rz.at[zi], zs.at[k], zw.at[k], z_peer[k]) for k in range(1, nzc)]
    for copy in over_z:
        copy.start()
    rz[zi] = ay[...]
    for k in range(1, nzc):
        remote(ay, rz.at[lax.rem(zi - k + nzc, nzc)], zs.at[k], zw.at[k], z_peer[k]).wait_recv()
    total = rz[0]
    for k in range(1, nzc):
        total = total + rz[k]
    gy[yi] = total
    back_y = [remote(gy.at[yi], gy.at[yi], gys.at[k], gyw.at[k], y_peer[k]) for k in range(1, ny)]
    for copy in back_y:
        copy.start()
    for k in range(1, ny):
        at = lax.rem(yi - k + ny, ny)
        remote(gy.at[at], gy.at[at], gys.at[k], gyw.at[k], y_peer[k]).wait_recv()
    gx[xi] = gy[...]
    back_x = [remote(gx.at[xi], gx.at[xi], gxs.at[k], gxw.at[k], x_peer[k]) for k in range(1, nx)]
    for copy in back_x:
        copy.start()
    for k in range(1, nx):
        at = lax.rem(xi - k + nx, nx)
        remote(gx.at[at], gx.at[at], gxs.at[k], gxw.at[k], x_peer[k]).wait_recv()
    back = remote(gx, gc, cs.at[1], cw.at[1], other)
    back.start()
    out[core] = gx[...]

    for copy in to_x:
        copy.wait_recv()
    total = em[0].astype(F32)
    for k in range(1, nx):
        total = total + ex[k].astype(F32)
    tiles[...] = total.astype(BF16)

    back.wait_recv()
    out[1 - core] = gc[...]
    for copy in [swap, back] + to_y + over_x + to_x + over_y + over_z + back_y + back_x:
        copy.wait_send()


def sum_all(nx, ny, nzc, vec, err, meta):
    rows = ROWS // (CORES * nx * ny)
    pair = [pltpu.SemaphoreType.DMA((2,))] * 2
    on_x = [pltpu.SemaphoreType.DMA((nx,))] * 2
    on_y = [pltpu.SemaphoreType.DMA((ny,))] * 2
    on_z = [pltpu.SemaphoreType.DMA((nzc,))] * 2
    return pl.pallas_call(
        functools.partial(sum_kernel, nx, ny, nzc),
        out_shape=(
            jax.ShapeDtypeStruct((CORES, nx, ny, rows, 128), F32),
            jax.ShapeDtypeStruct((96, 128), BF16),
        ),
        in_specs=[VM] * 3,
        out_specs=(VM, VM),
        scratch_shapes=[
            pltpu.VMEM((nx, ny, rows, 128), F32),
            pltpu.VMEM((nx, ny, rows, 128), F32),
            pltpu.VMEM((nx, ny, rows, 128), F32),
            pltpu.VMEM((ny, rows, 128), F32),
            pltpu.VMEM((ny, rows, 128), F32),
            pltpu.VMEM((rows, 128), F32),
            pltpu.VMEM((nzc, rows, 128), F32),
            pltpu.VMEM((ny, rows, 128), F32),
            pltpu.VMEM((nx, ny, rows, 128), F32),
            pltpu.VMEM((nx, ny, rows, 128), F32),
            pltpu.VMEM((ny, 48, 128), BF16),
            pltpu.VMEM((nx, 96, 128), BF16),
            pltpu.VMEM((nx, 96, 128), BF16),
        ]
        + pair
        + on_x
        + on_y
        + on_z
        + on_y
        + on_x
        + on_y
        + on_x,
        compiler_params=pltpu.CompilerParams(
            collective_id=1, has_side_effects=True, vmem_limit_bytes=32 << 20
        ),
        name="sums",
    )(vec.reshape(CORES, nx, ny, rows, 128), err, meta)


def unpack_kernel(vec, g_in, g_res, g_down, g_mid, g_up, g_head, lines):
    for zy in range(9):
        strip = vec[RES + zy * 32 : RES + zy * 32 + 32, :]
        for c in range(3):
            part = strip if c == 0 else pltpu.roll(strip, 128 - 32 * c, 1)
            g_res[zy * 3 + c] = part[:, 0:32]
    for t in range(27):
        a, b, c = t // 9, t // 3 % 3, t % 3
        if b == 1:
            at = MID + (a * 2 + c // 2) * 64
            part = vec[at : at + 64, :]
            if c % 2:
                part = pltpu.roll(part, 64, 1)
            g_mid[t] = part[:, 0:64]
        else:
            g_mid[t] = jnp.zeros((64, 64), F32)
    for pos in range(8):
        quarter = pos & 3
        at = DOWN + (pos >> 2) * 64
        part = vec[at : at + 64, :]
        if quarter:
            part = pltpu.roll(part, 128 - 32 * quarter, 1)
        g_down[tap_of(pos)] = part[:, 0:32]
        part = vec[UP + quarter * 32 : UP + quarter * 32 + 32, :]
        if pos >> 2:
            part = pltpu.roll(part, 64, 1)
        g_up[tap_of(pos)] = part[:, 0:64]
        part = vec[INP + (pos >> 2) * 32 : INP + (pos >> 2) * 32 + 32, :]
        if quarter:
            part = pltpu.roll(part, 128 - 32 * quarter, 1)
        lines[pos] = part
    for t in range(27):
        dz, dy, dx = t // 9, t // 3 % 3, t % 3
        total = None
        for pos in range(8):
            xo, zo, yo = pos >> 2, pos >> 1 & 1, pos & 1
            if 0 <= yo + dy - 1 < 2:
                at = (zo + dz) * 8 + (xo + dx) * 2 + yo + dy - 1
                line = lines[pos, at : at + 1, :]
                total = line if total is None else total + line
        g_in[t : t + 1, :] = total[:, 0:32]
    g_head[...] = vec[HEAD : HEAD + 8, :][0:3, 0:32]


def unpack(vec):
    return pl.pallas_call(
        unpack_kernel,
        out_shape=(
            jax.ShapeDtypeStruct((27, 32), F32),
            jax.ShapeDtypeStruct((27, 32, 32), F32),
            jax.ShapeDtypeStruct((8, 64, 32), F32),
            jax.ShapeDtypeStruct((27, 64, 64), F32),
            jax.ShapeDtypeStruct((8, 32, 64), F32),
            jax.ShapeDtypeStruct((3, 32), F32),
        ),
        in_specs=[VM],
        out_specs=(VM,) * 6,
        scratch_shapes=[pltpu.VMEM((8, 32, 128), F32)],
        compiler_params=pltpu.CompilerParams(vmem_limit_bytes=32 << 20),
        name="unpack",
    )(vec)


def local(
    tile_image, tile_target, owner_counts, tile_list, w_in, w_res, w_down, w_mid, w_up, head_weight
):
    ranks = lax.axis_size("xy")
    ng = lax.axis_size("gz")
    nx, ny = grid_of(ranks)
    live = jnp.arange(SLOTS) < owner_counts[0, 0]
    names = jnp.where(live, tile_list[0, 0], -1).astype(BF16)
    names = jnp.broadcast_to(jnp.pad(names, (0, 12))[:, None], (16, 128))
    block = jnp.concatenate(
        [
            jnp.concatenate(
                [tile_image.reshape(SLOTS, 8, 128), tile_target.reshape(SLOTS, 24, 128)], axis=1
            ).reshape(SLOTS * 32, 128),
            names,
        ],
        axis=0,
    )
    halo, full, meta = spread_tiles(nx, ny, ng, block)
    vec, err = local_step(
        2 * ng,
        128 * ranks,
        ng * ranks * 2048,
        halo,
        full,
        w_in,
        w_res.reshape(9, 3, 32, 32),
        w_down,
        w_mid,
        w_up,
        head_weight,
    )
    sums, tiles = sum_all(nx, ny, ng // CORES, vec, err, meta)
    grads = unpack(sums.reshape(ROWS, 128))
    return (tiles.reshape(1, 1, SLOTS, 3, 4, 2, 128),) + tuple(grads)


def solution(mesh):
    return jax.shard_map(
        local,
        mesh=mesh,
        in_specs=(
            P("gz", "xy", None, None, None, None),
            P("gz", "xy", None, None, None, None, None),
            P("gz", "xy"),
            P("gz", "xy", None),
            P(),
            P(),
            P(),
            P(),
            P(),
            P(),
        ),
        out_specs=(P("gz", "xy", None, None, None, None, None), P(), P(), P(), P(), P(), P()),
        check_vma=False,
    )
```

```python
import functools

import jax
import jax.numpy as jnp
from jax import lax
from jax.experimental import pallas as pl
from jax.experimental.pallas import tpu as pltpu
from jax.sharding import PartitionSpec as P

F32 = jnp.float32
BF16 = jnp.bfloat16
MESH = pl.DeviceIdType.MESH
SLOTS = 4
CORES = 2
ROWS = 1024
VM = pl.BlockSpec(memory_space=pltpu.VMEM)

RES, MID, DOWN, UP, INP, HEAD, USED = 0, 288, 672, 800, 928, 992, 1000


def grid_of(ranks):
    height = 8 if ranks == 32 else 2
    return ranks // height, height


def remote(src, dst, send, recv, where):
    return pltpu.make_async_remote_copy(
        src_ref=src, dst_ref=dst, send_sem=send, recv_sem=recv, device_id=where, device_id_type=MESH
    )


def greet(peers):
    barrier = pltpu.get_barrier_semaphore()
    for peer in peers:
        pl.semaphore_signal(barrier, inc=1, device_id=peer, device_id_type=MESH)
    pl.semaphore_wait(barrier, len(peers))


def spread_kernel(
    nx,
    ny,
    ng,
    img,
    tgt,
    counts,
    names,
    halo,
    full,
    meta,
    block,
    xg,
    placed,
    yr,
    mine,
    hr,
    xs,
    xr,
    ys,
    yw,
    hs,
    hw,
):
    ranks = nx * ny
    g = lax.axis_index("gz")
    j = lax.axis_index("xy")
    xi = j // ny
    yi = lax.rem(j, ny)
    x_peer = [(g, lax.rem(xi + k, nx) * ny + yi) for k in range(nx)]
    y_peer = [(g, xi * ny + lax.rem(yi + k, ny)) for k in range(ny)]
    around = [(dz, dj) for dz in (0, -1, 1, -2, 2) for dj in (0, -1, 1) if (dz, dj) != (0, 0)]
    near = [(lax.rem(g + dz + ng, ng), lax.rem(j + dj + ranks, ranks)) for dz, dj in around]
    for s in range(SLOTS):
        block[s * 32 : s * 32 + 32] = jnp.concatenate(
            [img[s].astype(F32), tgt[s].astype(F32)], axis=0
        ).astype(BF16)
    live = lax.broadcasted_iota(jnp.int32, (1, SLOTS), 1) < counts[...]
    held = jnp.where(live, names[...], -1).astype(F32)
    lines = [jnp.broadcast_to(held[:, s : s + 1], (1, 128)) for s in range(SLOTS)]
    lines.append(jnp.zeros((12, 128), F32))
    block[128:144] = jnp.concatenate(lines, axis=0).astype(BF16)
    greet(x_peer[1:] + y_peer[1:] + near)

    steps = [remote(block, xg.at[k], xs.at[k], xr.at[k], x_peer[k]) for k in range(1, nx)]
    for copy in steps:
        copy.start()
    xg[0] = block[...]
    for copy in steps:
        copy.wait()
    for k in range(nx):
        meta[k] = xg[k, 128:144, :]

    def place(k):
        first = ((xi * ny + lax.rem(yi + k, ny)) * 2).astype(F32)
        sums = [jnp.zeros((32, 128), F32), jnp.zeros((32, 128), F32)]
        for a in range(nx):
            names = xg[a, 128:144, :].astype(F32)
            for s in range(SLOTS):
                tile = xg[a, s * 32 : (s + 1) * 32, :].astype(F32)
                name = names[s : s + 1]
                for t in range(2):
                    sums[t] = sums[t] + jnp.where(name == first + t, tile, 0.0)
        for t in range(2):
            placed[k, t] = sums[t].astype(BF16)

    def y_copy(k):
        return remote(
            placed.at[k],
            yr.at[k],
            ys.at[k],
            yw.at[k],
            (g, xi * ny + lax.rem(yi + k, ny)),
        )

    def send_one(k, carry):
        place(k)
        y_copy(k).start()
        return carry

    lax.fori_loop(1, ny, send_one, 0)
    place(0)
    total = placed[0].astype(F32)
    for k in range(1, ny):
        y_copy(k).wait()
        total = total + yr[k].astype(F32)
    mine[...] = total.astype(BF16)

    copies = []
    for n, (dz, dj) in enumerate(around):
        rows = slice(0, 16) if abs(dz) == 2 else slice(0, 32)
        if dj == 0:
            src, dst = mine.at[:, rows], hr.at[2 - dz, 1:3, rows]
        elif dj == 1:
            src, dst = mine.at[1, rows], hr.at[2 - dz, 0, rows]
        else:
            src, dst = mine.at[0, rows], hr.at[2 - dz, 3, rows]
        copies.append(remote(src, dst, hs.at[n], hw.at[n], near[n]))
    for copy in copies:
        copy.start()
    hr[2, 1:3] = mine[...]
    for copy in copies:
        copy.wait()
    for z in range(5):
        halo[z] = hr[z, :, 0:16]
    for z in range(3):
        full[z] = hr[z + 1]


def spread_tiles(nx, ny, ng, img, tgt, counts, names):
    return pl.pallas_call(
        functools.partial(spread_kernel, nx, ny, ng),
        out_shape=(
            jax.ShapeDtypeStruct((5, 4, 16, 128), BF16),
            jax.ShapeDtypeStruct((3, 4, 32, 128), BF16),
            jax.ShapeDtypeStruct((nx, 16, 128), BF16),
        ),
        in_specs=[VM] * 4,
        out_specs=(VM, VM, VM),
        scratch_shapes=[
            pltpu.VMEM((144, 128), BF16),
            pltpu.VMEM((nx, 144, 128), BF16),
            pltpu.VMEM((ny, 2, 32, 128), BF16),
            pltpu.VMEM((ny, 2, 32, 128), BF16),
            pltpu.VMEM((2, 32, 128), BF16),
            pltpu.VMEM((5, 4, 32, 128), BF16),
            pltpu.SemaphoreType.DMA((nx,)),
            pltpu.SemaphoreType.DMA((nx,)),
            pltpu.SemaphoreType.DMA((ny,)),
            pltpu.SemaphoreType.DMA((ny,)),
            pltpu.SemaphoreType.DMA((14,)),
            pltpu.SemaphoreType.DMA((14,)),
        ],
        compiler_params=pltpu.CompilerParams(
            collective_id=0, has_side_effects=True, vmem_limit_bytes=32 << 20
        ),
        name="spread",
    )(img, tgt, counts, names)


def iota(shape, dim):
    return lax.broadcasted_iota(jnp.int32, shape, dim)


def dot(a, b):
    return jnp.dot(a, b, preferred_element_type=F32)


def dot_t(a, b):
    return lax.dot_general(a, b, (((1,), (1,)), ((), ())), preferred_element_type=F32)


def hot(cond):
    return jnp.where(cond, 1.0, 0.0).astype(BF16)


def eye(n):
    return hot(iota((n, n), 0) == iota((n, n), 1))


def before(v):
    return pltpu.roll(v, 1, 1)


def after(v):
    return pltpu.roll(v, v.shape[1] - 1, 1)


def put_fine(buf, at, v):
    prev = before(v[128:256]).astype(BF16)
    succ = after(v[0:128]).astype(BF16)
    even = v[0:128].astype(BF16)
    odd = v[128:256].astype(BF16)
    for zo in range(2):
        for yo in range(2):
            rows = slice(zo * 64 + yo * 32, zo * 64 + yo * 32 + 32)
            for n, part in enumerate((prev, even, odd, succ)):
                buf[at + zo, yo * 128 + n * 32 : yo * 128 + n * 32 + 32, :] = part[rows]


def put_coarse(buf, at, v):
    buf[at, 0:64, :] = before(v).astype(BF16)
    buf[at, 64:128, :] = v.astype(BF16)
    buf[at, 128:192, :] = after(v).astype(BF16)
    buf[at, 192:256, :] = jnp.zeros((64, v.shape[1]), BF16)


def tap_of(pos):
    return (pos >> 1 & 1) * 4 + (pos & 1) * 2 + (pos >> 2)


def step_kernel(
    nz,
    nx_cells,
    voxels,
    halo,
    full,
    w_in,
    w_res,
    w_down,
    w_mid,
    w_up,
    head,
    vec,
    err_ref,
    w0,
    w1,
    w1b,
    wm,
    wmb,
    tcol,
    tgt,
    h0s,
    c0,
    h1s,
    cd,
    qs,
    ss,
    gls,
    gss,
    cg,
    gds,
    cr,
    grs,
    gas,
    errs,
):
    g = lax.axis_index("gz")
    j = lax.axis_index("xy")
    wide = 256

    i32, i64 = eye(32), eye(64)
    for xo in range(2):
        fwd = jnp.zeros((288, 128), F32)
        for c in range(3):
            put = hot(iota((32, 128), 1) == iota((32, 128), 0) + 32 * (c + xo))
            fwd = fwd + dot(w_res[:, c].reshape(288, 32), put)
        fwd = fwd.astype(BF16)
        blank = jnp.zeros((32, 32), BF16)
        for zy in range(9):
            parts = [w_res[8 - zy, 2 - c] for c in range(3)]
            parts = [blank] + parts if xo else parts + [blank]
            bwd = dot_t(i32, jnp.concatenate(parts, axis=0)).astype(BF16)
            dz, dy = zy // 3, zy % 3
            for zo in range(2):
                for yo in range(2):
                    y_in = yo + dy - 1
                    if 0 <= y_in < 2:
                        rows = slice(xo * 128 + zo * 64 + yo * 32, xo * 128 + zo * 64 + yo * 32 + 32)
                        lanes = slice((zo + dz) * 256 + y_in * 128, (zo + dz) * 256 + y_in * 128 + 128)
                        w1[rows, lanes] = fwd[zy * 32 : zy * 32 + 32]
                        w1b[rows, lanes] = bwd
        for zo in range(2):
            for yo in range(2):
                rows = slice(xo * 128 + zo * 64 + yo * 32, xo * 128 + zo * 64 + yo * 32 + 32)
                lanes = slice((3 - 3 * zo) * 256, (3 - 3 * zo) * 256 + 256)
                w1[rows, lanes] = jnp.zeros((32, 256), BF16)
                w1b[rows, lanes] = jnp.zeros((32, 256), BF16)
    taps_t = dot_t(i32, w_in[...]).astype(BF16)
    col = iota((27, 32), 1)
    tap = iota((27, 32), 0)
    for pos in range(8):
        xo, zo, yo = pos >> 2, pos >> 1 & 1, pos & 1
        hit = jnp.zeros((27, 32), jnp.bool_)
        for t in range(27):
            dz, dy, dx = t // 9, t // 3 % 3, t % 3
            if 0 <= yo + dy - 1 < 2:
                at = (zo + dz) * 8 + (xo + dx) * 2 + yo + dy - 1
                hit = hit | ((tap == t) & (col == at))
        w0[pos * 32 : pos * 32 + 32, :] = dot(taps_t, hot(hit)).astype(BF16)
    wd_t = jnp.concatenate([w_down[tap_of(p)] for p in range(8)], axis=0)
    wd = dot_t(i64, wd_t).astype(BF16)
    wu = jnp.concatenate([w_up[tap_of(p)] for p in range(8)], axis=0)
    wu_t = dot_t(i64, wu).astype(BF16)
    blank = jnp.zeros((64, 64), BF16)
    for a in range(3):
        fwd = [dot_t(i64, w_mid[9 * a + 3 + c]).astype(BF16) for c in range(3)] + [blank]
        bwd = [w_mid[26 - (9 * a + 3 + c)] for c in range(3)] + [blank]
        wm[:, a * 256 : a * 256 + 256] = dot_t(i64, jnp.concatenate(fwd, axis=0)).astype(BF16)
        wmb[:, a * 256 : a * 256 + 256] = dot_t(i64, jnp.concatenate(bwd, axis=0)).astype(BF16)
    heads = dot(head[...], hot((iota((32, 256), 1) & 31) == iota((32, 256), 0)))
    hd = jnp.concatenate(
        [jnp.broadcast_to(heads[a : a + 1], (8, 256)) for a in range(3)]
        + [jnp.zeros((8, 256), F32)],
        axis=0,
    )
    same = (iota((32, 256), 0) & 7) == (iota((32, 256), 1) >> 5)
    hd = jnp.where(same, hd, 0.0).astype(BF16)
    hd_t = dot_t(eye(256), hd).astype(BF16)

    image = jnp.concatenate(
        [
            jnp.concatenate([halo[z, t].astype(F32)[0:8] for t in range(4)], axis=1)
            for z in range(5)
        ],
        axis=0,
    )
    z2 = iota((40, 512), 0) + 8 * g - 16
    x1 = iota((40, 512), 1) + 256 * j - 128
    inside = (z2 >= 0) & (z2 < 4 * nz) & (x1 >= 0) & (x1 < 2 * nx_cells)
    image = jnp.where(inside, image, 0.0).astype(BF16)
    place = iota((512, wide), 0)
    lane2 = 2 * iota((512, wide), 1) + 128
    pick = [hot(place == ((lane2 + k) & 511)) for k in (-1, 0, 1, 2)]
    parts = jnp.concatenate([dot(image, p) for p in pick], axis=0).astype(BF16)
    r = iota((176, 160), 0)
    zi = r >> 3
    source = ((r >> 1) & 3) * 40 + (zi - 1) * 2 + (r & 1)
    order = hot((iota((176, 160), 1) == source) & (zi >= 1) & (zi <= 20))
    tcol[...] = dot(order, parts).astype(BF16)
    target = jnp.concatenate(
        [
            jnp.concatenate([full[z, t].astype(F32)[8:32] for t in range(4)], axis=1)
            for z in range(3)
        ],
        axis=0,
    ).astype(BF16)
    parts = jnp.concatenate([dot(target, p) for p in pick[1:3]], axis=0).astype(BF16)
    r = iota((192, 144), 0)
    source = (
        ((r >> 2) & 1) * 72
        + (r >> 6) * 24
        + ((r >> 3) & 3) * 8
        + (((r >> 5) & 1) * 2 + ((r >> 1) & 1)) * 2
        + (r & 1)
    )
    order = hot((iota((192, 144), 1) == source) & (((r >> 3) & 3) < 3))
    placed = dot(order, parts)
    for n in range(6):
        tgt[n] = placed[n * 32 : n * 32 + 32]

    lane = iota((1, wide), 1)
    cell = jnp.where(lane < 192, lane, lane - 256) + 128 * j
    lane_in = jnp.where((cell >= 0) & (cell < nx_cells), 1.0, 0.0)

    def in_slab(zc):
        at = 2 * g + zc
        return lane_in * jnp.where((at >= 0) & (at < nz), 1.0, 0.0)

    def first_conv(n, carry):
        rows = tcol[pl.ds(pl.multiple_of(n * 16, 16), 32), :]
        h0 = jnp.maximum(dot(w0[...], rows), 0.0) * in_slab(n - 4)
        h0s[n] = h0.astype(BF16)
        put_fine(c0, 2 * n, h0)
        return carry

    lax.fori_loop(0, 10, first_conv, 0, unroll=True)

    def second_conv(n, carry):
        cols = c0[pl.ds(2 * n + 1, 4)].reshape(1024, wide)
        h1 = jnp.maximum(h0s[n + 1].astype(F32) + dot(w1[...], cols), 0.0).astype(BF16)
        h1s[n] = h1
        put_coarse(cd, n, jnp.maximum(dot(wd, h1), 0.0) * in_slab(n - 3))
        return carry

    lax.fori_loop(0, 8, second_conv, 0, unroll=True)

    def middle(n, carry):
        cols = cd[pl.ds(n, 3)].reshape(768, wide)
        q = jnp.maximum(cd[n + 1, 64:128].astype(F32) + dot(wm[...], cols), 0.0).astype(BF16)
        qs[n] = q
        s = jnp.maximum(h1s[n + 1].astype(F32) + dot(wu, q), 0.0).astype(BF16)
        ss[n] = s
        aff = jax.nn.sigmoid(dot(hd, s))
        err = aff - tgt[n]
        errs[n] = err.astype(BF16)
        gl = (err * aff * (1.0 - aff) / voxels).astype(BF16)
        gls[n] = gl
        gs = jnp.where(s.astype(F32) > 0, dot(hd_t, gl), 0.0).astype(BF16)
        gss[n] = gs
        gq = jnp.where(q.astype(F32) > 0, dot(wu_t, gs), 0.0) * in_slab(n - 2)
        put_coarse(cg, n, gq)
        return carry

    lax.fori_loop(0, 6, middle, 0, unroll=True)

    def back(n, carry):
        cols = cg[pl.ds(n, 3)].reshape(768, wide)
        gdd = cg[n + 1, 64:128].astype(F32) + dot(wmb[...], cols)
        gdd = jnp.where(cd[n + 2, 64:128].astype(F32) > 0, gdd, 0.0).astype(BF16)
        gds[n] = gdd
        gr = gss[n + 1].astype(F32) + dot(wd_t, gdd)
        gr = jnp.where(h1s[n + 2].astype(F32) > 0, gr, 0.0) * in_slab(n - 1)
        grs[n] = gr.astype(BF16)
        put_fine(cr, 2 * n, gr)
        return carry

    lax.fori_loop(0, 4, back, 0, unroll=True)

    for n in range(2):
        cols = cr[2 * n + 1 : 2 * n + 5, :, 0:128].reshape(1024, 128)
        ga = grs[n + 1, :, 0:128].astype(F32) + dot(w1b[...], cols)
        gas[n] = jnp.where(h0s[n + 4, :, 0:128].astype(F32) > 0, ga, 0.0).astype(BF16)

    def own(ref, first):
        return jnp.concatenate([ref[first, :, 0:128], ref[first + 1, :, 0:128]], axis=1)

    rows = jnp.concatenate([errs[2, :, 0:128], errs[3, :, 0:128]], axis=0)
    src = iota((128, 256), 0)
    dst = iota((128, 256), 1)
    parts = jnp.concatenate([dot(rows, hot(dst == 2 * src + xo)) for xo in range(2)], axis=0)
    r = iota((32, 128), 0)
    source = ((r >> 2) & 1) * 32 + (r >> 3) * 8 + ((r >> 1) & 1) * 2 + (r & 1)
    q = iota((32, 128), 1)
    order = hot((q == source) | (q == source + 68))
    tiles = dot(order, parts.astype(BF16))
    err_ref[...] = jnp.concatenate([tiles[0:24, 0:128], tiles[0:24, 128:256]], axis=0).astype(BF16)

    gr = own(grs, 1)
    for zi in range(4):
        for yi in range(2):
            lanes = slice(yi * 128, yi * 128 + 128)
            cols = jnp.concatenate([c0[7 + zi, lanes, 0:128], c0[9 + zi, lanes, 0:128]], axis=1)
            part = dot_t(gr, cols)
            for zo in range(2):
                for yo in range(2):
                    dz, dy = zi - zo, yi - yo + 1
                    if 0 <= dz < 3:
                        rows = zo * 64 + yo * 32
                        both = part[rows : rows + 32] + pltpu.roll(
                            part[128 + rows : 128 + rows + 32], 96, 1
                        )
                        at = RES + (dz * 3 + dy) * 32
                        if zi == dz and yi == max(dy - 1, 0):
                            vec[at : at + 32, :] = both
                        else:
                            vec[at : at + 32, :] += both
    gq = jnp.concatenate([cg[2, 64:128, 0:128], cg[3, 64:128, 0:128]], axis=1)
    for a in range(3):
        for half in range(2):
            lanes = slice(half * 128, half * 128 + 128)
            cols = jnp.concatenate([cd[2 + a, lanes, 0:128], cd[3 + a, lanes, 0:128]], axis=1)
            at = MID + (a * 2 + half) * 64
            vec[at : at + 64, :] = dot_t(gq, cols)
    gdd = own(gds, 1)
    none = jnp.zeros((64, 256), BF16)
    for at, fine, coarse in ((DOWN, own(h1s, 3), gdd), (UP, own(gss, 2), own(qs, 2))):
        vec[at : at + 128, :] = dot_t(
            fine[0:128], jnp.concatenate([coarse, none], axis=0)
        ) + dot_t(fine[128:256], jnp.concatenate([none, coarse], axis=0))
    cols = jnp.concatenate([tcol[64:96, 0:128], tcol[80:112, 0:128]], axis=1)
    inp = dot_t(cols, own(gas, 0))
    vec[INP : INP + 32, :] = inp[:, 0:128]
    vec[INP + 32 : INP + 64, :] = inp[:, 128:256]
    heads = jnp.where(same, dot_t(own(gls, 2), own(ss, 2)), 0.0)
    vec[HEAD:ROWS, :] = jnp.zeros((ROWS - HEAD, 128), F32)
    for a in range(3):
        line = jnp.sum(heads[a * 8 : a * 8 + 8], axis=0, keepdims=True)
        line = line[:, 0:128] + line[:, 128:256]
        line = line + pltpu.roll(line, 64, 1)
        line = line + pltpu.roll(line, 32, 1)
        vec[HEAD + a : HEAD + a + 1, :] = line


def local_step(nz, nx_cells, voxels, halo, full, w_in, w_res, w_down, w_mid, w_up, head):
    wide = 256
    return pl.pallas_call(
        functools.partial(step_kernel, nz, nx_cells, float(voxels)),
        out_shape=(
            jax.ShapeDtypeStruct((ROWS, 128), F32),
            jax.ShapeDtypeStruct((48, 128), BF16),
        ),
        in_specs=[VM] * 8,
        out_specs=(VM, VM),
        scratch_shapes=[
            pltpu.VMEM((256, 32), BF16),
            pltpu.VMEM((256, 1024), BF16),
            pltpu.VMEM((256, 1024), BF16),
            pltpu.VMEM((64, 768), BF16),
            pltpu.VMEM((64, 768), BF16),
            pltpu.VMEM((176, wide), BF16),
            pltpu.VMEM((6, 32, wide), F32),
            pltpu.VMEM((10, 256, wide), BF16),
            pltpu.VMEM((20, 256, wide), BF16),
            pltpu.VMEM((8, 256, wide), BF16),
            pltpu.VMEM((8, 256, wide), BF16),
            pltpu.VMEM((6, 64, wide), BF16),
            pltpu.VMEM((6, 256, wide), BF16),
            pltpu.VMEM((6, 32, wide), BF16),
            pltpu.VMEM((6, 256, wide), BF16),
            pltpu.VMEM((6, 256, wide), BF16),
            pltpu.VMEM((4, 64, wide), BF16),
            pltpu.VMEM((8, 256, wide), BF16),
            pltpu.VMEM((4, 256, wide), BF16),
            pltpu.VMEM((2, 256, 128), BF16),
            pltpu.VMEM((6, 32, wide), BF16),
        ],
        compiler_params=pltpu.CompilerParams(vmem_limit_bytes=48 << 20),
        name="step",
    )(halo, full, w_in, w_res, w_down, w_mid, w_up, head)


def sum_kernel(
    nx,
    ny,
    nzc,
    vec,
    err,
    meta,
    out,
    tiles,
    rc,
    ac,
    rx,
    ax,
    ry,
    ay,
    rz,
    gy,
    gx,
    gc,
    ey,
    em,
    ex,
    cs,
    cw,
    xs,
    xw,
    ys,
    yw,
    zs,
    zw,
    eys,
    eyw,
    exs,
    exw,
    gys,
    gyw,
    gxs,
    gxw,
):
    g = lax.axis_index("gz")
    j = lax.axis_index("xy")
    xi = j // ny
    yi = lax.rem(j, ny)
    zi = g // CORES
    core = lax.rem(g, CORES)
    other = (zi * CORES + 1 - core, j)
    x_at = [lax.rem(xi + k, nx) for k in range(nx)]
    y_at = [lax.rem(yi + k, ny) for k in range(ny)]
    x_peer = [(g, x_at[k] * ny + yi) for k in range(nx)]
    y_peer = [(g, xi * ny + y_at[k]) for k in range(ny)]
    z_peer = [(lax.rem(zi + k, nzc) * CORES + core, j) for k in range(nzc)]
    greet([other] + x_peer[1:] + y_peer[1:] + z_peer[1:])

    swap = remote(vec.at[1 - core], rc, cs.at[0], cw.at[0], other)
    swap.start()
    to_y = [remote(err, ey.at[k], eys.at[k], eyw.at[k], y_peer[k]) for k in range(1, ny)]
    for copy in to_y:
        copy.start()
    ey[0] = err[...]
    swap.wait_recv()
    ac[...] = vec[core] + rc[...]
    over_x = [remote(ac.at[x_at[k]], rx.at[k], xs.at[k], xw.at[k], x_peer[k]) for k in range(1, nx)]
    for copy in over_x:
        copy.start()

    for copy in to_y:
        copy.wait_recv()
    def answer(a, carry):
        names = meta[a].astype(F32)
        sums = [jnp.zeros((24, 128), F32) for _ in range(SLOTS)]
        for k in range(ny):
            first = ((xi * ny + lax.rem(yi - k + ny, ny)) * 2).astype(F32)
            pair = ey[k].astype(F32)
            for t in range(2):
                for s in range(SLOTS):
                    sums[s] = sums[s] + jnp.where(
                        names[s : s + 1] == first + t, pair[t * 24 : t * 24 + 24], 0.0
                    )
        em[a] = jnp.concatenate(sums, axis=0).astype(BF16)
        return carry

    lax.fori_loop(0, nx, answer, 0)
    to_x = [
        remote(em.at[nx - k], ex.at[k], exs.at[k], exw.at[k], x_peer[k]) for k in range(1, nx)
    ]
    for copy in to_x:
        copy.start()

    for copy in over_x:
        copy.wait_recv()
    total = ac[xi]
    for k in range(1, nx):
        total = total + rx[k]
    ax[...] = total
    over_y = [remote(ax.at[y_at[k]], ry.at[k], ys.at[k], yw.at[k], y_peer[k]) for k in range(1, ny)]
    for copy in over_y:
        copy.start()
    for copy in over_y:
        copy.wait_recv()
    total = ax[yi]
    for k in range(1, ny):
        total = total + ry[k]
    ay[...] = total
    over_z = [remote(ay, rz.at[zi], zs.at[k], zw.at[k], z_peer[k]) for k in range(1, nzc)]
    for copy in over_z:
        copy.start()
    rz[zi] = ay[...]
    for k in range(1, nzc):
        remote(ay, rz.at[lax.rem(zi - k + nzc, nzc)], zs.at[k], zw.at[k], z_peer[k]).wait_recv()
    total = rz[0]
    for k in range(1, nzc):
        total = total + rz[k]
    gy[yi] = total
    back_y = [remote(gy.at[yi], gy.at[yi], gys.at[k], gyw.at[k], y_peer[k]) for k in range(1, ny)]
    for copy in back_y:
        copy.start()
    for k in range(1, ny):
        at = lax.rem(yi - k + ny, ny)
        remote(gy.at[at], gy.at[at], gys.at[k], gyw.at[k], y_peer[k]).wait_recv()
    gx[xi] = gy[...]
    back_x = [remote(gx.at[xi], gx.at[xi], gxs.at[k], gxw.at[k], x_peer[k]) for k in range(1, nx)]
    for copy in back_x:
        copy.start()
    for k in range(1, nx):
        at = lax.rem(xi - k + nx, nx)
        remote(gx.at[at], gx.at[at], gxs.at[k], gxw.at[k], x_peer[k]).wait_recv()
    back = remote(gx, gc, cs.at[1], cw.at[1], other)
    back.start()
    out[core] = gx[...]

    for copy in to_x:
        copy.wait_recv()
    total = em[0].astype(F32)
    for k in range(1, nx):
        total = total + ex[k].astype(F32)
    tiles[...] = total.astype(BF16)

    back.wait_recv()
    out[1 - core] = gc[...]
    for copy in [swap, back] + to_y + over_x + to_x + over_y + over_z + back_y + back_x:
        copy.wait_send()


def sum_all(nx, ny, nzc, vec, err, meta):
    rows = ROWS // (CORES * nx * ny)
    pair = [pltpu.SemaphoreType.DMA((2,))] * 2
    on_x = [pltpu.SemaphoreType.DMA((nx,))] * 2
    on_y = [pltpu.SemaphoreType.DMA((ny,))] * 2
    on_z = [pltpu.SemaphoreType.DMA((nzc,))] * 2
    return pl.pallas_call(
        functools.partial(sum_kernel, nx, ny, nzc),
        out_shape=(
            jax.ShapeDtypeStruct((CORES, nx, ny, rows, 128), F32),
            jax.ShapeDtypeStruct((96, 128), BF16),
        ),
        in_specs=[VM] * 3,
        out_specs=(VM, VM),
        scratch_shapes=[
            pltpu.VMEM((nx, ny, rows, 128), F32),
            pltpu.VMEM((nx, ny, rows, 128), F32),
            pltpu.VMEM((nx, ny, rows, 128), F32),
            pltpu.VMEM((ny, rows, 128), F32),
            pltpu.VMEM((ny, rows, 128), F32),
            pltpu.VMEM((rows, 128), F32),
            pltpu.VMEM((nzc, rows, 128), F32),
            pltpu.VMEM((ny, rows, 128), F32),
            pltpu.VMEM((nx, ny, rows, 128), F32),
            pltpu.VMEM((nx, ny, rows, 128), F32),
            pltpu.VMEM((ny, 48, 128), BF16),
            pltpu.VMEM((nx, 96, 128), BF16),
            pltpu.VMEM((nx, 96, 128), BF16),
        ]
        + pair
        + on_x
        + on_y
        + on_z
        + on_y
        + on_x
        + on_y
        + on_x,
        compiler_params=pltpu.CompilerParams(
            collective_id=1, has_side_effects=True, vmem_limit_bytes=32 << 20
        ),
        name="sums",
    )(vec.reshape(CORES, nx, ny, rows, 128), err, meta)


def unpack_kernel(vec, tiles, err, g_in, g_res, g_down, g_mid, g_up, g_head, lines):
    err[...] = tiles[...]
    for zy in range(9):
        strip = vec[RES + zy * 32 : RES + zy * 32 + 32, :]
        for c in range(3):
            part = strip if c == 0 else pltpu.roll(strip, 128 - 32 * c, 1)
            g_res[zy * 3 + c] = part[:, 0:32]
    for t in range(27):
        a, b, c = t // 9, t // 3 % 3, t % 3
        if b == 1:
            at = MID + (a * 2 + c // 2) * 64
            part = vec[at : at + 64, :]
            if c % 2:
                part = pltpu.roll(part, 64, 1)
            g_mid[t] = part[:, 0:64]
        else:
            g_mid[t] = jnp.zeros((64, 64), F32)
    for pos in range(8):
        quarter = pos & 3
        for at, grad in ((DOWN, g_down), (UP, g_up)):
            part = vec[at + quarter * 32 : at + quarter * 32 + 32, :]
            if pos >> 2:
                part = pltpu.roll(part, 64, 1)
            grad[tap_of(pos)] = part[:, 0:64]
        part = vec[INP + (pos >> 2) * 32 : INP + (pos >> 2) * 32 + 32, :]
        if quarter:
            part = pltpu.roll(part, 128 - 32 * quarter, 1)
        lines[pos] = part
    for t in range(27):
        dz, dy, dx = t // 9, t // 3 % 3, t % 3
        total = None
        for pos in range(8):
            xo, zo, yo = pos >> 2, pos >> 1 & 1, pos & 1
            if 0 <= yo + dy - 1 < 2:
                at = (zo + dz) * 8 + (xo + dx) * 2 + yo + dy - 1
                line = lines[pos, at : at + 1, :]
                total = line if total is None else total + line
        g_in[t : t + 1, :] = total[:, 0:32]
    g_head[...] = vec[HEAD : HEAD + 8, :][0:3, 0:32]


def unpack(vec, tiles):
    return pl.pallas_call(
        unpack_kernel,
        out_shape=(
            jax.ShapeDtypeStruct((96, 128), BF16),
            jax.ShapeDtypeStruct((27, 32), F32),
            jax.ShapeDtypeStruct((27, 32, 32), F32),
            jax.ShapeDtypeStruct((8, 32, 64), F32),
            jax.ShapeDtypeStruct((27, 64, 64), F32),
            jax.ShapeDtypeStruct((8, 32, 64), F32),
            jax.ShapeDtypeStruct((3, 32), F32),
        ),
        in_specs=[VM] * 2,
        out_specs=(VM,) * 7,
        scratch_shapes=[pltpu.VMEM((8, 32, 128), F32)],
        compiler_params=pltpu.CompilerParams(vmem_limit_bytes=32 << 20),
        name="unpack",
    )(vec, tiles)


def local(
    tile_image, tile_target, owner_counts, tile_list, w_in, w_res, w_down, w_mid, w_up, head_weight
):
    ranks = lax.axis_size("xy")
    ng = lax.axis_size("gz")
    nx, ny = grid_of(ranks)
    halo, full, meta = spread_tiles(
        nx,
        ny,
        ng,
        tile_image.reshape(SLOTS, 8, 128),
        tile_target.reshape(SLOTS, 24, 128),
        owner_counts,
        tile_list.reshape(1, SLOTS),
    )
    vec, err = local_step(
        2 * ng,
        128 * ranks,
        ng * ranks * 2048,
        halo,
        full,
        w_in,
        w_res.reshape(9, 3, 32, 32),
        jnp.transpose(w_down, (0, 2, 1)),
        w_mid,
        w_up,
        head_weight,
    )
    sums, tiles = sum_all(nx, ny, ng // CORES, vec, err, meta)
    tiles, g_in, g_res, g_down, g_mid, g_up, g_head = unpack(sums.reshape(ROWS, 128), tiles)
    tiles = tiles.reshape(1, 1, SLOTS, 3, 4, 2, 128)
    return (tiles, g_in, g_res, jnp.transpose(g_down, (0, 2, 1)), g_mid, g_up, g_head)


def solution(mesh):
    return jax.shard_map(
        local,
        mesh=mesh,
        in_specs=(
            P("gz", "xy", None, None, None, None),
            P("gz", "xy", None, None, None, None, None),
            P("gz", "xy"),
            P("gz", "xy", None),
            P(),
            P(),
            P(),
            P(),
            P(),
            P(),
        ),
        out_specs=(P("gz", "xy", None, None, None, None, None), P(), P(), P(), P(), P(), P()),
        check_vma=False,
    )
```

```python
import functools
import types

import jax
import jax.numpy as jnp
from jax import lax
from jax.experimental import pallas as pl
from jax.experimental.pallas import tpu as pltpu
from jax.sharding import PartitionSpec as P

F32 = jnp.float32
BF16 = jnp.bfloat16
MESH = pl.DeviceIdType.MESH
SLOTS = 4
CORES = 2
ROWS = 1024
VM = pl.BlockSpec(memory_space=pltpu.VMEM)

RES, MID, DOWN, UP, INP, HEAD, USED = 0, 288, 672, 800, 928, 992, 1000


def grid_of(ranks):
    height = 8 if ranks == 32 else 2
    return ranks // height, height


def remote(src, dst, send, recv, where):
    return pltpu.make_async_remote_copy(
        src_ref=src, dst_ref=dst, send_sem=send, recv_sem=recv, device_id=where, device_id_type=MESH
    )


def iota(shape, dim):
    return lax.broadcasted_iota(jnp.int32, shape, dim)


def dot(a, b):
    return jnp.dot(a, b, preferred_element_type=F32)


def dot_t(a, b):
    return lax.dot_general(a, b, (((1,), (1,)), ((), ())), preferred_element_type=F32)


def hot(cond):
    return jnp.where(cond, 1.0, 0.0).astype(BF16)


def eye(n):
    return hot(iota((n, n), 0) == iota((n, n), 1))


def before(v):
    return pltpu.roll(v, 1, 1)


def after(v):
    return pltpu.roll(v, v.shape[1] - 1, 1)


def put_fine(buf, at, v):
    prev = before(v[128:256]).astype(BF16)
    succ = after(v[0:128]).astype(BF16)
    even = v[0:128].astype(BF16)
    odd = v[128:256].astype(BF16)
    for zo in range(2):
        for yo in range(2):
            rows = slice(zo * 64 + yo * 32, zo * 64 + yo * 32 + 32)
            for n, part in enumerate((prev, even, odd, succ)):
                buf[at + zo, yo * 128 + n * 32 : yo * 128 + n * 32 + 32, :] = part[rows]


def put_coarse(buf, at, v):
    buf[at, 0:64, :] = before(v).astype(BF16)
    buf[at, 64:128, :] = v.astype(BF16)
    buf[at, 128:192, :] = after(v).astype(BF16)
    buf[at, 192:256, :] = jnp.zeros((64, v.shape[1]), BF16)


def tap_of(pos):
    return (pos >> 1 & 1) * 4 + (pos & 1) * 2 + (pos >> 2)


def whole_kernel(nx, ny, ng, names, *refs):
    r = types.SimpleNamespace(**dict(zip(names, refs)))
    ranks = nx * ny
    nzc = ng // CORES
    nz = 2 * ng
    nx_cells = 128 * ranks
    voxels = float(ng * ranks * 2048)
    wide = 256
    g = lax.axis_index("gz")
    j = lax.axis_index("xy")
    xi = j // ny
    yi = lax.rem(j, ny)
    zi = g // CORES
    core = lax.rem(g, CORES)
    other = (zi * CORES + 1 - core, j)
    x_at = [lax.rem(xi + k, nx) for k in range(nx)]
    y_at = [lax.rem(yi + k, ny) for k in range(ny)]
    x_peer = [(g, x_at[k] * ny + yi) for k in range(nx)]
    y_peer = [(g, xi * ny + y_at[k]) for k in range(ny)]
    z_peer = [(lax.rem(zi + k, nzc) * CORES + core, j) for k in range(nzc)]
    around = [(dz, dj) for dz in (0, -1, 1, -2, 2) for dj in (0, -1, 1) if (dz, dj) != (0, 0)]
    near = [(lax.rem(g + dz + ng, ng), lax.rem(j + dj + ranks, ranks)) for dz, dj in around]

    moves = (
        (r.tile_list, r.list_v),
        (r.counts, r.count_v),
        (r.img, r.xgi.at[0]),
        (r.target, r.xgt.at[0]),
        (r.w_res, r.w_res_v),
        (r.w_mid, r.w_mid_v),
        (r.w_down, r.w_down_v),
        (r.w_up, r.w_up_v),
        (r.w_in, r.w_in_v),
        (r.head, r.head_v),
    )
    loads = [pltpu.make_async_copy(src, dst, r.loaded.at[n]) for n, (src, dst) in enumerate(moves)]
    for copy in loads:
        copy.start()
    barrier = pltpu.get_barrier_semaphore()
    peers = [other] + x_peer[1:] + y_peer[1:] + z_peer[1:] + near
    for peer in peers:
        pl.semaphore_signal(barrier, inc=1, device_id=peer, device_id_type=MESH)
    for copy in loads[0:2]:
        copy.wait()
    live = lax.broadcasted_iota(jnp.int32, (1, SLOTS), 1) < r.count_v[...]
    held = jnp.where(live, r.list_v[...], -1).astype(F32)
    lines = [jnp.broadcast_to(held[:, s : s + 1], (1, 128)) for s in range(SLOTS)]
    lines.append(jnp.zeros((12, 128), F32))
    r.meta[0] = jnp.concatenate(lines, axis=0).astype(BF16)
    pl.semaphore_wait(barrier, len(peers))

    name_x = [
        remote(r.meta.at[0], r.meta.at[k], r.s_name.at[k], r.r_name.at[k], x_peer[k])
        for k in range(1, nx)
    ]
    img_x = [
        remote(r.img, r.xgi.at[k], r.s_ix.at[k], r.r_ix.at[k], x_peer[k]) for k in range(1, nx)
    ]
    tgt_x = [
        remote(r.target, r.xgt.at[k], r.s_tx.at[k], r.r_tx.at[k], x_peer[k]) for k in range(1, nx)
    ]
    for copy in name_x + img_x + tgt_x:
        copy.start()
    for copy in loads[4:]:
        copy.wait()

    i32, i64 = eye(32), eye(64)
    for xo in range(2):
        fwd = jnp.zeros((288, 128), F32)
        for c in range(3):
            put = hot(iota((32, 128), 1) == iota((32, 128), 0) + 32 * (c + xo))
            fwd = fwd + dot(r.w_res_v[:, c].reshape(288, 32), put)
        fwd = fwd.astype(BF16)
        blank = jnp.zeros((32, 32), BF16)
        for zy in range(9):
            parts = [r.w_res_v[8 - zy, 2 - c] for c in range(3)]
            parts = [blank] + parts if xo else parts + [blank]
            bwd = dot_t(i32, jnp.concatenate(parts, axis=0)).astype(BF16)
            dz, dy = zy // 3, zy % 3
            for zo in range(2):
                for yo in range(2):
                    y_in = yo + dy - 1
                    if 0 <= y_in < 2:
                        rows = slice(xo * 128 + zo * 64 + yo * 32, xo * 128 + zo * 64 + yo * 32 + 32)
                        lanes = slice((zo + dz) * 256 + y_in * 128, (zo + dz) * 256 + y_in * 128 + 128)
                        r.w1[rows, lanes] = fwd[zy * 32 : zy * 32 + 32]
                        r.w1b[rows, lanes] = bwd
        for zo in range(2):
            for yo in range(2):
                rows = slice(xo * 128 + zo * 64 + yo * 32, xo * 128 + zo * 64 + yo * 32 + 32)
                lanes = slice((3 - 3 * zo) * 256, (3 - 3 * zo) * 256 + 256)
                r.w1[rows, lanes] = jnp.zeros((32, 256), BF16)
                r.w1b[rows, lanes] = jnp.zeros((32, 256), BF16)
    taps_t = dot_t(i32, r.w_in_v[...]).astype(BF16)
    col = iota((27, 32), 1)
    tap = iota((27, 32), 0)
    for pos in range(8):
        xo, zo, yo = pos >> 2, pos >> 1 & 1, pos & 1
        hit = jnp.zeros((27, 32), jnp.bool_)
        for t in range(27):
            dz, dy, dx = t // 9, t // 3 % 3, t % 3
            if 0 <= yo + dy - 1 < 2:
                at = (zo + dz) * 8 + (xo + dx) * 2 + yo + dy - 1
                hit = hit | ((tap == t) & (col == at))
        r.w0[pos * 32 : pos * 32 + 32, :] = dot(taps_t, hot(hit)).astype(BF16)
    wd_t = jnp.concatenate([r.w_down_v[tap_of(p)] for p in range(8)], axis=0)
    wd = dot_t(i64, wd_t).astype(BF16)
    wu = jnp.concatenate([r.w_up_v[tap_of(p)] for p in range(8)], axis=0)
    wu_t = dot_t(i64, wu).astype(BF16)
    blank = jnp.zeros((64, 64), BF16)
    for a in range(3):
        fwd = [dot_t(i64, r.w_mid_v[9 * a + 3 + c]).astype(BF16) for c in range(3)] + [blank]
        bwd = [r.w_mid_v[26 - (9 * a + 3 + c)] for c in range(3)] + [blank]
        r.wm[:, a * 256 : a * 256 + 256] = dot_t(i64, jnp.concatenate(fwd, axis=0)).astype(BF16)
        r.wmb[:, a * 256 : a * 256 + 256] = dot_t(i64, jnp.concatenate(bwd, axis=0)).astype(BF16)
    heads = dot(r.head_v[...], hot((iota((32, 256), 1) & 31) == iota((32, 256), 0)))
    hd = jnp.concatenate(
        [jnp.broadcast_to(heads[a : a + 1], (8, 256)) for a in range(3)]
        + [jnp.zeros((8, 256), F32)],
        axis=0,
    )
    same = (iota((32, 256), 0) & 7) == (iota((32, 256), 1) >> 5)
    hd = jnp.where(same, hd, 0.0).astype(BF16)
    hd_t = dot_t(eye(256), hd).astype(BF16)


    for copy in [loads[2]]:
        copy.wait()
    for copy in name_x + img_x:
        copy.wait_recv()

    def select(k, tiles, rows):
        first = ((xi * ny + lax.rem(yi + k, ny)) * 2).astype(F32)
        sums = [jnp.zeros((rows, 128), F32), jnp.zeros((rows, 128), F32)]
        for a in range(nx):
            called = r.meta[a].astype(F32)
            held = tiles[a].astype(F32)
            for s in range(SLOTS):
                tile = held[s * rows : s * rows + rows]
                for t in range(2):
                    sums[t] = sums[t] + jnp.where(called[s : s + 1] == first + t, tile, 0.0)
        return jnp.concatenate(sums, axis=0).astype(BF16)

    def img_y(k):
        peer = (g, xi * ny + lax.rem(yi + k, ny))
        return remote(r.pli.at[k], r.yri.at[k], r.s_iy.at[k], r.r_iy.at[k], peer)

    def tgt_y(k):
        peer = (g, xi * ny + lax.rem(yi + k, ny))
        return remote(r.plt.at[k], r.yrt.at[k], r.s_ty.at[k], r.r_ty.at[k], peer)

    def send_img(k, carry):
        r.pli[k] = select(k, r.xgi, 8)
        img_y(k).start()
        return carry

    def send_tgt(k, carry):
        r.plt[k] = select(k, r.xgt, 24)
        tgt_y(k).start()
        return carry

    lax.fori_loop(1, ny, send_img, 0)
    loads[3].wait()
    for copy in tgt_x:
        copy.wait_recv()
    lax.fori_loop(1, ny, send_tgt, 0)
    r.pli[0] = select(0, r.xgi, 8)
    r.plt[0] = select(0, r.xgt, 24)

    total = r.pli[0].astype(F32)
    for k in range(1, ny):
        img_y(k).wait_recv()
        total = total + r.yri[k].astype(F32)
    r.mi[...] = total.astype(BF16)
    img_n = [
        remote(r.mi, r.hri.at[2 - dz, 1 - dj], r.s_in.at[n], r.r_in.at[n], near[n])
        for n, (dz, dj) in enumerate(around)
    ]
    for copy in img_n:
        copy.start()
    r.hri[2, 1] = r.mi[...]
    total = r.plt[0].astype(F32)
    for k in range(1, ny):
        tgt_y(k).wait_recv()
        total = total + r.yrt[k].astype(F32)
    r.mt[...] = total.astype(BF16)
    tgt_n = [
        remote(r.mt, r.hrt.at[1 - dz, 1 - dj], r.s_tn.at[n], r.r_tn.at[n], near[n])
        for n, (dz, dj) in enumerate(around)
        if abs(dz) < 2
    ]
    for copy in tgt_n:
        copy.start()
    r.hrt[1, 1] = r.mt[...]
    for copy in img_n:
        copy.wait_recv()

    def wide_rows(ref, z, rows):
        left, own, right = (ref[z, n].astype(F32) for n in range(3))
        return jnp.concatenate([left[rows:], own[:rows], own[rows:], right[:rows]], axis=1)

    image = jnp.concatenate([wide_rows(r.hri, z, 8) for z in range(5)], axis=0)
    z2 = iota((40, 512), 0) + 8 * g - 16
    x1 = iota((40, 512), 1) + 256 * j - 128
    inside = (z2 >= 0) & (z2 < 4 * nz) & (x1 >= 0) & (x1 < 2 * nx_cells)
    image = jnp.where(inside, image, 0.0).astype(BF16)
    place = iota((512, wide), 0)
    lane2 = 2 * iota((512, wide), 1) + 128
    pick = [hot(place == ((lane2 + k) & 511)) for k in (-1, 0, 1, 2)]
    parts = jnp.concatenate([dot(image, p) for p in pick], axis=0).astype(BF16)
    row = iota((176, 160), 0)
    zrow = row >> 3
    source = ((row >> 1) & 3) * 40 + (zrow - 1) * 2 + (row & 1)
    order = hot((iota((176, 160), 1) == source) & (zrow >= 1) & (zrow <= 20))
    r.tcol[...] = dot(order, parts).astype(BF16)

    lane = iota((1, wide), 1)
    cell = jnp.where(lane < 192, lane, lane - 256) + 128 * j
    lane_in = jnp.where((cell >= 0) & (cell < nx_cells), 1.0, 0.0)

    def in_slab(zc):
        at = 2 * g + zc
        return lane_in * jnp.where((at >= 0) & (at < nz), 1.0, 0.0)

    def first_conv(n, carry):
        rows = r.tcol[pl.ds(pl.multiple_of(n * 16, 16), 32), :]
        h0 = jnp.maximum(dot(r.w0[...], rows), 0.0) * in_slab(n - 4)
        r.h0s[n] = h0.astype(BF16)
        put_fine(r.c0, 2 * n, h0)
        return carry

    lax.fori_loop(0, 10, first_conv, 0, unroll=True)

    def second_conv(n, carry):
        cols = r.c0[pl.ds(2 * n + 1, 4)].reshape(1024, wide)
        h1 = jnp.maximum(r.h0s[n + 1].astype(F32) + dot(r.w1[...], cols), 0.0).astype(BF16)
        r.h1s[n] = h1
        put_coarse(r.cd, n, jnp.maximum(dot(wd, h1), 0.0) * in_slab(n - 3))
        return carry

    lax.fori_loop(0, 8, second_conv, 0, unroll=True)


    for copy in tgt_n:
        copy.wait_recv()
    target = jnp.concatenate([wide_rows(r.hrt, z, 24) for z in range(3)], axis=0).astype(BF16)
    parts = jnp.concatenate([dot(target, p) for p in pick[1:3]], axis=0).astype(BF16)
    row = iota((192, 144), 0)
    source = (
        ((row >> 2) & 1) * 72
        + (row >> 6) * 24
        + ((row >> 3) & 3) * 8
        + (((row >> 5) & 1) * 2 + ((row >> 1) & 1)) * 2
        + (row & 1)
    )
    order = hot((iota((192, 144), 1) == source) & (((row >> 3) & 3) < 3))
    placed = dot(order, parts)
    for n in range(6):
        r.tgt[n] = placed[n * 32 : n * 32 + 32]


    def middle(n, carry):
        cols = r.cd[pl.ds(n, 3)].reshape(768, wide)
        q = jnp.maximum(r.cd[n + 1, 64:128].astype(F32) + dot(r.wm[...], cols), 0.0).astype(BF16)
        r.qs[n] = q
        s = jnp.maximum(r.h1s[n + 1].astype(F32) + dot(wu, q), 0.0).astype(BF16)
        r.ss[n] = s
        aff = jax.nn.sigmoid(dot(hd, s))
        err = aff - r.tgt[n]
        r.errs[n] = err.astype(BF16)
        gl = (err * aff * (1.0 - aff) / voxels).astype(BF16)
        r.gls[n] = gl
        gs = jnp.where(s.astype(F32) > 0, dot(hd_t, gl), 0.0).astype(BF16)
        r.gss[n] = gs
        gq = jnp.where(q.astype(F32) > 0, dot(wu_t, gs), 0.0) * in_slab(n - 2)
        put_coarse(r.cg, n, gq)
        return carry

    lax.fori_loop(0, 6, middle, 0, unroll=True)


    def own(ref, first):
        return jnp.concatenate([ref[first, :, 0:128], ref[first + 1, :, 0:128]], axis=1)


    rows = jnp.concatenate([r.errs[2, :, 0:128], r.errs[3, :, 0:128]], axis=0)
    src = iota((128, 256), 0)
    dst = iota((128, 256), 1)
    parts = jnp.concatenate([dot(rows, hot(dst == 2 * src + xo)) for xo in range(2)], axis=0)
    row = iota((32, 128), 0)
    source = ((row >> 2) & 1) * 32 + (row >> 3) * 8 + ((row >> 1) & 1) * 2 + (row & 1)
    q = iota((32, 128), 1)
    order = hot((q == source) | (q == source + 68))
    tiles = dot(order, parts.astype(BF16))
    r.err[...] = jnp.concatenate([tiles[0:24, 0:128], tiles[0:24, 128:256]], axis=0).astype(BF16)


    err_y = [remote(r.err, r.ey.at[k], r.s_ey.at[k], r.r_ey.at[k], y_peer[k]) for k in range(1, ny)]
    for copy in err_y:
        copy.start()
    r.ey[0] = r.err[...]

    def back(n, carry):
        cols = r.cg[pl.ds(n, 3)].reshape(768, wide)
        gdd = r.cg[n + 1, 64:128].astype(F32) + dot(r.wmb[...], cols)
        gdd = jnp.where(r.cd[n + 2, 64:128].astype(F32) > 0, gdd, 0.0).astype(BF16)
        r.gds[n] = gdd
        gr = r.gss[n + 1].astype(F32) + dot(wd_t, gdd)
        gr = jnp.where(r.h1s[n + 2].astype(F32) > 0, gr, 0.0) * in_slab(n - 1)
        r.grs[n] = gr.astype(BF16)
        put_fine(r.cr, 2 * n, gr)
        return carry

    lax.fori_loop(0, 4, back, 0, unroll=True)

    for n in range(2):
        cols = r.cr[2 * n + 1 : 2 * n + 5, :, 0:128].reshape(1024, 128)
        ga = r.grs[n + 1, :, 0:128].astype(F32) + dot(r.w1b[...], cols)
        r.gas[n] = jnp.where(r.h0s[n + 4, :, 0:128].astype(F32) > 0, ga, 0.0).astype(BF16)


    gr = own(r.grs, 1)
    for z_in in range(4):
        for y_in in range(2):
            lanes = slice(y_in * 128, y_in * 128 + 128)
            cols = jnp.concatenate([r.c0[7 + z_in, lanes, 0:128], r.c0[9 + z_in, lanes, 0:128]], axis=1)
            part = dot_t(gr, cols)
            for zo in range(2):
                for yo in range(2):
                    dz, dy = z_in - zo, y_in - yo + 1
                    if 0 <= dz < 3:
                        rows = zo * 64 + yo * 32
                        both = part[rows : rows + 32] + pltpu.roll(
                            part[128 + rows : 128 + rows + 32], 96, 1
                        )
                        at = RES + (dz * 3 + dy) * 32
                        if z_in == dz and y_in == max(dy - 1, 0):
                            r.vec[at : at + 32, :] = both
                        else:
                            r.vec[at : at + 32, :] += both
    gq = jnp.concatenate([r.cg[2, 64:128, 0:128], r.cg[3, 64:128, 0:128]], axis=1)
    for a in range(3):
        for half in range(2):
            lanes = slice(half * 128, half * 128 + 128)
            cols = jnp.concatenate([r.cd[2 + a, lanes, 0:128], r.cd[3 + a, lanes, 0:128]], axis=1)
            at = MID + (a * 2 + half) * 64
            r.vec[at : at + 64, :] = dot_t(gq, cols)
    gdd = own(r.gds, 1)
    none = jnp.zeros((64, 256), BF16)
    for at, fine, coarse in ((DOWN, own(r.h1s, 3), gdd), (UP, own(r.gss, 2), own(r.qs, 2))):
        r.vec[at : at + 128, :] = dot_t(
            fine[0:128], jnp.concatenate([coarse, none], axis=0)
        ) + dot_t(fine[128:256], jnp.concatenate([none, coarse], axis=0))
    cols = jnp.concatenate([r.tcol[64:96, 0:128], r.tcol[80:112, 0:128]], axis=1)
    inp = dot_t(cols, own(r.gas, 0))
    r.vec[INP : INP + 32, :] = inp[:, 0:128]
    r.vec[INP + 32 : INP + 64, :] = inp[:, 128:256]
    heads = jnp.where(same, dot_t(own(r.gls, 2), own(r.ss, 2)), 0.0)
    r.vec[HEAD:ROWS, :] = jnp.zeros((ROWS - HEAD, 128), F32)
    for a in range(3):
        line = jnp.sum(heads[a * 8 : a * 8 + 8], axis=0, keepdims=True)
        line = line[:, 0:128] + line[:, 128:256]
        line = line + pltpu.roll(line, 64, 1)
        line = line + pltpu.roll(line, 32, 1)
        r.vec[HEAD + a : HEAD + a + 1, :] = line


    half = ROWS // CORES
    rows_x = half // nx
    rows_y = rows_x // ny

    def piece(k, size):
        return pl.ds(pl.multiple_of(k * size, size), size)

    swap = remote(r.vec.at[piece(1 - core, half)], r.rc, r.s_c.at[0], r.r_c.at[0], other)
    swap.start()
    for copy in err_y:
        copy.wait_recv()

    def answer(a, carry):
        called = r.meta[a].astype(F32)
        sums = [jnp.zeros((24, 128), F32) for _ in range(SLOTS)]
        for k in range(ny):
            first = ((xi * ny + lax.rem(yi - k + ny, ny)) * 2).astype(F32)
            pair = r.ey[k].astype(F32)
            for t in range(2):
                for s in range(SLOTS):
                    sums[s] = sums[s] + jnp.where(
                        called[s : s + 1] == first + t, pair[t * 24 : t * 24 + 24], 0.0
                    )
        r.em[a] = jnp.concatenate(sums, axis=0).astype(BF16)
        return carry

    lax.fori_loop(0, nx, answer, 0)
    swap.wait_recv()
    r.ac[...] = r.vec[piece(core, half), :] + r.rc[...]
    over_x = [
        remote(r.ac.at[piece(x_at[k], rows_x)], r.rx.at[k], r.s_x.at[k], r.r_x.at[k], x_peer[k])
        for k in range(1, nx)
    ]
    err_x = [
        remote(r.em.at[nx - k], r.ex.at[k], r.s_ex.at[k], r.r_ex.at[k], x_peer[k])
        for k in range(1, nx)
    ]
    for copy in over_x + err_x:
        copy.start()
    for copy in over_x:
        copy.wait_recv()
    total = r.ac[piece(xi, rows_x), :]
    for k in range(1, nx):
        total = total + r.rx[k]
    r.ax[...] = total
    over_y = [
        remote(r.ax.at[piece(y_at[k], rows_y)], r.ry.at[k], r.s_y.at[k], r.r_y.at[k], y_peer[k])
        for k in range(1, ny)
    ]
    for copy in over_y:
        copy.start()
    for copy in over_y:
        copy.wait_recv()
    total = r.ax[piece(yi, rows_y), :]
    for k in range(1, ny):
        total = total + r.ry[k]
    r.ay[...] = total
    over_z = [remote(r.ay, r.rz.at[zi], r.s_z.at[k], r.r_z.at[k], z_peer[k]) for k in range(1, nzc)]
    for copy in over_z:
        copy.start()
    r.rz[zi] = r.ay[...]
    for k in range(1, nzc):
        at = lax.rem(zi - k + nzc, nzc)
        remote(r.ay, r.rz.at[at], r.s_z.at[k], r.r_z.at[k], z_peer[k]).wait_recv()
    total = r.rz[0]
    for k in range(1, nzc):
        total = total + r.rz[k]
    r.gy[yi] = total
    back_y = [
        remote(r.gy.at[yi], r.gy.at[yi], r.s_gy.at[k], r.r_gy.at[k], y_peer[k])
        for k in range(1, ny)
    ]
    for copy in back_y:
        copy.start()
    for k in range(1, ny):
        at = lax.rem(yi - k + ny, ny)
        remote(r.gy.at[at], r.gy.at[at], r.s_gy.at[k], r.r_gy.at[k], y_peer[k]).wait_recv()
    r.gx[xi] = r.gy[...].reshape(rows_x, 128)
    back_x = [
        remote(r.gx.at[xi], r.gx.at[xi], r.s_gx.at[k], r.r_gx.at[k], x_peer[k])
        for k in range(1, nx)
    ]
    for copy in back_x:
        copy.start()
    for k in range(1, nx):
        at = lax.rem(xi - k + nx, nx)
        remote(r.gx.at[at], r.gx.at[at], r.s_gx.at[k], r.r_gx.at[k], x_peer[k]).wait_recv()
    back_c = remote(r.gx, r.gc, r.s_c.at[1], r.r_c.at[1], other)
    back_c.start()
    r.out[piece(core, half), :] = r.gx[...].reshape(half, 128)
    for copy in err_x:
        copy.wait_recv()
    total = r.em[0].astype(F32)
    for k in range(1, nx):
        total = total + r.ex[k].astype(F32)
    r.tiles[...] = total.astype(BF16)
    back_c.wait_recv()
    r.out[piece(1 - core, half), :] = r.gc[...].reshape(half, 128)
    sent = [swap, back_c] + name_x + img_x + tgt_x + img_n + tgt_n + err_y + err_x
    sent += [img_y(k) for k in range(1, ny)] + [tgt_y(k) for k in range(1, ny)]
    for copy in sent + over_x + over_y + over_z + back_y + back_x:
        copy.wait_send()


def whole(nx, ny, ng, operands):
    wide = 256
    nzc = ng // CORES
    half = ROWS // CORES
    rows_x = half // nx
    rows_y = rows_x // ny
    buffers = dict(
        list_v=((1, SLOTS), jnp.int32),
        count_v=((1, 1), jnp.int32),
        w_res_v=((9, 3, 32, 32), BF16),
        w_mid_v=((27, 64, 64), BF16),
        w_down_v=((8, 32, 64), BF16),
        w_up_v=((8, 32, 64), BF16),
        w_in_v=((27, 32), BF16),
        head_v=((3, 32), BF16),
        meta=((nx, 16, 128), BF16),
        xgi=((nx, 32, 128), BF16),
        xgt=((nx, 96, 128), BF16),
        pli=((ny, 16, 128), BF16),
        plt=((ny, 48, 128), BF16),
        yri=((ny, 16, 128), BF16),
        yrt=((ny, 48, 128), BF16),
        mi=((16, 128), BF16),
        mt=((48, 128), BF16),
        hri=((5, 3, 16, 128), BF16),
        hrt=((3, 3, 48, 128), BF16),
        w0=((256, 32), BF16),
        w1=((256, 1024), BF16),
        w1b=((256, 1024), BF16),
        wm=((64, 768), BF16),
        wmb=((64, 768), BF16),
        tcol=((176, wide), BF16),
        tgt=((6, 32, wide), F32),
        h0s=((10, 256, wide), BF16),
        c0=((20, 256, wide), BF16),
        h1s=((8, 256, wide), BF16),
        cd=((8, 256, wide), BF16),
        qs=((6, 64, wide), BF16),
        ss=((6, 256, wide), BF16),
        gls=((6, 32, wide), BF16),
        gss=((6, 256, wide), BF16),
        cg=((6, 256, wide), BF16),
        gds=((4, 64, wide), BF16),
        cr=((8, 256, wide), BF16),
        grs=((4, 256, wide), BF16),
        gas=((2, 256, 128), BF16),
        errs=((6, 32, wide), BF16),
        vec=((ROWS, 128), F32),
        err=((48, 128), BF16),
        rc=((half, 128), F32),
        ac=((half, 128), F32),
        rx=((nx, rows_x, 128), F32),
        ax=((rows_x, 128), F32),
        ry=((ny, rows_y, 128), F32),
        ay=((rows_y, 128), F32),
        rz=((nzc, rows_y, 128), F32),
        gy=((ny, rows_y, 128), F32),
        gx=((nx, rows_x, 128), F32),
        gc=((nx, rows_x, 128), F32),
        ey=((ny, 48, 128), BF16),
        em=((nx, 96, 128), BF16),
        ex=((nx, 96, 128), BF16),
    )
    sems = dict(loaded=10)
    for kind, count in (
        ("name", nx),
        ("ix", nx),
        ("tx", nx),
        ("iy", ny),
        ("ty", ny),
        ("in", 14),
        ("tn", 14),
        ("ey", ny),
        ("ex", nx),
        ("c", 2),
        ("x", nx),
        ("y", ny),
        ("z", nzc),
        ("gy", ny),
        ("gx", nx),
    ):
        sems["s_" + kind] = count
        sems["r_" + kind] = count
    names = list(operands) + ["out", "tiles"] + list(buffers) + list(sems)
    return pl.pallas_call(
        functools.partial(whole_kernel, nx, ny, ng, names),
        out_shape=(
            jax.ShapeDtypeStruct((ROWS, 128), F32),
            jax.ShapeDtypeStruct((96, 128), BF16),
        ),
        in_specs=[pl.BlockSpec(memory_space=pltpu.MemorySpace.HBM)] * len(operands),
        out_specs=(VM, VM),
        scratch_shapes=[pltpu.VMEM(shape, dtype) for shape, dtype in buffers.values()]
        + [pltpu.SemaphoreType.DMA((count,)) for count in sems.values()],
        compiler_params=pltpu.CompilerParams(
            collective_id=0, has_side_effects=True, vmem_limit_bytes=40 << 20
        ),
        name="whole",
    )(*operands.values())


def unpack_kernel(vec, tiles, err, g_in, g_res, g_down, g_mid, g_up, g_head, lines):
    err[...] = tiles[...]
    for zy in range(9):
        strip = vec[RES + zy * 32 : RES + zy * 32 + 32, :]
        for c in range(3):
            part = strip if c == 0 else pltpu.roll(strip, 128 - 32 * c, 1)
            g_res[zy * 3 + c] = part[:, 0:32]
    for t in range(27):
        a, b, c = t // 9, t // 3 % 3, t % 3
        if b == 1:
            at = MID + (a * 2 + c // 2) * 64
            part = vec[at : at + 64, :]
            if c % 2:
                part = pltpu.roll(part, 64, 1)
            g_mid[t] = part[:, 0:64]
        else:
            g_mid[t] = jnp.zeros((64, 64), F32)
    for pos in range(8):
        quarter = pos & 3
        for at, grad in ((DOWN, g_down), (UP, g_up)):
            part = vec[at + quarter * 32 : at + quarter * 32 + 32, :]
            if pos >> 2:
                part = pltpu.roll(part, 64, 1)
            grad[tap_of(pos)] = part[:, 0:64]
        part = vec[INP + (pos >> 2) * 32 : INP + (pos >> 2) * 32 + 32, :]
        if quarter:
            part = pltpu.roll(part, 128 - 32 * quarter, 1)
        lines[pos] = part
    for t in range(27):
        dz, dy, dx = t // 9, t // 3 % 3, t % 3
        total = None
        for pos in range(8):
            xo, zo, yo = pos >> 2, pos >> 1 & 1, pos & 1
            if 0 <= yo + dy - 1 < 2:
                at = (zo + dz) * 8 + (xo + dx) * 2 + yo + dy - 1
                line = lines[pos, at : at + 1, :]
                total = line if total is None else total + line
        g_in[t : t + 1, :] = total[:, 0:32]
    g_head[...] = vec[HEAD : HEAD + 8, :][0:3, 0:32]


def unpack(vec, tiles):
    return pl.pallas_call(
        unpack_kernel,
        out_shape=(
            jax.ShapeDtypeStruct((96, 128), BF16),
            jax.ShapeDtypeStruct((27, 32), F32),
            jax.ShapeDtypeStruct((27, 32, 32), F32),
            jax.ShapeDtypeStruct((8, 32, 64), F32),
            jax.ShapeDtypeStruct((27, 64, 64), F32),
            jax.ShapeDtypeStruct((8, 32, 64), F32),
            jax.ShapeDtypeStruct((3, 32), F32),
        ),
        in_specs=[VM] * 2,
        out_specs=(VM,) * 7,
        scratch_shapes=[pltpu.VMEM((8, 32, 128), F32)],
        compiler_params=pltpu.CompilerParams(vmem_limit_bytes=32 << 20),
        name="unpack",
    )(vec, tiles)


def local(
    tile_image, tile_target, owner_counts, tile_list, w_in, w_res, w_down, w_mid, w_up, head_weight
):
    ranks = lax.axis_size("xy")
    ng = lax.axis_size("gz")
    nx, ny = grid_of(ranks)
    operands = dict(
        img=tile_image.reshape(SLOTS * 8, 128),
        target=tile_target.reshape(SLOTS * 24, 128),
        counts=owner_counts,
        tile_list=tile_list.reshape(1, SLOTS),
        w_in=w_in,
        w_res=w_res.reshape(9, 3, 32, 32),
        w_down=jnp.transpose(w_down, (0, 2, 1)),
        w_mid=w_mid,
        w_up=w_up,
        head=head_weight,
    )
    sums, tiles = whole(nx, ny, ng, operands)
    tiles, g_in, g_res, g_down, g_mid, g_up, g_head = unpack(sums, tiles)
    tiles = tiles.reshape(1, 1, SLOTS, 3, 4, 2, 128)
    return (tiles, g_in, g_res, jnp.transpose(g_down, (0, 2, 1)), g_mid, g_up, g_head)


def solution(mesh):
    return jax.shard_map(
        local,
        mesh=mesh,
        in_specs=(
            P("gz", "xy", None, None, None, None),
            P("gz", "xy", None, None, None, None, None),
            P("gz", "xy"),
            P("gz", "xy", None),
            P(),
            P(),
            P(),
            P(),
            P(),
            P(),
        ),
        out_specs=(P("gz", "xy", None, None, None, None, None), P(), P(), P(), P(), P(), P()),
        check_vma=False,
    )
```

```python
import functools
import types

import jax
import jax.numpy as jnp
from jax import lax
from jax.experimental import pallas as pl
from jax.experimental.pallas import tpu as pltpu
from jax.sharding import PartitionSpec as P

F32 = jnp.float32
BF16 = jnp.bfloat16
MESH = pl.DeviceIdType.MESH
SLOTS = 4
CORES = 2
ROWS = 1024
VM = pl.BlockSpec(memory_space=pltpu.VMEM)

RES, MID, DOWN, UP, INP, HEAD, USED = 0, 288, 672, 800, 928, 992, 1000


def grid_of(ranks):
    height = 8 if ranks == 32 else 2
    return ranks // height, height


def remote(src, dst, send, recv, where):
    return pltpu.make_async_remote_copy(
        src_ref=src, dst_ref=dst, send_sem=send, recv_sem=recv, device_id=where, device_id_type=MESH
    )


def iota(shape, dim):
    return lax.broadcasted_iota(jnp.int32, shape, dim)


def dot(a, b):
    return jnp.dot(a, b, preferred_element_type=F32)


def dot_t(a, b):
    return lax.dot_general(a, b, (((1,), (1,)), ((), ())), preferred_element_type=F32)


def hot(cond):
    return jnp.where(cond, 1.0, 0.0).astype(BF16)


def eye(n):
    return hot(iota((n, n), 0) == iota((n, n), 1))


def before(v):
    return pltpu.roll(v, 1, 1)


def after(v):
    return pltpu.roll(v, v.shape[1] - 1, 1)


def put_fine(buf, at, v):
    prev = before(v[128:256]).astype(BF16)
    succ = after(v[0:128]).astype(BF16)
    even = v[0:128].astype(BF16)
    odd = v[128:256].astype(BF16)
    for zo in range(2):
        for yo in range(2):
            rows = slice(zo * 64 + yo * 32, zo * 64 + yo * 32 + 32)
            for n, part in enumerate((prev, even, odd, succ)):
                buf[at + zo, yo * 128 + n * 32 : yo * 128 + n * 32 + 32, :] = part[rows]


def put_coarse(buf, at, v):
    buf[at, 0:64, :] = before(v).astype(BF16)
    buf[at, 64:128, :] = v.astype(BF16)
    buf[at, 128:192, :] = after(v).astype(BF16)
    buf[at, 192:256, :] = jnp.zeros((64, v.shape[1]), BF16)


def tap_of(pos):
    return (pos >> 1 & 1) * 4 + (pos & 1) * 2 + (pos >> 2)


def whole_kernel(nx, ny, ng, names, *refs):
    r = types.SimpleNamespace(**dict(zip(names, refs)))
    ranks = nx * ny
    nzc = ng // CORES
    nz = 2 * ng
    nx_cells = 128 * ranks
    voxels = float(ng * ranks * 2048)
    wide = 256
    g = lax.axis_index("gz")
    j = lax.axis_index("xy")
    xi = j // ny
    yi = lax.rem(j, ny)
    zi = g // CORES
    core = lax.rem(g, CORES)
    other = (zi * CORES + 1 - core, j)
    x_at = [lax.rem(xi + k, nx) for k in range(nx)]
    y_at = [lax.rem(yi + k, ny) for k in range(ny)]
    x_peer = [(g, x_at[k] * ny + yi) for k in range(nx)]
    y_peer = [(g, xi * ny + y_at[k]) for k in range(ny)]
    z_peer = [(lax.rem(zi + k, nzc) * CORES + core, j) for k in range(nzc)]
    around = [(dz, dj) for dz in (0, -1, 1, -2, 2) for dj in (0, -1, 1) if (dz, dj) != (0, 0)]
    near = [(lax.rem(g + dz + ng, ng), lax.rem(j + dj + ranks, ranks)) for dz, dj in around]

    moves = (
        (r.tile_list, r.list_v),
        (r.counts, r.count_v),
        (r.img, r.xgi.at[0]),
        (r.target, r.xgt.at[0]),
        (r.w_res, r.w_res_v),
        (r.w_mid, r.w_mid_v),
        (r.w_down, r.w_down_v),
        (r.w_up, r.w_up_v),
        (r.w_in, r.w_in_v),
        (r.head, r.head_v),
    )
    loads = [pltpu.make_async_copy(src, dst, r.loaded.at[n]) for n, (src, dst) in enumerate(moves)]
    for copy in loads:
        copy.start()
    barrier = pltpu.get_barrier_semaphore()
    peers = [other] + x_peer[1:] + y_peer[1:] + z_peer[1:] + near
    for peer in peers:
        pl.semaphore_signal(barrier, inc=1, device_id=peer, device_id_type=MESH)
    for copy in loads[0:2]:
        copy.wait()
    live = lax.broadcasted_iota(jnp.int32, (1, SLOTS), 1) < r.count_v[...]
    held = jnp.where(live, r.list_v[...], -1).astype(F32)
    lines = [jnp.broadcast_to(held[:, s : s + 1], (1, 128)) for s in range(SLOTS)]
    lines.append(jnp.zeros((12, 128), F32))
    r.meta[0] = jnp.concatenate(lines, axis=0).astype(BF16)
    pl.semaphore_wait(barrier, len(peers))

    name_x = [
        remote(r.meta.at[0], r.meta.at[k], r.s_name.at[k], r.r_name.at[k], x_peer[k])
        for k in range(1, nx)
    ]
    img_x = [
        remote(r.img, r.xgi.at[k], r.s_ix.at[k], r.r_ix.at[k], x_peer[k]) for k in range(1, nx)
    ]
    tgt_x = [
        remote(r.target, r.xgt.at[k], r.s_tx.at[k], r.r_tx.at[k], x_peer[k]) for k in range(1, nx)
    ]
    for copy in name_x + img_x + tgt_x:
        copy.start()
    for copy in loads[4:]:
        copy.wait()

    i32, i64 = eye(32), eye(64)
    for xo in range(2):
        fwd = jnp.zeros((288, 128), F32)
        for c in range(3):
            put = hot(iota((32, 128), 1) == iota((32, 128), 0) + 32 * (c + xo))
            fwd = fwd + dot(r.w_res_v[:, c].reshape(288, 32), put)
        fwd = fwd.astype(BF16)
        blank = jnp.zeros((32, 32), BF16)
        for zy in range(9):
            parts = [r.w_res_v[8 - zy, 2 - c] for c in range(3)]
            parts = [blank] + parts if xo else parts + [blank]
            bwd = dot_t(i32, jnp.concatenate(parts, axis=0)).astype(BF16)
            dz, dy = zy // 3, zy % 3
            for zo in range(2):
                for yo in range(2):
                    y_in = yo + dy - 1
                    if 0 <= y_in < 2:
                        rows = slice(xo * 128 + zo * 64 + yo * 32, xo * 128 + zo * 64 + yo * 32 + 32)
                        lanes = slice((zo + dz) * 256 + y_in * 128, (zo + dz) * 256 + y_in * 128 + 128)
                        r.w1[rows, lanes] = fwd[zy * 32 : zy * 32 + 32]
                        r.w1b[rows, lanes] = bwd
        for zo in range(2):
            for yo in range(2):
                rows = slice(xo * 128 + zo * 64 + yo * 32, xo * 128 + zo * 64 + yo * 32 + 32)
                lanes = slice((3 - 3 * zo) * 256, (3 - 3 * zo) * 256 + 256)
                r.w1[rows, lanes] = jnp.zeros((32, 256), BF16)
                r.w1b[rows, lanes] = jnp.zeros((32, 256), BF16)
    taps_t = dot_t(i32, r.w_in_v[...]).astype(BF16)
    col = iota((27, 32), 1)
    tap = iota((27, 32), 0)
    for pos in range(8):
        xo, zo, yo = pos >> 2, pos >> 1 & 1, pos & 1
        hit = jnp.zeros((27, 32), jnp.bool_)
        for t in range(27):
            dz, dy, dx = t // 9, t // 3 % 3, t % 3
            if 0 <= yo + dy - 1 < 2:
                at = (zo + dz) * 8 + (xo + dx) * 2 + yo + dy - 1
                hit = hit | ((tap == t) & (col == at))
        r.w0[pos * 32 : pos * 32 + 32, :] = dot(taps_t, hot(hit)).astype(BF16)
    wd_t = jnp.concatenate([r.w_down_v[tap_of(p)] for p in range(8)], axis=0)
    wd = dot_t(i64, wd_t).astype(BF16)
    wu = jnp.concatenate([r.w_up_v[tap_of(p)] for p in range(8)], axis=0)
    wu_t = dot_t(i64, wu).astype(BF16)
    blank = jnp.zeros((64, 64), BF16)
    for a in range(3):
        fwd = [dot_t(i64, r.w_mid_v[9 * a + 3 + c]).astype(BF16) for c in range(3)] + [blank]
        bwd = [r.w_mid_v[26 - (9 * a + 3 + c)] for c in range(3)] + [blank]
        r.wm[:, a * 256 : a * 256 + 256] = dot_t(i64, jnp.concatenate(fwd, axis=0)).astype(BF16)
        r.wmb[:, a * 256 : a * 256 + 256] = dot_t(i64, jnp.concatenate(bwd, axis=0)).astype(BF16)
    heads = dot(r.head_v[...], hot((iota((32, 256), 1) & 31) == iota((32, 256), 0)))
    hd = jnp.concatenate(
        [jnp.broadcast_to(heads[a : a + 1], (8, 256)) for a in range(3)]
        + [jnp.zeros((8, 256), F32)],
        axis=0,
    )
    same = (iota((32, 256), 0) & 7) == (iota((32, 256), 1) >> 5)
    hd = jnp.where(same, hd, 0.0).astype(BF16)
    hd_t = dot_t(eye(256), hd).astype(BF16)


    for copy in [loads[2]]:
        copy.wait()
    for copy in name_x + img_x:
        copy.wait_recv()

    def select(k, tiles, rows):
        first = ((xi * ny + lax.rem(yi + k, ny)) * 2).astype(F32)
        sums = [jnp.zeros((rows, 128), F32), jnp.zeros((rows, 128), F32)]
        for a in range(nx):
            called = r.meta[a].astype(F32)
            held = tiles[a].astype(F32)
            for s in range(SLOTS):
                tile = held[s * rows : s * rows + rows]
                for t in range(2):
                    sums[t] = sums[t] + jnp.where(called[s : s + 1] == first + t, tile, 0.0)
        return jnp.concatenate(sums, axis=0).astype(BF16)

    def img_y(k):
        peer = (g, xi * ny + lax.rem(yi + k, ny))
        return remote(r.pli.at[k], r.yri.at[k], r.s_iy.at[k], r.r_iy.at[k], peer)

    def tgt_y(k):
        peer = (g, xi * ny + lax.rem(yi + k, ny))
        return remote(r.plt.at[k], r.yrt.at[k], r.s_ty.at[k], r.r_ty.at[k], peer)

    def send_img(k, carry):
        r.pli[k] = select(k, r.xgi, 8)
        img_y(k).start()
        return carry

    def send_tgt(k, carry):
        r.plt[k] = select(k, r.xgt, 24)
        tgt_y(k).start()
        return carry

    lax.fori_loop(1, ny, send_img, 0)
    loads[3].wait()
    for copy in tgt_x:
        copy.wait_recv()
    lax.fori_loop(1, ny, send_tgt, 0)
    r.pli[0] = select(0, r.xgi, 8)
    r.plt[0] = select(0, r.xgt, 24)

    total = r.pli[0].astype(F32)
    for k in range(1, ny):
        img_y(k).wait_recv()
        total = total + r.yri[k].astype(F32)
    r.mi[...] = total.astype(BF16)
    img_n = [
        remote(r.mi, r.hri.at[2 - dz, 1 - dj], r.s_in.at[n], r.r_in.at[n], near[n])
        for n, (dz, dj) in enumerate(around)
    ]
    for copy in img_n:
        copy.start()
    r.hri[2, 1] = r.mi[...]
    total = r.plt[0].astype(F32)
    for k in range(1, ny):
        tgt_y(k).wait_recv()
        total = total + r.yrt[k].astype(F32)
    r.mt[...] = total.astype(BF16)
    tgt_n = [
        remote(r.mt, r.hrt.at[1 - dz, 1 - dj], r.s_tn.at[n], r.r_tn.at[n], near[n])
        for n, (dz, dj) in enumerate(around)
        if abs(dz) < 2
    ]
    for copy in tgt_n:
        copy.start()
    r.hrt[1, 1] = r.mt[...]
    for copy in img_n:
        copy.wait_recv()

    def wide_rows(ref, z, rows):
        left, own, right = (ref[z, n].astype(F32) for n in range(3))
        return jnp.concatenate([left[rows:], own[:rows], own[rows:], right[:rows]], axis=1)

    image = jnp.concatenate([wide_rows(r.hri, z, 8) for z in range(5)], axis=0)
    z2 = iota((40, 512), 0) + 8 * g - 16
    x1 = iota((40, 512), 1) + 256 * j - 128
    inside = (z2 >= 0) & (z2 < 4 * nz) & (x1 >= 0) & (x1 < 2 * nx_cells)
    image = jnp.where(inside, image, 0.0).astype(BF16)
    place = iota((512, wide), 0)
    lane2 = 2 * iota((512, wide), 1) + 128
    pick = [hot(place == ((lane2 + k) & 511)) for k in (-1, 0, 1, 2)]
    parts = jnp.concatenate([dot(image, p) for p in pick], axis=0).astype(BF16)
    row = iota((176, 160), 0)
    zrow = row >> 3
    source = ((row >> 1) & 3) * 40 + (zrow - 1) * 2 + (row & 1)
    order = hot((iota((176, 160), 1) == source) & (zrow >= 1) & (zrow <= 20))
    r.tcol[...] = dot(order, parts).astype(BF16)

    lane = iota((1, wide), 1)
    cell = jnp.where(lane < 192, lane, lane - 256) + 128 * j
    lane_in = jnp.where((cell >= 0) & (cell < nx_cells), 1.0, 0.0)

    def in_slab(zc):
        at = 2 * g + zc
        return lane_in * jnp.where((at >= 0) & (at < nz), 1.0, 0.0)

    def first_conv(n, carry):
        rows = r.tcol[pl.ds(pl.multiple_of(n * 16, 16), 32), :]
        h0 = jnp.maximum(dot(r.w0[...], rows), 0.0) * in_slab(n - 4)
        r.h0s[n] = h0.astype(BF16)
        put_fine(r.c0, 2 * n, h0)
        return carry

    lax.fori_loop(0, 10, first_conv, 0, unroll=True)

    def second_conv(n, carry):
        cols = r.c0[pl.ds(2 * n + 1, 4)].reshape(1024, wide)
        h1 = jnp.maximum(r.h0s[n + 1].astype(F32) + dot(r.w1[...], cols), 0.0).astype(BF16)
        r.h1s[n] = h1
        put_coarse(r.cd, n, jnp.maximum(dot(wd, h1), 0.0) * in_slab(n - 3))
        return carry

    lax.fori_loop(0, 8, second_conv, 0, unroll=True)


    for copy in tgt_n:
        copy.wait_recv()
    target = jnp.concatenate([wide_rows(r.hrt, z, 24) for z in range(3)], axis=0).astype(BF16)
    parts = jnp.concatenate([dot(target, p) for p in pick[1:3]], axis=0).astype(BF16)
    row = iota((192, 144), 0)
    source = (
        ((row >> 2) & 1) * 72
        + (row >> 6) * 24
        + ((row >> 3) & 3) * 8
        + (((row >> 5) & 1) * 2 + ((row >> 1) & 1)) * 2
        + (row & 1)
    )
    order = hot((iota((192, 144), 1) == source) & (((row >> 3) & 3) < 3))
    placed = dot(order, parts)
    for n in range(6):
        r.tgt[n] = placed[n * 32 : n * 32 + 32]


    def middle(n, carry):
        cols = r.cd[pl.ds(n, 3)].reshape(768, wide)
        q = jnp.maximum(r.cd[n + 1, 64:128].astype(F32) + dot(r.wm[...], cols), 0.0).astype(BF16)
        r.qs[n] = q
        s = jnp.maximum(r.h1s[n + 1].astype(F32) + dot(wu, q), 0.0).astype(BF16)
        r.ss[n] = s
        aff = jax.nn.sigmoid(dot(hd, s))
        err = aff - r.tgt[n]
        r.errs[n] = err.astype(BF16)
        gl = (err * aff * (1.0 - aff) / voxels).astype(BF16)
        r.gls[n] = gl
        gs = jnp.where(s.astype(F32) > 0, dot(hd_t, gl), 0.0).astype(BF16)
        r.gss[n] = gs
        gq = jnp.where(q.astype(F32) > 0, dot(wu_t, gs), 0.0) * in_slab(n - 2)
        put_coarse(r.cg, n, gq)
        return carry

    lax.fori_loop(0, 6, middle, 0, unroll=True)


    def own(ref, first):
        return jnp.concatenate([ref[first, :, 0:128], ref[first + 1, :, 0:128]], axis=1)


    rows = jnp.concatenate([r.errs[2, :, 0:128], r.errs[3, :, 0:128]], axis=0)
    src = iota((128, 256), 0)
    dst = iota((128, 256), 1)
    parts = jnp.concatenate([dot(rows, hot(dst == 2 * src + xo)) for xo in range(2)], axis=0)
    row = iota((32, 128), 0)
    source = ((row >> 2) & 1) * 32 + (row >> 3) * 8 + ((row >> 1) & 1) * 2 + (row & 1)
    q = iota((32, 128), 1)
    order = hot((q == source) | (q == source + 68))
    tiles = dot(order, parts.astype(BF16))
    r.err[...] = jnp.concatenate([tiles[0:24, 0:128], tiles[0:24, 128:256]], axis=0).astype(BF16)


    err_y = [remote(r.err, r.ey.at[k], r.s_ey.at[k], r.r_ey.at[k], y_peer[k]) for k in range(1, ny)]
    for copy in err_y:
        copy.start()
    r.ey[0] = r.err[...]

    def back(n, carry):
        cols = r.cg[pl.ds(n, 3)].reshape(768, wide)
        gdd = r.cg[n + 1, 64:128].astype(F32) + dot(r.wmb[...], cols)
        gdd = jnp.where(r.cd[n + 2, 64:128].astype(F32) > 0, gdd, 0.0).astype(BF16)
        r.gds[n] = gdd
        gr = r.gss[n + 1].astype(F32) + dot(wd_t, gdd)
        gr = jnp.where(r.h1s[n + 2].astype(F32) > 0, gr, 0.0) * in_slab(n - 1)
        r.grs[n] = gr.astype(BF16)
        put_fine(r.cr, 2 * n, gr)
        return carry

    lax.fori_loop(0, 4, back, 0, unroll=True)

    for n in range(2):
        cols = r.cr[2 * n + 1 : 2 * n + 5, :, 0:128].reshape(1024, 128)
        ga = r.grs[n + 1, :, 0:128].astype(F32) + dot(r.w1b[...], cols)
        r.gas[n] = jnp.where(r.h0s[n + 4, :, 0:128].astype(F32) > 0, ga, 0.0).astype(BF16)


    gr = own(r.grs, 1)
    for z_in in range(4):
        for y_in in range(2):
            lanes = slice(y_in * 128, y_in * 128 + 128)
            cols = jnp.concatenate([r.c0[7 + z_in, lanes, 0:128], r.c0[9 + z_in, lanes, 0:128]], axis=1)
            part = dot_t(gr, cols)
            for zo in range(2):
                for yo in range(2):
                    dz, dy = z_in - zo, y_in - yo + 1
                    if 0 <= dz < 3:
                        rows = zo * 64 + yo * 32
                        both = part[rows : rows + 32] + pltpu.roll(
                            part[128 + rows : 128 + rows + 32], 96, 1
                        )
                        at = RES + (dz * 3 + dy) * 32
                        if z_in == dz and y_in == max(dy - 1, 0):
                            r.vec[at : at + 32, :] = both
                        else:
                            r.vec[at : at + 32, :] += both
    gq = jnp.concatenate([r.cg[2, 64:128, 0:128], r.cg[3, 64:128, 0:128]], axis=1)
    for a in range(3):
        for half in range(2):
            lanes = slice(half * 128, half * 128 + 128)
            cols = jnp.concatenate([r.cd[2 + a, lanes, 0:128], r.cd[3 + a, lanes, 0:128]], axis=1)
            at = MID + (a * 2 + half) * 64
            r.vec[at : at + 64, :] = dot_t(gq, cols)
    gdd = own(r.gds, 1)
    none = jnp.zeros((64, 256), BF16)
    for at, fine, coarse in ((DOWN, own(r.h1s, 3), gdd), (UP, own(r.gss, 2), own(r.qs, 2))):
        r.vec[at : at + 128, :] = dot_t(
            fine[0:128], jnp.concatenate([coarse, none], axis=0)
        ) + dot_t(fine[128:256], jnp.concatenate([none, coarse], axis=0))
    cols = jnp.concatenate([r.tcol[64:96, 0:128], r.tcol[80:112, 0:128]], axis=1)
    inp = dot_t(cols, own(r.gas, 0))
    r.vec[INP : INP + 32, :] = inp[:, 0:128]
    r.vec[INP + 32 : INP + 64, :] = inp[:, 128:256]
    heads = jnp.where(same, dot_t(own(r.gls, 2), own(r.ss, 2)), 0.0)
    r.vec[HEAD:ROWS, :] = jnp.zeros((ROWS - HEAD, 128), F32)
    for a in range(3):
        line = jnp.sum(heads[a * 8 : a * 8 + 8], axis=0, keepdims=True)
        line = line[:, 0:128] + line[:, 128:256]
        line = line + pltpu.roll(line, 64, 1)
        line = line + pltpu.roll(line, 32, 1)
        r.vec[HEAD + a : HEAD + a + 1, :] = line


    half = ROWS // CORES
    rows_x = half // nx

    def piece(k, size):
        return pl.ds(pl.multiple_of(k * size, size), size)

    swap = remote(r.vec.at[piece(1 - core, half)], r.rc, r.s_c.at[0], r.r_c.at[0], other)
    swap.start()
    for copy in err_y:
        copy.wait_recv()

    def answer(a, carry):
        called = r.meta[a].astype(F32)
        sums = [jnp.zeros((24, 128), F32) for _ in range(SLOTS)]
        for k in range(ny):
            first = ((xi * ny + lax.rem(yi - k + ny, ny)) * 2).astype(F32)
            pair = r.ey[k].astype(F32)
            for t in range(2):
                for s in range(SLOTS):
                    sums[s] = sums[s] + jnp.where(
                        called[s : s + 1] == first + t, pair[t * 24 : t * 24 + 24], 0.0
                    )
        r.em[a] = jnp.concatenate(sums, axis=0).astype(BF16)
        return carry

    lax.fori_loop(0, nx, answer, 0)
    swap.wait_recv()
    r.ac[...] = r.vec[piece(core, half), :] + r.rc[...]
    over_x = [
        remote(r.ac.at[piece(x_at[k], rows_x)], r.rx.at[k], r.s_x.at[k], r.r_x.at[k], x_peer[k])
        for k in range(1, nx)
    ]
    err_x = [
        remote(r.em.at[nx - k], r.ex.at[k], r.s_ex.at[k], r.r_ex.at[k], x_peer[k])
        for k in range(1, nx)
    ]
    for copy in over_x + err_x:
        copy.start()
    for copy in over_x:
        copy.wait_recv()
    total = r.ac[piece(xi, rows_x), :]
    for k in range(1, nx):
        total = total + r.rx[k]

    def share(buf, at, peers, send, recv):
        return [
            remote(buf.at[at], buf.at[at], send.at[k], recv.at[k], peers[k])
            for k in range(1, len(peers))
        ]

    def gathered(buf, at, peers, send, recv):
        count = len(peers)
        for k in range(1, count):
            where = lax.rem(at - k + count, count)
            remote(buf.at[where], buf.at[where], send.at[k], recv.at[k], peers[k]).wait_recv()
        total = buf[0].astype(F32)
        for n in range(1, count):
            total = total + buf[n].astype(F32)
        return total

    part = rows_x // 2
    r.ya[yi] = total[0:part].astype(r.ya.dtype)
    y_first = share(r.ya, yi, y_peer, r.s_ya, r.r_ya)
    for copy in y_first:
        copy.start()
    r.za[zi] = total[part:].astype(r.za.dtype)
    z_first = share(r.za, zi, z_peer, r.s_za, r.r_za)
    for copy in z_first:
        copy.start()
    r.zb[zi] = gathered(r.ya, yi, y_peer, r.s_ya, r.r_ya).astype(r.zb.dtype)
    z_then = share(r.zb, zi, z_peer, r.s_zb, r.r_zb)
    for copy in z_then:
        copy.start()
    r.yb[yi] = gathered(r.za, zi, z_peer, r.s_za, r.r_za).astype(r.yb.dtype)
    y_then = share(r.yb, yi, y_peer, r.s_yb, r.r_yb)
    for copy in y_then:
        copy.start()
    r.gx[xi, 0:part] = gathered(r.zb, zi, z_peer, r.s_zb, r.r_zb)
    r.gx[xi, part:] = gathered(r.yb, yi, y_peer, r.s_yb, r.r_yb)
    back_x = [
        remote(r.gx.at[xi], r.gx.at[xi], r.s_gx.at[k], r.r_gx.at[k], x_peer[k])
        for k in range(1, nx)
    ]
    for copy in back_x:
        copy.start()
    for k in range(1, nx):
        at = lax.rem(xi - k + nx, nx)
        remote(r.gx.at[at], r.gx.at[at], r.s_gx.at[k], r.r_gx.at[k], x_peer[k]).wait_recv()
    back_c = remote(r.gx, r.gc, r.s_c.at[1], r.r_c.at[1], other)
    back_c.start()
    r.out[piece(core, half), :] = r.gx[...].reshape(half, 128)
    for copy in err_x:
        copy.wait_recv()
    total = r.em[0].astype(F32)
    for k in range(1, nx):
        total = total + r.ex[k].astype(F32)
    r.tiles[...] = total.astype(BF16)
    back_c.wait_recv()
    r.out[piece(1 - core, half), :] = r.gc[...].reshape(half, 128)
    sent = [swap, back_c] + name_x + img_x + tgt_x + img_n + tgt_n + err_y + err_x
    sent += [img_y(k) for k in range(1, ny)] + [tgt_y(k) for k in range(1, ny)]
    for copy in sent + over_x + y_first + z_first + z_then + y_then + back_x:
        copy.wait_send()


def whole(nx, ny, ng, operands):
    wide = 256
    nzc = ng // CORES
    half = ROWS // CORES
    rows_x = half // nx
    buffers = dict(
        list_v=((1, SLOTS), jnp.int32),
        count_v=((1, 1), jnp.int32),
        w_res_v=((9, 3, 32, 32), BF16),
        w_mid_v=((27, 64, 64), BF16),
        w_down_v=((8, 32, 64), BF16),
        w_up_v=((8, 32, 64), BF16),
        w_in_v=((27, 32), BF16),
        head_v=((3, 32), BF16),
        meta=((nx, 16, 128), BF16),
        xgi=((nx, 32, 128), BF16),
        xgt=((nx, 96, 128), BF16),
        pli=((ny, 16, 128), BF16),
        plt=((ny, 48, 128), BF16),
        yri=((ny, 16, 128), BF16),
        yrt=((ny, 48, 128), BF16),
        mi=((16, 128), BF16),
        mt=((48, 128), BF16),
        hri=((5, 3, 16, 128), BF16),
        hrt=((3, 3, 48, 128), BF16),
        w0=((256, 32), BF16),
        w1=((256, 1024), BF16),
        w1b=((256, 1024), BF16),
        wm=((64, 768), BF16),
        wmb=((64, 768), BF16),
        tcol=((176, wide), BF16),
        tgt=((6, 32, wide), F32),
        h0s=((10, 256, wide), BF16),
        c0=((20, 256, wide), BF16),
        h1s=((8, 256, wide), BF16),
        cd=((8, 256, wide), BF16),
        qs=((6, 64, wide), BF16),
        ss=((6, 256, wide), BF16),
        gls=((6, 32, wide), BF16),
        gss=((6, 256, wide), BF16),
        cg=((6, 256, wide), BF16),
        gds=((4, 64, wide), BF16),
        cr=((8, 256, wide), BF16),
        grs=((4, 256, wide), BF16),
        gas=((2, 256, 128), BF16),
        errs=((6, 32, wide), BF16),
        vec=((ROWS, 128), F32),
        err=((48, 128), BF16),
        rc=((half, 128), F32),
        ac=((half, 128), F32),
        rx=((nx, rows_x, 128), F32),
        ya=((ny, rows_x // 2, 128), F32),
        za=((nzc, rows_x // 2, 128), F32),
        yb=((ny, rows_x // 2, 128), F32),
        zb=((nzc, rows_x // 2, 128), F32),
        gx=((nx, rows_x, 128), F32),
        gc=((nx, rows_x, 128), F32),
        ey=((ny, 48, 128), BF16),
        em=((nx, 96, 128), BF16),
        ex=((nx, 96, 128), BF16),
    )
    sems = dict(loaded=10)
    for kind, count in (
        ("name", nx),
        ("ix", nx),
        ("tx", nx),
        ("iy", ny),
        ("ty", ny),
        ("in", 14),
        ("tn", 14),
        ("ey", ny),
        ("ex", nx),
        ("c", 2),
        ("x", nx),
        ("ya", ny),
        ("za", nzc),
        ("yb", ny),
        ("zb", nzc),
        ("gx", nx),
    ):
        sems["s_" + kind] = count
        sems["r_" + kind] = count
    names = list(operands) + ["out", "tiles"] + list(buffers) + list(sems)
    return pl.pallas_call(
        functools.partial(whole_kernel, nx, ny, ng, names),
        out_shape=(
            jax.ShapeDtypeStruct((ROWS, 128), F32),
            jax.ShapeDtypeStruct((96, 128), BF16),
        ),
        in_specs=[pl.BlockSpec(memory_space=pltpu.MemorySpace.HBM)] * len(operands),
        out_specs=(VM, VM),
        scratch_shapes=[pltpu.VMEM(shape, dtype) for shape, dtype in buffers.values()]
        + [pltpu.SemaphoreType.DMA((count,)) for count in sems.values()],
        compiler_params=pltpu.CompilerParams(
            collective_id=0, has_side_effects=True, vmem_limit_bytes=56 << 20
        ),
        name="whole",
    )(*operands.values())


def unpack_kernel(
    sums, tiles, err, g_in, g_res, g_down, g_mid, g_up, g_head, lines, vec, sems
):
    load = pltpu.make_async_copy(sums, vec, sems.at[0])
    load.start()
    load_err = pltpu.make_async_copy(tiles, err, sems.at[1])
    load_err.start()
    for t in range(27):
        if t // 3 % 3 != 1:
            g_mid[t] = jnp.zeros((64, 64), F32)
    load.wait()
    for zy in range(9):
        strip = vec[RES + zy * 32 : RES + zy * 32 + 32, :]
        for c in range(3):
            part = strip if c == 0 else pltpu.roll(strip, 128 - 32 * c, 1)
            g_res[zy * 3 + c] = part[:, 0:32]
    for t in range(27):
        a, b, c = t // 9, t // 3 % 3, t % 3
        if b == 1:
            at = MID + (a * 2 + c // 2) * 64
            part = vec[at : at + 64, :]
            if c % 2:
                part = pltpu.roll(part, 64, 1)
            g_mid[t] = part[:, 0:64]
    for pos in range(8):
        quarter = pos & 3
        for at, grad in ((DOWN, g_down), (UP, g_up)):
            part = vec[at + quarter * 32 : at + quarter * 32 + 32, :]
            if pos >> 2:
                part = pltpu.roll(part, 64, 1)
            grad[tap_of(pos)] = part[:, 0:64]
        part = vec[INP + (pos >> 2) * 32 : INP + (pos >> 2) * 32 + 32, :]
        if quarter:
            part = pltpu.roll(part, 128 - 32 * quarter, 1)
        lines[pos] = part
    for t in range(27):
        dz, dy, dx = t // 9, t // 3 % 3, t % 3
        total = None
        for pos in range(8):
            xo, zo, yo = pos >> 2, pos >> 1 & 1, pos & 1
            if 0 <= yo + dy - 1 < 2:
                at = (zo + dz) * 8 + (xo + dx) * 2 + yo + dy - 1
                line = lines[pos, at : at + 1, :]
                total = line if total is None else total + line
        g_in[t : t + 1, :] = total[:, 0:32]
    g_head[...] = vec[HEAD : HEAD + 8, :][0:3, 0:32]
    load_err.wait()


def unpack(vec, tiles):
    return pl.pallas_call(
        unpack_kernel,
        out_shape=(
            jax.ShapeDtypeStruct((96, 128), BF16),
            jax.ShapeDtypeStruct((27, 32), F32),
            jax.ShapeDtypeStruct((27, 32, 32), F32),
            jax.ShapeDtypeStruct((8, 32, 64), F32),
            jax.ShapeDtypeStruct((27, 64, 64), F32),
            jax.ShapeDtypeStruct((8, 32, 64), F32),
            jax.ShapeDtypeStruct((3, 32), F32),
        ),
        in_specs=[pl.BlockSpec(memory_space=pltpu.MemorySpace.HBM)] * 2,
        out_specs=(VM,) * 7,
        scratch_shapes=[
            pltpu.VMEM((8, 32, 128), F32),
            pltpu.VMEM((ROWS, 128), F32),
            pltpu.SemaphoreType.DMA((2,)),
        ],
        compiler_params=pltpu.CompilerParams(vmem_limit_bytes=56 << 20),
        name="unpack",
    )(vec, tiles)


def local(
    tile_image, tile_target, owner_counts, tile_list, w_in, w_res, w_down, w_mid, w_up, head_weight
):
    ranks = lax.axis_size("xy")
    ng = lax.axis_size("gz")
    nx, ny = grid_of(ranks)
    operands = dict(
        img=tile_image.reshape(SLOTS * 8, 128),
        target=tile_target.reshape(SLOTS * 24, 128),
        counts=owner_counts,
        tile_list=tile_list.reshape(1, SLOTS),
        w_in=w_in,
        w_res=w_res.reshape(9, 3, 32, 32),
        w_down=jnp.transpose(w_down, (0, 2, 1)),
        w_mid=w_mid,
        w_up=w_up,
        head=head_weight,
    )
    sums, tiles = whole(nx, ny, ng, operands)
    tiles, g_in, g_res, g_down, g_mid, g_up, g_head = unpack(sums, tiles)
    tiles = tiles.reshape(1, 1, SLOTS, 3, 4, 2, 128)
    return (tiles, g_in, g_res, jnp.transpose(g_down, (0, 2, 1)), g_mid, g_up, g_head)


def solution(mesh):
    return jax.shard_map(
        local,
        mesh=mesh,
        in_specs=(
            P("gz", "xy", None, None, None, None),
            P("gz", "xy", None, None, None, None, None),
            P("gz", "xy"),
            P("gz", "xy", None),
            P(),
            P(),
            P(),
            P(),
            P(),
            P(),
        ),
        out_specs=(P("gz", "xy", None, None, None, None, None), P(), P(), P(), P(), P(), P()),
        check_vma=False,
    )
```

```python
import functools
import types

import jax
import jax.numpy as jnp
from jax import lax
from jax.experimental import pallas as pl
from jax.experimental.pallas import tpu as pltpu
from jax.sharding import PartitionSpec as P

F32 = jnp.float32
BF16 = jnp.bfloat16
MESH = pl.DeviceIdType.MESH
SLOTS = 4
CORES = 2
ROWS = 1024
VM = pl.BlockSpec(memory_space=pltpu.VMEM)

RES, MID, DOWN, UP, INP, HEAD, USED = 0, 288, 672, 800, 928, 992, 1000


def grid_of(ranks):
    height = 8 if ranks == 32 else 2
    return ranks // height, height


def remote(src, dst, send, recv, where):
    return pltpu.make_async_remote_copy(
        src_ref=src, dst_ref=dst, send_sem=send, recv_sem=recv, device_id=where, device_id_type=MESH
    )


def iota(shape, dim):
    return lax.broadcasted_iota(jnp.int32, shape, dim)


def dot(a, b):
    return jnp.dot(a, b, preferred_element_type=F32)


def dot_t(a, b):
    return lax.dot_general(a, b, (((1,), (1,)), ((), ())), preferred_element_type=F32)


def hot(cond):
    return jnp.where(cond, 1.0, 0.0).astype(BF16)


def eye(n):
    return hot(iota((n, n), 0) == iota((n, n), 1))


def before(v):
    return pltpu.roll(v, 1, 1)


def after(v):
    return pltpu.roll(v, v.shape[1] - 1, 1)


def put_fine(buf, at, v):
    prev = before(v[128:256]).astype(BF16)
    succ = after(v[0:128]).astype(BF16)
    even = v[0:128].astype(BF16)
    odd = v[128:256].astype(BF16)
    for zo in range(2):
        for yo in range(2):
            rows = slice(zo * 64 + yo * 32, zo * 64 + yo * 32 + 32)
            for n, part in enumerate((prev, even, odd, succ)):
                buf[at + zo, yo * 128 + n * 32 : yo * 128 + n * 32 + 32, :] = part[rows]


def put_coarse(buf, at, v):
    buf[at, 0:64, :] = before(v).astype(BF16)
    buf[at, 64:128, :] = v.astype(BF16)
    buf[at, 128:192, :] = after(v).astype(BF16)
    buf[at, 192:256, :] = jnp.zeros((64, v.shape[1]), BF16)


def tap_of(pos):
    return (pos >> 1 & 1) * 4 + (pos & 1) * 2 + (pos >> 2)


def whole_kernel(nx, ny, ng, names, *refs):
    r = types.SimpleNamespace(**dict(zip(names, refs)))
    ranks = nx * ny
    nzc = ng // CORES
    nz = 2 * ng
    nx_cells = 128 * ranks
    voxels = float(ng * ranks * 2048)
    wide = 256
    g = lax.axis_index("gz")
    j = lax.axis_index("xy")
    xi = j // ny
    yi = lax.rem(j, ny)
    zi = g // CORES
    core = lax.rem(g, CORES)
    other = (zi * CORES + 1 - core, j)
    x_at = [lax.rem(xi + k, nx) for k in range(nx)]
    y_at = [lax.rem(yi + k, ny) for k in range(ny)]
    x_peer = [(g, x_at[k] * ny + yi) for k in range(nx)]
    y_peer = [(g, xi * ny + y_at[k]) for k in range(ny)]
    z_peer = [(lax.rem(zi + k, nzc) * CORES + core, j) for k in range(nzc)]
    around = [(dz, dj) for dz in (0, -1, 1, -2, 2) for dj in (0, -1, 1) if (dz, dj) != (0, 0)]
    near = [(lax.rem(g + dz + ng, ng), lax.rem(j + dj + ranks, ranks)) for dz, dj in around]

    moves = (
        (r.tile_list, r.list_v),
        (r.counts, r.count_v),
        (r.img, r.xgi.at[0]),
        (r.target, r.xgt.at[0]),
        (r.w_res, r.w_res_v),
        (r.w_mid, r.w_mid_v),
        (r.w_down, r.w_down_v),
        (r.w_up, r.w_up_v),
        (r.w_in, r.w_in_v),
        (r.head, r.head_v),
    )
    loads = [pltpu.make_async_copy(src, dst, r.loaded.at[n]) for n, (src, dst) in enumerate(moves)]
    for copy in loads:
        copy.start()
    barrier = pltpu.get_barrier_semaphore()
    peers = [other] + x_peer[1:] + y_peer[1:] + z_peer[1:] + near
    for peer in peers:
        pl.semaphore_signal(barrier, inc=1, device_id=peer, device_id_type=MESH)
    for copy in loads[0:2]:
        copy.wait()
    live = lax.broadcasted_iota(jnp.int32, (1, SLOTS), 1) < r.count_v[...]
    held = jnp.where(live, r.list_v[...], -1).astype(F32)
    lines = [jnp.broadcast_to(held[:, s : s + 1], (1, 128)) for s in range(SLOTS)]
    lines.append(jnp.zeros((12, 128), F32))
    r.meta[0] = jnp.concatenate(lines, axis=0).astype(BF16)
    pl.semaphore_wait(barrier, len(peers))

    name_x = [
        remote(r.meta.at[0], r.meta.at[k], r.s_name.at[k], r.r_name.at[k], x_peer[k])
        for k in range(1, nx)
    ]
    img_x = [
        remote(r.img, r.xgi.at[k], r.s_ix.at[k], r.r_ix.at[k], x_peer[k]) for k in range(1, nx)
    ]
    tgt_x = [
        remote(r.target, r.xgt.at[k], r.s_tx.at[k], r.r_tx.at[k], x_peer[k]) for k in range(1, nx)
    ]
    for copy in name_x + img_x + tgt_x:
        copy.start()
    for copy in loads[4:]:
        copy.wait()

    i32, i64 = eye(32), eye(64)
    for xo in range(2):
        fwd = jnp.zeros((288, 128), F32)
        for c in range(3):
            put = hot(iota((32, 128), 1) == iota((32, 128), 0) + 32 * (c + xo))
            fwd = fwd + dot(r.w_res_v[:, c].reshape(288, 32), put)
        fwd = fwd.astype(BF16)
        blank = jnp.zeros((32, 32), BF16)
        for zy in range(9):
            parts = [r.w_res_v[8 - zy, 2 - c] for c in range(3)]
            parts = [blank] + parts if xo else parts + [blank]
            bwd = dot_t(i32, jnp.concatenate(parts, axis=0)).astype(BF16)
            dz, dy = zy // 3, zy % 3
            for zo in range(2):
                for yo in range(2):
                    y_in = yo + dy - 1
                    if 0 <= y_in < 2:
                        rows = slice(xo * 128 + zo * 64 + yo * 32, xo * 128 + zo * 64 + yo * 32 + 32)
                        lanes = slice((zo + dz) * 256 + y_in * 128, (zo + dz) * 256 + y_in * 128 + 128)
                        r.w1[rows, lanes] = fwd[zy * 32 : zy * 32 + 32]
                        r.w1b[rows, lanes] = bwd
        for zo in range(2):
            for yo in range(2):
                rows = slice(xo * 128 + zo * 64 + yo * 32, xo * 128 + zo * 64 + yo * 32 + 32)
                lanes = slice((3 - 3 * zo) * 256, (3 - 3 * zo) * 256 + 256)
                r.w1[rows, lanes] = jnp.zeros((32, 256), BF16)
                r.w1b[rows, lanes] = jnp.zeros((32, 256), BF16)
    taps_t = dot_t(i32, r.w_in_v[...]).astype(BF16)
    col = iota((27, 32), 1)
    tap = iota((27, 32), 0)
    for pos in range(8):
        xo, zo, yo = pos >> 2, pos >> 1 & 1, pos & 1
        hit = jnp.zeros((27, 32), jnp.bool_)
        for t in range(27):
            dz, dy, dx = t // 9, t // 3 % 3, t % 3
            if 0 <= yo + dy - 1 < 2:
                at = (zo + dz) * 8 + (xo + dx) * 2 + yo + dy - 1
                hit = hit | ((tap == t) & (col == at))
        r.w0[pos * 32 : pos * 32 + 32, :] = dot(taps_t, hot(hit)).astype(BF16)
    wd_t = jnp.concatenate([r.w_down_v[tap_of(p)] for p in range(8)], axis=0)
    wd = dot_t(i64, wd_t).astype(BF16)
    wu = jnp.concatenate([r.w_up_v[tap_of(p)] for p in range(8)], axis=0)
    wu_t = dot_t(i64, wu).astype(BF16)
    blank = jnp.zeros((64, 64), BF16)
    for a in range(3):
        fwd = [dot_t(i64, r.w_mid_v[9 * a + 3 + c]).astype(BF16) for c in range(3)] + [blank]
        bwd = [r.w_mid_v[26 - (9 * a + 3 + c)] for c in range(3)] + [blank]
        r.wm[:, a * 256 : a * 256 + 256] = dot_t(i64, jnp.concatenate(fwd, axis=0)).astype(BF16)
        r.wmb[:, a * 256 : a * 256 + 256] = dot_t(i64, jnp.concatenate(bwd, axis=0)).astype(BF16)
    heads = dot(r.head_v[...], hot((iota((32, 256), 1) & 31) == iota((32, 256), 0)))
    hd = jnp.concatenate(
        [jnp.broadcast_to(heads[a : a + 1], (8, 256)) for a in range(3)]
        + [jnp.zeros((8, 256), F32)],
        axis=0,
    )
    same = (iota((32, 256), 0) & 7) == (iota((32, 256), 1) >> 5)
    hd = jnp.where(same, hd, 0.0).astype(BF16)
    hd_t = dot_t(eye(256), hd).astype(BF16)


    for copy in [loads[2]]:
        copy.wait()
    for copy in name_x + img_x:
        copy.wait_recv()

    def select(k, tiles, rows):
        first = ((xi * ny + lax.rem(yi + k, ny)) * 2).astype(F32)
        sums = [jnp.zeros((rows, 128), F32), jnp.zeros((rows, 128), F32)]
        for a in range(nx):
            called = r.meta[a].astype(F32)
            held = tiles[a].astype(F32)
            for s in range(SLOTS):
                tile = held[s * rows : s * rows + rows]
                for t in range(2):
                    sums[t] = sums[t] + jnp.where(called[s : s + 1] == first + t, tile, 0.0)
        return jnp.concatenate(sums, axis=0).astype(BF16)

    def img_y(k):
        peer = (g, xi * ny + lax.rem(yi + k, ny))
        return remote(r.pli.at[k], r.yri.at[k], r.s_iy.at[k], r.r_iy.at[k], peer)

    def tgt_y(k):
        peer = (g, xi * ny + lax.rem(yi + k, ny))
        return remote(r.plt.at[k], r.yrt.at[k], r.s_ty.at[k], r.r_ty.at[k], peer)

    def send_img(k, carry):
        r.pli[k] = select(k, r.xgi, 8)
        img_y(k).start()
        return carry

    def send_tgt(k, carry):
        r.plt[k] = select(k, r.xgt, 24)
        tgt_y(k).start()
        return carry

    lax.fori_loop(1, ny, send_img, 0)
    loads[3].wait()
    for copy in tgt_x:
        copy.wait_recv()
    lax.fori_loop(1, ny, send_tgt, 0)
    r.pli[0] = select(0, r.xgi, 8)
    r.plt[0] = select(0, r.xgt, 24)

    total = r.pli[0].astype(F32)
    for k in range(1, ny):
        img_y(k).wait_recv()
        total = total + r.yri[k].astype(F32)
    r.mi[...] = total.astype(BF16)
    img_n = [
        remote(r.mi, r.hri.at[2 - dz, 1 - dj], r.s_in.at[n], r.r_in.at[n], near[n])
        for n, (dz, dj) in enumerate(around)
    ]
    for copy in img_n:
        copy.start()
    r.hri[2, 1] = r.mi[...]
    total = r.plt[0].astype(F32)
    for k in range(1, ny):
        tgt_y(k).wait_recv()
        total = total + r.yrt[k].astype(F32)
    r.mt[...] = total.astype(BF16)
    tgt_n = [
        remote(r.mt, r.hrt.at[1 - dz, 1 - dj], r.s_tn.at[n], r.r_tn.at[n], near[n])
        for n, (dz, dj) in enumerate(around)
        if abs(dz) < 2
    ]
    for copy in tgt_n:
        copy.start()
    r.hrt[1, 1] = r.mt[...]
    for copy in img_n:
        copy.wait_recv()

    def wide_rows(ref, z, rows):
        left, own, right = (ref[z, n].astype(F32) for n in range(3))
        return jnp.concatenate([left[rows:], own[:rows], own[rows:], right[:rows]], axis=1)

    image = jnp.concatenate([wide_rows(r.hri, z, 8) for z in range(5)], axis=0)
    z2 = iota((40, 512), 0) + 8 * g - 16
    x1 = iota((40, 512), 1) + 256 * j - 128
    inside = (z2 >= 0) & (z2 < 4 * nz) & (x1 >= 0) & (x1 < 2 * nx_cells)
    image = jnp.where(inside, image, 0.0).astype(BF16)
    place = iota((512, wide), 0)
    lane2 = 2 * iota((512, wide), 1) + 128
    pick = [hot(place == ((lane2 + k) & 511)) for k in (-1, 0, 1, 2)]
    parts = jnp.concatenate([dot(image, p) for p in pick], axis=0).astype(BF16)
    row = iota((176, 160), 0)
    zrow = row >> 3
    source = ((row >> 1) & 3) * 40 + (zrow - 1) * 2 + (row & 1)
    order = hot((iota((176, 160), 1) == source) & (zrow >= 1) & (zrow <= 20))
    r.tcol[...] = dot(order, parts).astype(BF16)

    lane = iota((1, wide), 1)
    cell = jnp.where(lane < 192, lane, lane - 256) + 128 * j
    lane_in = jnp.where((cell >= 0) & (cell < nx_cells), 1.0, 0.0)

    def in_slab(zc):
        at = 2 * g + zc
        return lane_in * jnp.where((at >= 0) & (at < nz), 1.0, 0.0)

    def first_conv(n, carry):
        rows = r.tcol[pl.ds(pl.multiple_of(n * 16, 16), 32), :]
        h0 = jnp.maximum(dot(r.w0[...], rows), 0.0) * in_slab(n - 4)
        r.h0s[n] = h0.astype(BF16)
        put_fine(r.c0, 2 * n, h0)
        return carry

    lax.fori_loop(0, 10, first_conv, 0, unroll=True)

    def second_conv(n, carry):
        cols = r.c0[pl.ds(2 * n + 1, 4)].reshape(1024, wide)
        h1 = jnp.maximum(r.h0s[n + 1].astype(F32) + dot(r.w1[...], cols), 0.0).astype(BF16)
        r.h1s[n] = h1
        put_coarse(r.cd, n, jnp.maximum(dot(wd, h1), 0.0) * in_slab(n - 3))
        return carry

    lax.fori_loop(0, 8, second_conv, 0, unroll=True)


    for copy in tgt_n:
        copy.wait_recv()
    target = jnp.concatenate([wide_rows(r.hrt, z, 24) for z in range(3)], axis=0).astype(BF16)
    parts = jnp.concatenate([dot(target, p) for p in pick[1:3]], axis=0).astype(BF16)
    row = iota((192, 144), 0)
    source = (
        ((row >> 2) & 1) * 72
        + (row >> 6) * 24
        + ((row >> 3) & 3) * 8
        + (((row >> 5) & 1) * 2 + ((row >> 1) & 1)) * 2
        + (row & 1)
    )
    order = hot((iota((192, 144), 1) == source) & (((row >> 3) & 3) < 3))
    placed = dot(order, parts)
    for n in range(6):
        r.tgt[n] = placed[n * 32 : n * 32 + 32]


    def middle(n, carry):
        cols = r.cd[pl.ds(n, 3)].reshape(768, wide)
        q = jnp.maximum(r.cd[n + 1, 64:128].astype(F32) + dot(r.wm[...], cols), 0.0).astype(BF16)
        r.qs[n] = q
        s = jnp.maximum(r.h1s[n + 1].astype(F32) + dot(wu, q), 0.0).astype(BF16)
        r.ss[n] = s
        aff = jax.nn.sigmoid(dot(hd, s))
        err = aff - r.tgt[n]
        r.errs[n] = err.astype(BF16)
        gl = (err * aff * (1.0 - aff) / voxels).astype(BF16)
        r.gls[n] = gl
        gs = jnp.where(s.astype(F32) > 0, dot(hd_t, gl), 0.0).astype(BF16)
        r.gss[n] = gs
        gq = jnp.where(q.astype(F32) > 0, dot(wu_t, gs), 0.0) * in_slab(n - 2)
        put_coarse(r.cg, n, gq)
        return carry

    lax.fori_loop(0, 6, middle, 0, unroll=True)


    def own(ref, first):
        return jnp.concatenate([ref[first, :, 0:128], ref[first + 1, :, 0:128]], axis=1)


    rows = jnp.concatenate([r.errs[2, :, 0:128], r.errs[3, :, 0:128]], axis=0)
    src = iota((128, 256), 0)
    dst = iota((128, 256), 1)
    parts = jnp.concatenate([dot(rows, hot(dst == 2 * src + xo)) for xo in range(2)], axis=0)
    row = iota((32, 128), 0)
    source = ((row >> 2) & 1) * 32 + (row >> 3) * 8 + ((row >> 1) & 1) * 2 + (row & 1)
    q = iota((32, 128), 1)
    order = hot((q == source) | (q == source + 68))
    tiles = dot(order, parts.astype(BF16))
    r.err[...] = jnp.concatenate([tiles[0:24, 0:128], tiles[0:24, 128:256]], axis=0).astype(BF16)


    err_y = [remote(r.err, r.ey.at[k], r.s_ey.at[k], r.r_ey.at[k], y_peer[k]) for k in range(1, ny)]
    for copy in err_y:
        copy.start()
    r.ey[0] = r.err[...]

    def back(n, carry):
        cols = r.cg[pl.ds(n, 3)].reshape(768, wide)
        gdd = r.cg[n + 1, 64:128].astype(F32) + dot(r.wmb[...], cols)
        gdd = jnp.where(r.cd[n + 2, 64:128].astype(F32) > 0, gdd, 0.0).astype(BF16)
        r.gds[n] = gdd
        gr = r.gss[n + 1].astype(F32) + dot(wd_t, gdd)
        gr = jnp.where(r.h1s[n + 2].astype(F32) > 0, gr, 0.0) * in_slab(n - 1)
        r.grs[n] = gr.astype(BF16)
        put_fine(r.cr, 2 * n, gr)
        return carry

    lax.fori_loop(0, 4, back, 0, unroll=True)

    for n in range(2):
        cols = r.cr[2 * n + 1 : 2 * n + 5, :, 0:128].reshape(1024, 128)
        ga = r.grs[n + 1, :, 0:128].astype(F32) + dot(r.w1b[...], cols)
        r.gas[n] = jnp.where(r.h0s[n + 4, :, 0:128].astype(F32) > 0, ga, 0.0).astype(BF16)


    gr = own(r.grs, 1)
    for z_in in range(4):
        for y_in in range(2):
            lanes = slice(y_in * 128, y_in * 128 + 128)
            cols = jnp.concatenate([r.c0[7 + z_in, lanes, 0:128], r.c0[9 + z_in, lanes, 0:128]], axis=1)
            part = dot_t(gr, cols)
            for zo in range(2):
                for yo in range(2):
                    dz, dy = z_in - zo, y_in - yo + 1
                    if 0 <= dz < 3:
                        rows = zo * 64 + yo * 32
                        both = part[rows : rows + 32] + pltpu.roll(
                            part[128 + rows : 128 + rows + 32], 96, 1
                        )
                        at = RES + (dz * 3 + dy) * 32
                        if z_in == dz and y_in == max(dy - 1, 0):
                            r.vec[at : at + 32, :] = both
                        else:
                            r.vec[at : at + 32, :] += both
    gq = jnp.concatenate([r.cg[2, 64:128, 0:128], r.cg[3, 64:128, 0:128]], axis=1)
    for a in range(3):
        for half in range(2):
            lanes = slice(half * 128, half * 128 + 128)
            cols = jnp.concatenate([r.cd[2 + a, lanes, 0:128], r.cd[3 + a, lanes, 0:128]], axis=1)
            at = MID + (a * 2 + half) * 64
            r.vec[at : at + 64, :] = dot_t(gq, cols)
    gdd = own(r.gds, 1)
    none = jnp.zeros((64, 256), BF16)
    for at, fine, coarse in ((DOWN, own(r.h1s, 3), gdd), (UP, own(r.gss, 2), own(r.qs, 2))):
        r.vec[at : at + 128, :] = dot_t(
            fine[0:128], jnp.concatenate([coarse, none], axis=0)
        ) + dot_t(fine[128:256], jnp.concatenate([none, coarse], axis=0))
    cols = jnp.concatenate([r.tcol[64:96, 0:128], r.tcol[80:112, 0:128]], axis=1)
    inp = dot_t(cols, own(r.gas, 0))
    r.vec[INP : INP + 32, :] = inp[:, 0:128]
    r.vec[INP + 32 : INP + 64, :] = inp[:, 128:256]
    heads = jnp.where(same, dot_t(own(r.gls, 2), own(r.ss, 2)), 0.0)
    r.vec[HEAD:ROWS, :] = jnp.zeros((ROWS - HEAD, 128), F32)
    for a in range(3):
        line = jnp.sum(heads[a * 8 : a * 8 + 8], axis=0, keepdims=True)
        line = line[:, 0:128] + line[:, 128:256]
        line = line + pltpu.roll(line, 64, 1)
        line = line + pltpu.roll(line, 32, 1)
        r.vec[HEAD + a : HEAD + a + 1, :] = line


    half = ROWS // CORES
    rows_x = half // nx

    def piece(k, size):
        return pl.ds(pl.multiple_of(k * size, size), size)

    swap = remote(r.vec.at[piece(1 - core, half)], r.rc, r.s_c.at[0], r.r_c.at[0], other)
    swap.start()
    for copy in err_y:
        copy.wait_recv()

    def answer(a, carry):
        called = r.meta[a].astype(F32)
        sums = [jnp.zeros((24, 128), F32) for _ in range(SLOTS)]
        for k in range(ny):
            first = ((xi * ny + lax.rem(yi - k + ny, ny)) * 2).astype(F32)
            pair = r.ey[k].astype(F32)
            for t in range(2):
                for s in range(SLOTS):
                    sums[s] = sums[s] + jnp.where(
                        called[s : s + 1] == first + t, pair[t * 24 : t * 24 + 24], 0.0
                    )
        r.em[a] = jnp.concatenate(sums, axis=0).astype(BF16)
        return carry

    lax.fori_loop(0, nx, answer, 0)
    swap.wait_recv()
    r.ac[...] = r.vec[piece(core, half), :] + r.rc[...]
    over_x = [
        remote(r.ac.at[piece(x_at[k], rows_x)], r.rx.at[k], r.s_x.at[k], r.r_x.at[k], x_peer[k])
        for k in range(1, nx)
    ]
    err_x = [
        remote(r.em.at[nx - k], r.ex.at[k], r.s_ex.at[k], r.r_ex.at[k], x_peer[k])
        for k in range(1, nx)
    ]
    for copy in over_x:
        copy.start()
    for copy in over_x:
        copy.wait_recv()
    total = r.ac[piece(xi, rows_x), :]
    for k in range(1, nx):
        total = total + r.rx[k]

    def share(buf, at, peers, send, recv):
        return [
            remote(buf.at[at], buf.at[at], send.at[k], recv.at[k], peers[k])
            for k in range(1, len(peers))
        ]

    def gathered(buf, at, peers, send, recv):
        count = len(peers)
        for k in range(1, count):
            where = lax.rem(at - k + count, count)
            remote(buf.at[where], buf.at[where], send.at[k], recv.at[k], peers[k]).wait_recv()
        total = buf[0].astype(F32)
        for n in range(1, count):
            total = total + buf[n].astype(F32)
        return total

    part = rows_x // 2
    r.ya[yi] = total[0:part].astype(r.ya.dtype)
    y_first = share(r.ya, yi, y_peer, r.s_ya, r.r_ya)
    for copy in y_first:
        copy.start()
    r.za[zi] = total[part:].astype(r.za.dtype)
    z_first = share(r.za, zi, z_peer, r.s_za, r.r_za)
    for copy in z_first + err_x:
        copy.start()
    r.zb[zi] = gathered(r.ya, yi, y_peer, r.s_ya, r.r_ya).astype(r.zb.dtype)
    z_then = share(r.zb, zi, z_peer, r.s_zb, r.r_zb)
    for copy in z_then:
        copy.start()
    r.yb[yi] = gathered(r.za, zi, z_peer, r.s_za, r.r_za).astype(r.yb.dtype)
    y_then = share(r.yb, yi, y_peer, r.s_yb, r.r_yb)
    for copy in y_then:
        copy.start()
    r.gx[xi, 0:part] = gathered(r.zb, zi, z_peer, r.s_zb, r.r_zb)
    r.gx[xi, part:] = gathered(r.yb, yi, y_peer, r.s_yb, r.r_yb)
    back_x = [
        remote(r.gx.at[xi], r.gx.at[xi], r.s_gx.at[k], r.r_gx.at[k], x_peer[k])
        for k in range(1, nx)
    ]
    for copy in back_x:
        copy.start()
    for k in range(1, nx):
        at = lax.rem(xi - k + nx, nx)
        remote(r.gx.at[at], r.gx.at[at], r.s_gx.at[k], r.r_gx.at[k], x_peer[k]).wait_recv()
    back_c = remote(r.gx, r.gc, r.s_c.at[1], r.r_c.at[1], other)
    back_c.start()
    def store(buf, side, at):
        rows = lambda n: pl.ds(pl.multiple_of(side * half + n * rows_x, rows_x), rows_x)
        return [
            pltpu.make_async_copy(buf.at[n], r.out.at[rows(n)], r.stored.at[at, n])
            for n in range(nx)
        ]

    stores = store(r.gx, core, 0)
    for copy in stores:
        copy.start()
    for copy in err_x:
        copy.wait_recv()
    total = r.em[0].astype(F32)
    for k in range(1, nx):
        total = total + r.ex[k].astype(F32)
    r.tiles[...] = total.astype(BF16)
    back_c.wait_recv()
    last = store(r.gc, 1 - core, 1)
    for copy in last:
        copy.start()
    for copy in stores + last:
        copy.wait()
    sent = [swap, back_c] + name_x + img_x + tgt_x + img_n + tgt_n + err_y + err_x
    sent += [img_y(k) for k in range(1, ny)] + [tgt_y(k) for k in range(1, ny)]
    for copy in sent + over_x + y_first + z_first + z_then + y_then + back_x:
        copy.wait_send()


def whole(nx, ny, ng, operands):
    wide = 256
    nzc = ng // CORES
    half = ROWS // CORES
    rows_x = half // nx
    buffers = dict(
        list_v=((1, SLOTS), jnp.int32),
        count_v=((1, 1), jnp.int32),
        w_res_v=((9, 3, 32, 32), BF16),
        w_mid_v=((27, 64, 64), BF16),
        w_down_v=((8, 32, 64), BF16),
        w_up_v=((8, 32, 64), BF16),
        w_in_v=((27, 32), BF16),
        head_v=((3, 32), BF16),
        meta=((nx, 16, 128), BF16),
        xgi=((nx, 32, 128), BF16),
        xgt=((nx, 96, 128), BF16),
        pli=((ny, 16, 128), BF16),
        plt=((ny, 48, 128), BF16),
        yri=((ny, 16, 128), BF16),
        yrt=((ny, 48, 128), BF16),
        mi=((16, 128), BF16),
        mt=((48, 128), BF16),
        hri=((5, 3, 16, 128), BF16),
        hrt=((3, 3, 48, 128), BF16),
        w0=((256, 32), BF16),
        w1=((256, 1024), BF16),
        w1b=((256, 1024), BF16),
        wm=((64, 768), BF16),
        wmb=((64, 768), BF16),
        tcol=((176, wide), BF16),
        tgt=((6, 32, wide), F32),
        h0s=((10, 256, wide), BF16),
        c0=((20, 256, wide), BF16),
        h1s=((8, 256, wide), BF16),
        cd=((8, 256, wide), BF16),
        qs=((6, 64, wide), BF16),
        ss=((6, 256, wide), BF16),
        gls=((6, 32, wide), BF16),
        gss=((6, 256, wide), BF16),
        cg=((6, 256, wide), BF16),
        gds=((4, 64, wide), BF16),
        cr=((8, 256, wide), BF16),
        grs=((4, 256, wide), BF16),
        gas=((2, 256, 128), BF16),
        errs=((6, 32, wide), BF16),
        vec=((ROWS, 128), F32),
        err=((48, 128), BF16),
        rc=((half, 128), F32),
        ac=((half, 128), F32),
        rx=((nx, rows_x, 128), F32),
        ya=((ny, rows_x // 2, 128), BF16),
        za=((nzc, rows_x // 2, 128), BF16),
        yb=((ny, rows_x // 2, 128), BF16),
        zb=((nzc, rows_x // 2, 128), BF16),
        gx=((nx, rows_x, 128), F32),
        gc=((nx, rows_x, 128), F32),
        ey=((ny, 48, 128), BF16),
        em=((nx, 96, 128), BF16),
        ex=((nx, 96, 128), BF16),
    )
    sems = dict(loaded=10)
    for kind, count in (
        ("name", nx),
        ("ix", nx),
        ("tx", nx),
        ("iy", ny),
        ("ty", ny),
        ("in", 14),
        ("tn", 14),
        ("ey", ny),
        ("ex", nx),
        ("c", 2),
        ("x", nx),
        ("ya", ny),
        ("za", nzc),
        ("yb", ny),
        ("zb", nzc),
        ("gx", nx),
    ):
        sems["s_" + kind] = count
        sems["r_" + kind] = count
    names = list(operands) + ["out", "tiles"] + list(buffers) + list(sems) + ["stored"]
    return pl.pallas_call(
        functools.partial(whole_kernel, nx, ny, ng, names),
        out_shape=(
            jax.ShapeDtypeStruct((ROWS, 128), F32),
            jax.ShapeDtypeStruct((96, 128), BF16),
        ),
        in_specs=[pl.BlockSpec(memory_space=pltpu.MemorySpace.HBM)] * len(operands),
        out_specs=(pl.BlockSpec(memory_space=pltpu.MemorySpace.HBM), VM),
        scratch_shapes=[pltpu.VMEM(shape, dtype) for shape, dtype in buffers.values()]
        + [pltpu.SemaphoreType.DMA((count,)) for count in sems.values()]
        + [pltpu.SemaphoreType.DMA((2, nx))],
        compiler_params=pltpu.CompilerParams(
            collective_id=0, has_side_effects=True, vmem_limit_bytes=56 << 20
        ),
        name="whole",
    )(*operands.values())


def unpack_kernel(
    sums, tiles, err, g_in, g_res, g_down, g_mid, g_up, g_head, lines, vec, sems
):
    ends = (RES, MID, DOWN, INP, USED)
    loads = [
        pltpu.make_async_copy(sums.at[a:b], vec.at[a:b], sems.at[n])
        for n, (a, b) in enumerate(zip(ends[:-1], ends[1:]))
    ]
    load_err = pltpu.make_async_copy(tiles, err, sems.at[4])
    for copy in loads + [load_err]:
        copy.start()
    for t in range(27):
        if t // 3 % 3 != 1:
            g_mid[t] = jnp.zeros((64, 64), F32)
    loads[0].wait()
    for zy in range(9):
        strip = vec[RES + zy * 32 : RES + zy * 32 + 32, :]
        for c in range(3):
            part = strip if c == 0 else pltpu.roll(strip, 128 - 32 * c, 1)
            g_res[zy * 3 + c] = part[:, 0:32]
    loads[1].wait()
    for t in range(27):
        a, b, c = t // 9, t // 3 % 3, t % 3
        if b == 1:
            at = MID + (a * 2 + c // 2) * 64
            part = vec[at : at + 64, :]
            if c % 2:
                part = pltpu.roll(part, 64, 1)
            g_mid[t] = part[:, 0:64]
    loads[2].wait()
    loads[3].wait()
    for pos in range(8):
        quarter = pos & 3
        for at, grad in ((DOWN, g_down), (UP, g_up)):
            part = vec[at + quarter * 32 : at + quarter * 32 + 32, :]
            if pos >> 2:
                part = pltpu.roll(part, 64, 1)
            grad[tap_of(pos)] = part[:, 0:64]
        part = vec[INP + (pos >> 2) * 32 : INP + (pos >> 2) * 32 + 32, :]
        if quarter:
            part = pltpu.roll(part, 128 - 32 * quarter, 1)
        lines[pos] = part
    for t in range(27):
        dz, dy, dx = t // 9, t // 3 % 3, t % 3
        total = None
        for pos in range(8):
            xo, zo, yo = pos >> 2, pos >> 1 & 1, pos & 1
            if 0 <= yo + dy - 1 < 2:
                at = (zo + dz) * 8 + (xo + dx) * 2 + yo + dy - 1
                line = lines[pos, at : at + 1, :]
                total = line if total is None else total + line
        g_in[t : t + 1, :] = total[:, 0:32]
    g_head[...] = vec[HEAD : HEAD + 8, :][0:3, 0:32]
    load_err.wait()


def unpack(vec, tiles):
    return pl.pallas_call(
        unpack_kernel,
        out_shape=(
            jax.ShapeDtypeStruct((96, 128), BF16),
            jax.ShapeDtypeStruct((27, 32), F32),
            jax.ShapeDtypeStruct((27, 32, 32), F32),
            jax.ShapeDtypeStruct((8, 32, 64), F32),
            jax.ShapeDtypeStruct((27, 64, 64), F32),
            jax.ShapeDtypeStruct((8, 32, 64), F32),
            jax.ShapeDtypeStruct((3, 32), F32),
        ),
        in_specs=[pl.BlockSpec(memory_space=pltpu.MemorySpace.HBM)] * 2,
        out_specs=(VM,) * 7,
        scratch_shapes=[
            pltpu.VMEM((8, 32, 128), F32),
            pltpu.VMEM((ROWS, 128), F32),
            pltpu.SemaphoreType.DMA((5,)),
        ],
        compiler_params=pltpu.CompilerParams(vmem_limit_bytes=56 << 20),
        name="unpack",
    )(vec, tiles)


def local(
    tile_image, tile_target, owner_counts, tile_list, w_in, w_res, w_down, w_mid, w_up, head_weight
):
    ranks = lax.axis_size("xy")
    ng = lax.axis_size("gz")
    nx, ny = grid_of(ranks)
    operands = dict(
        img=tile_image.reshape(SLOTS * 8, 128),
        target=tile_target.reshape(SLOTS * 24, 128),
        counts=owner_counts,
        tile_list=tile_list.reshape(1, SLOTS),
        w_in=w_in,
        w_res=w_res.reshape(9, 3, 32, 32),
        w_down=jnp.transpose(w_down, (0, 2, 1)),
        w_mid=w_mid,
        w_up=w_up,
        head=head_weight,
    )
    sums, tiles = whole(nx, ny, ng, operands)
    tiles, g_in, g_res, g_down, g_mid, g_up, g_head = unpack(sums, tiles)
    tiles = tiles.reshape(1, 1, SLOTS, 3, 4, 2, 128)
    return (tiles, g_in, g_res, jnp.transpose(g_down, (0, 2, 1)), g_mid, g_up, g_head)


def solution(mesh):
    return jax.shard_map(
        local,
        mesh=mesh,
        in_specs=(
            P("gz", "xy", None, None, None, None),
            P("gz", "xy", None, None, None, None, None),
            P("gz", "xy"),
            P("gz", "xy", None),
            P(),
            P(),
            P(),
            P(),
            P(),
            P(),
        ),
        out_specs=(P("gz", "xy", None, None, None, None, None), P(), P(), P(), P(), P(), P()),
        check_vma=False,
    )
```

```python
import functools
import types

import jax
import jax.numpy as jnp
from jax import lax
from jax.experimental import pallas as pl
from jax.experimental.pallas import tpu as pltpu
from jax.sharding import PartitionSpec as P

F32 = jnp.float32
BF16 = jnp.bfloat16
MESH = pl.DeviceIdType.MESH
SLOTS = 4
CORES = 2
ROWS = 1024
VM = pl.BlockSpec(memory_space=pltpu.VMEM)

RES, MID, DOWN, UP, INP, HEAD, USED = 0, 288, 672, 800, 928, 992, 1000


def grid_of(ranks):
    height = 8 if ranks == 32 else 2
    return ranks // height, height


def remote(src, dst, send, recv, where):
    return pltpu.make_async_remote_copy(
        src_ref=src, dst_ref=dst, send_sem=send, recv_sem=recv, device_id=where, device_id_type=MESH
    )


def iota(shape, dim):
    return lax.broadcasted_iota(jnp.int32, shape, dim)


def dot(a, b):
    return jnp.dot(a, b, preferred_element_type=F32)


def dot_t(a, b):
    return lax.dot_general(a, b, (((1,), (1,)), ((), ())), preferred_element_type=F32)


def hot(cond):
    return jnp.where(cond, 1.0, 0.0).astype(BF16)


def eye(n):
    return hot(iota((n, n), 0) == iota((n, n), 1))


def before(v):
    return pltpu.roll(v, 1, 1)


def after(v):
    return pltpu.roll(v, v.shape[1] - 1, 1)


def put_fine(buf, at, v):
    prev = before(v[128:256]).astype(BF16)
    succ = after(v[0:128]).astype(BF16)
    even = v[0:128].astype(BF16)
    odd = v[128:256].astype(BF16)
    for zo in range(2):
        for yo in range(2):
            rows = slice(zo * 64 + yo * 32, zo * 64 + yo * 32 + 32)
            for n, part in enumerate((prev, even, odd, succ)):
                buf[at + zo, yo * 128 + n * 32 : yo * 128 + n * 32 + 32, :] = part[rows]


def put_coarse(buf, at, v):
    buf[at, 0:64, :] = before(v).astype(BF16)
    buf[at, 64:128, :] = v.astype(BF16)
    buf[at, 128:192, :] = after(v).astype(BF16)
    buf[at, 192:256, :] = jnp.zeros((64, v.shape[1]), BF16)


def tap_of(pos):
    return (pos >> 1 & 1) * 4 + (pos & 1) * 2 + (pos >> 2)


def whole_kernel(nx, ny, ng, names, *refs):
    r = types.SimpleNamespace(**dict(zip(names, refs)))
    ranks = nx * ny
    nzc = ng // CORES
    nz = 2 * ng
    nx_cells = 128 * ranks
    voxels = float(ng * ranks * 2048)
    wide = 256
    g = lax.axis_index("gz")
    j = lax.axis_index("xy")
    xi = j // ny
    yi = lax.rem(j, ny)
    zi = g // CORES
    core = lax.rem(g, CORES)
    other = (zi * CORES + 1 - core, j)
    x_at = [lax.rem(xi + k, nx) for k in range(nx)]
    y_at = [lax.rem(yi + k, ny) for k in range(ny)]
    x_peer = [(g, x_at[k] * ny + yi) for k in range(nx)]
    y_peer = [(g, xi * ny + y_at[k]) for k in range(ny)]
    z_peer = [(lax.rem(zi + k, nzc) * CORES + core, j) for k in range(nzc)]
    around = [(dz, dj) for dz in (0, -1, 1, -2, 2) for dj in (0, -1, 1) if (dz, dj) != (0, 0)]
    near = [(lax.rem(g + dz + ng, ng), lax.rem(j + dj + ranks, ranks)) for dz, dj in around]

    moves = (
        (r.tile_list, r.list_v),
        (r.counts, r.count_v),
        (r.img, r.xgi.at[0]),
        (r.target, r.xgt.at[0]),
        (r.w_res, r.w_res_v),
        (r.w_mid, r.w_mid_v),
        (r.w_down, r.w_down_v),
        (r.w_up, r.w_up_v),
        (r.w_in, r.w_in_v),
        (r.head, r.head_v),
    )
    loads = [pltpu.make_async_copy(src, dst, r.loaded.at[n]) for n, (src, dst) in enumerate(moves)]
    for copy in loads:
        copy.start()
    barrier = pltpu.get_barrier_semaphore()
    peers = [other] + x_peer[1:] + y_peer[1:] + z_peer[1:] + near
    for peer in peers:
        pl.semaphore_signal(barrier, inc=1, device_id=peer, device_id_type=MESH)
    for copy in loads[0:2]:
        copy.wait()
    live = lax.broadcasted_iota(jnp.int32, (1, SLOTS), 1) < r.count_v[...]
    held = jnp.where(live, r.list_v[...], -1).astype(F32)
    lines = [jnp.broadcast_to(held[:, s : s + 1], (1, 128)) for s in range(SLOTS)]
    lines.append(jnp.zeros((12, 128), F32))
    r.meta[0] = jnp.concatenate(lines, axis=0).astype(BF16)
    pl.semaphore_wait(barrier, len(peers))

    name_x = [
        remote(r.meta.at[0], r.meta.at[k], r.s_name.at[k], r.r_name.at[k], x_peer[k])
        for k in range(1, nx)
    ]
    img_x = [
        remote(r.img, r.xgi.at[k], r.s_ix.at[k], r.r_ix.at[k], x_peer[k]) for k in range(1, nx)
    ]
    tgt_x = [
        remote(r.target, r.xgt.at[k], r.s_tx.at[k], r.r_tx.at[k], x_peer[k]) for k in range(1, nx)
    ]
    for copy in name_x + img_x + tgt_x:
        copy.start()
    for copy in loads[4:]:
        copy.wait()

    i32, i64 = eye(32), eye(64)
    for xo in range(2):
        fwd = jnp.zeros((288, 128), F32)
        for c in range(3):
            put = hot(iota((32, 128), 1) == iota((32, 128), 0) + 32 * (c + xo))
            fwd = fwd + dot(r.w_res_v[:, c].reshape(288, 32), put)
        fwd = fwd.astype(BF16)
        blank = jnp.zeros((32, 32), BF16)
        for zy in range(9):
            parts = [r.w_res_v[8 - zy, 2 - c] for c in range(3)]
            parts = [blank] + parts if xo else parts + [blank]
            bwd = dot_t(i32, jnp.concatenate(parts, axis=0)).astype(BF16)
            dz, dy = zy // 3, zy % 3
            for zo in range(2):
                for yo in range(2):
                    y_in = yo + dy - 1
                    if 0 <= y_in < 2:
                        rows = slice(xo * 128 + zo * 64 + yo * 32, xo * 128 + zo * 64 + yo * 32 + 32)
                        lanes = slice((zo + dz) * 256 + y_in * 128, (zo + dz) * 256 + y_in * 128 + 128)
                        r.w1[rows, lanes] = fwd[zy * 32 : zy * 32 + 32]
                        r.w1b[rows, lanes] = bwd
        for zo in range(2):
            for yo in range(2):
                rows = slice(xo * 128 + zo * 64 + yo * 32, xo * 128 + zo * 64 + yo * 32 + 32)
                lanes = slice((3 - 3 * zo) * 256, (3 - 3 * zo) * 256 + 256)
                r.w1[rows, lanes] = jnp.zeros((32, 256), BF16)
                r.w1b[rows, lanes] = jnp.zeros((32, 256), BF16)
    taps_t = dot_t(i32, r.w_in_v[...]).astype(BF16)
    col = iota((27, 32), 1)
    tap = iota((27, 32), 0)
    for pos in range(8):
        xo, zo, yo = pos >> 2, pos >> 1 & 1, pos & 1
        hit = jnp.zeros((27, 32), jnp.bool_)
        for t in range(27):
            dz, dy, dx = t // 9, t // 3 % 3, t % 3
            if 0 <= yo + dy - 1 < 2:
                at = (zo + dz) * 8 + (xo + dx) * 2 + yo + dy - 1
                hit = hit | ((tap == t) & (col == at))
        r.w0[pos * 32 : pos * 32 + 32, :] = dot(taps_t, hot(hit)).astype(BF16)
    wd_t = jnp.concatenate([r.w_down_v[tap_of(p)] for p in range(8)], axis=0)
    wd = dot_t(i64, wd_t).astype(BF16)
    wu = jnp.concatenate([r.w_up_v[tap_of(p)] for p in range(8)], axis=0)
    wu_t = dot_t(i64, wu).astype(BF16)
    blank = jnp.zeros((64, 64), BF16)
    for a in range(3):
        fwd = [dot_t(i64, r.w_mid_v[9 * a + 3 + c]).astype(BF16) for c in range(3)] + [blank]
        bwd = [r.w_mid_v[26 - (9 * a + 3 + c)] for c in range(3)] + [blank]
        r.wm[:, a * 256 : a * 256 + 256] = dot_t(i64, jnp.concatenate(fwd, axis=0)).astype(BF16)
        r.wmb[:, a * 256 : a * 256 + 256] = dot_t(i64, jnp.concatenate(bwd, axis=0)).astype(BF16)
    heads = dot(r.head_v[...], hot((iota((32, 256), 1) & 31) == iota((32, 256), 0)))
    hd = jnp.concatenate(
        [jnp.broadcast_to(heads[a : a + 1], (8, 256)) for a in range(3)]
        + [jnp.zeros((8, 256), F32)],
        axis=0,
    )
    same = (iota((32, 256), 0) & 7) == (iota((32, 256), 1) >> 5)
    hd = jnp.where(same, hd, 0.0).astype(BF16)
    hd_t = dot_t(eye(256), hd).astype(BF16)


    for copy in [loads[2]]:
        copy.wait()
    for copy in name_x + img_x:
        copy.wait_recv()

    def select(k, tiles, rows):
        first = ((xi * ny + lax.rem(yi + k, ny)) * 2).astype(F32)
        sums = [jnp.zeros((rows, 128), F32), jnp.zeros((rows, 128), F32)]
        for a in range(nx):
            called = r.meta[a].astype(F32)
            held = tiles[a].astype(F32)
            for s in range(SLOTS):
                tile = held[s * rows : s * rows + rows]
                for t in range(2):
                    sums[t] = sums[t] + jnp.where(called[s : s + 1] == first + t, tile, 0.0)
        return jnp.concatenate(sums, axis=0).astype(BF16)

    def img_y(k):
        peer = (g, xi * ny + lax.rem(yi + k, ny))
        return remote(r.pli.at[k], r.yri.at[k], r.s_iy.at[k], r.r_iy.at[k], peer)

    def tgt_y(k):
        peer = (g, xi * ny + lax.rem(yi + k, ny))
        return remote(r.plt.at[k], r.yrt.at[k], r.s_ty.at[k], r.r_ty.at[k], peer)

    def send_img(k, carry):
        r.pli[k] = select(k, r.xgi, 8)
        img_y(k).start()
        return carry

    def send_tgt(k, carry):
        r.plt[k] = select(k, r.xgt, 24)
        tgt_y(k).start()
        return carry

    lax.fori_loop(1, ny, send_img, 0)
    loads[3].wait()
    for copy in tgt_x:
        copy.wait_recv()
    lax.fori_loop(1, ny, send_tgt, 0)
    r.pli[0] = select(0, r.xgi, 8)
    r.plt[0] = select(0, r.xgt, 24)

    total = r.pli[0].astype(F32)
    for k in range(1, ny):
        img_y(k).wait_recv()
        total = total + r.yri[k].astype(F32)
    r.mi[...] = total.astype(BF16)
    img_n = [
        remote(r.mi, r.hri.at[2 - dz, 1 - dj], r.s_in.at[n], r.r_in.at[n], near[n])
        for n, (dz, dj) in enumerate(around)
    ]
    for copy in img_n:
        copy.start()
    r.hri[2, 1] = r.mi[...]
    total = r.plt[0].astype(F32)
    for k in range(1, ny):
        tgt_y(k).wait_recv()
        total = total + r.yrt[k].astype(F32)
    r.mt[...] = total.astype(BF16)
    tgt_n = [
        remote(r.mt, r.hrt.at[1 - dz, 1 - dj], r.s_tn.at[n], r.r_tn.at[n], near[n])
        for n, (dz, dj) in enumerate(around)
        if abs(dz) < 2
    ]
    for copy in tgt_n:
        copy.start()
    r.hrt[1, 1] = r.mt[...]
    for copy in img_n:
        copy.wait_recv()

    def wide_rows(ref, z, rows):
        left, own, right = (ref[z, n].astype(F32) for n in range(3))
        return jnp.concatenate([left[rows:], own[:rows], own[rows:], right[:rows]], axis=1)

    image = jnp.concatenate([wide_rows(r.hri, z, 8) for z in range(5)], axis=0)
    z2 = iota((40, 512), 0) + 8 * g - 16
    x1 = iota((40, 512), 1) + 256 * j - 128
    inside = (z2 >= 0) & (z2 < 4 * nz) & (x1 >= 0) & (x1 < 2 * nx_cells)
    image = jnp.where(inside, image, 0.0).astype(BF16)
    place = iota((512, wide), 0)
    lane2 = 2 * iota((512, wide), 1) + 128
    pick = [hot(place == ((lane2 + k) & 511)) for k in (-1, 0, 1, 2)]
    parts = jnp.concatenate([dot(image, p) for p in pick], axis=0).astype(BF16)
    row = iota((176, 160), 0)
    zrow = row >> 3
    source = ((row >> 1) & 3) * 40 + (zrow - 1) * 2 + (row & 1)
    order = hot((iota((176, 160), 1) == source) & (zrow >= 1) & (zrow <= 20))
    r.tcol[...] = dot(order, parts).astype(BF16)

    lane = iota((1, wide), 1)
    cell = jnp.where(lane < 192, lane, lane - 256) + 128 * j
    lane_in = jnp.where((cell >= 0) & (cell < nx_cells), 1.0, 0.0)

    def in_slab(zc):
        at = 2 * g + zc
        return lane_in * jnp.where((at >= 0) & (at < nz), 1.0, 0.0)

    def first_conv(n, carry):
        rows = r.tcol[pl.ds(pl.multiple_of(n * 16, 16), 32), :]
        h0 = jnp.maximum(dot(r.w0[...], rows), 0.0) * in_slab(n - 4)
        r.h0s[n] = h0.astype(BF16)
        put_fine(r.c0, 2 * n, h0)
        return carry

    lax.fori_loop(0, 10, first_conv, 0, unroll=True)

    def second_conv(n, carry):
        cols = r.c0[pl.ds(2 * n + 1, 4)].reshape(1024, wide)
        h1 = jnp.maximum(r.h0s[n + 1].astype(F32) + dot(r.w1[...], cols), 0.0).astype(BF16)
        r.h1s[n] = h1
        put_coarse(r.cd, n, jnp.maximum(dot(wd, h1), 0.0) * in_slab(n - 3))
        return carry

    lax.fori_loop(0, 8, second_conv, 0, unroll=True)


    for copy in tgt_n:
        copy.wait_recv()
    target = jnp.concatenate([wide_rows(r.hrt, z, 24) for z in range(3)], axis=0).astype(BF16)
    parts = jnp.concatenate([dot(target, p) for p in pick[1:3]], axis=0).astype(BF16)
    row = iota((192, 144), 0)
    source = (
        ((row >> 2) & 1) * 72
        + (row >> 6) * 24
        + ((row >> 3) & 3) * 8
        + (((row >> 5) & 1) * 2 + ((row >> 1) & 1)) * 2
        + (row & 1)
    )
    order = hot((iota((192, 144), 1) == source) & (((row >> 3) & 3) < 3))
    placed = dot(order, parts)
    for n in range(6):
        r.tgt[n] = placed[n * 32 : n * 32 + 32]


    def middle(n, carry):
        cols = r.cd[pl.ds(n, 3)].reshape(768, wide)
        q = jnp.maximum(r.cd[n + 1, 64:128].astype(F32) + dot(r.wm[...], cols), 0.0).astype(BF16)
        r.qs[n] = q
        s = jnp.maximum(r.h1s[n + 1].astype(F32) + dot(wu, q), 0.0).astype(BF16)
        r.ss[n] = s
        aff = jax.nn.sigmoid(dot(hd, s))
        err = aff - r.tgt[n]
        r.errs[n] = err.astype(BF16)
        gl = (err * aff * (1.0 - aff) / voxels).astype(BF16)
        r.gls[n] = gl
        gs = jnp.where(s.astype(F32) > 0, dot(hd_t, gl), 0.0).astype(BF16)
        r.gss[n] = gs
        gq = jnp.where(q.astype(F32) > 0, dot(wu_t, gs), 0.0) * in_slab(n - 2)
        put_coarse(r.cg, n, gq)
        return carry

    lax.fori_loop(0, 6, middle, 0, unroll=True)


    def own(ref, first):
        return jnp.concatenate([ref[first, :, 0:128], ref[first + 1, :, 0:128]], axis=1)


    rows = jnp.concatenate([r.errs[2, :, 0:128], r.errs[3, :, 0:128]], axis=0)
    src = iota((128, 256), 0)
    dst = iota((128, 256), 1)
    parts = jnp.concatenate([dot(rows, hot(dst == 2 * src + xo)) for xo in range(2)], axis=0)
    row = iota((32, 128), 0)
    source = ((row >> 2) & 1) * 32 + (row >> 3) * 8 + ((row >> 1) & 1) * 2 + (row & 1)
    q = iota((32, 128), 1)
    order = hot((q == source) | (q == source + 68))
    tiles = dot(order, parts.astype(BF16))
    r.err[...] = jnp.concatenate([tiles[0:24, 0:128], tiles[0:24, 128:256]], axis=0).astype(BF16)


    err_y = [remote(r.err, r.ey.at[k], r.s_ey.at[k], r.r_ey.at[k], y_peer[k]) for k in range(1, ny)]
    for copy in err_y:
        copy.start()
    r.ey[0] = r.err[...]

    def back(n, carry):
        cols = r.cg[pl.ds(n, 3)].reshape(768, wide)
        gdd = r.cg[n + 1, 64:128].astype(F32) + dot(r.wmb[...], cols)
        gdd = jnp.where(r.cd[n + 2, 64:128].astype(F32) > 0, gdd, 0.0).astype(BF16)
        r.gds[n] = gdd
        gr = r.gss[n + 1].astype(F32) + dot(wd_t, gdd)
        gr = jnp.where(r.h1s[n + 2].astype(F32) > 0, gr, 0.0) * in_slab(n - 1)
        r.grs[n] = gr.astype(BF16)
        put_fine(r.cr, 2 * n, gr)
        return carry

    lax.fori_loop(0, 4, back, 0, unroll=True)

    for n in range(2):
        cols = r.cr[2 * n + 1 : 2 * n + 5, :, 0:128].reshape(1024, 128)
        ga = r.grs[n + 1, :, 0:128].astype(F32) + dot(r.w1b[...], cols)
        r.gas[n] = jnp.where(r.h0s[n + 4, :, 0:128].astype(F32) > 0, ga, 0.0).astype(BF16)


    gr = own(r.grs, 1)
    for z_in in range(4):
        for y_in in range(2):
            lanes = slice(y_in * 128, y_in * 128 + 128)
            cols = jnp.concatenate([r.c0[7 + z_in, lanes, 0:128], r.c0[9 + z_in, lanes, 0:128]], axis=1)
            part = dot_t(gr, cols)
            for zo in range(2):
                for yo in range(2):
                    dz, dy = z_in - zo, y_in - yo + 1
                    if 0 <= dz < 3:
                        rows = zo * 64 + yo * 32
                        both = part[rows : rows + 32] + pltpu.roll(
                            part[128 + rows : 128 + rows + 32], 96, 1
                        )
                        at = RES + (dz * 3 + dy) * 32
                        if z_in == dz and y_in == max(dy - 1, 0):
                            r.vec[at : at + 32, :] = both
                        else:
                            r.vec[at : at + 32, :] += both
    gq = jnp.concatenate([r.cg[2, 64:128, 0:128], r.cg[3, 64:128, 0:128]], axis=1)
    for a in range(3):
        for half in range(2):
            lanes = slice(half * 128, half * 128 + 128)
            cols = jnp.concatenate([r.cd[2 + a, lanes, 0:128], r.cd[3 + a, lanes, 0:128]], axis=1)
            at = MID + (a * 2 + half) * 64
            r.vec[at : at + 64, :] = dot_t(gq, cols)
    gdd = own(r.gds, 1)
    none = jnp.zeros((64, 256), BF16)
    for at, fine, coarse in ((DOWN, own(r.h1s, 3), gdd), (UP, own(r.gss, 2), own(r.qs, 2))):
        r.vec[at : at + 128, :] = dot_t(
            fine[0:128], jnp.concatenate([coarse, none], axis=0)
        ) + dot_t(fine[128:256], jnp.concatenate([none, coarse], axis=0))
    cols = jnp.concatenate([r.tcol[64:96, 0:128], r.tcol[80:112, 0:128]], axis=1)
    inp = dot_t(cols, own(r.gas, 0))
    r.vec[INP : INP + 32, :] = inp[:, 0:128]
    r.vec[INP + 32 : INP + 64, :] = inp[:, 128:256]
    heads = jnp.where(same, dot_t(own(r.gls, 2), own(r.ss, 2)), 0.0)
    r.vec[HEAD:ROWS, :] = jnp.zeros((ROWS - HEAD, 128), F32)
    for a in range(3):
        line = jnp.sum(heads[a * 8 : a * 8 + 8], axis=0, keepdims=True)
        line = line[:, 0:128] + line[:, 128:256]
        line = line + pltpu.roll(line, 64, 1)
        line = line + pltpu.roll(line, 32, 1)
        r.vec[HEAD + a : HEAD + a + 1, :] = line


    half = ROWS // CORES
    rows_x = half // nx

    def piece(k, size):
        return pl.ds(pl.multiple_of(k * size, size), size)

    swap = remote(r.vec.at[piece(1 - core, half)], r.rc, r.s_c.at[0], r.r_c.at[0], other)
    swap.start()
    for copy in err_y:
        copy.wait_recv()

    def answer(a, carry):
        called = r.meta[a].astype(F32)
        sums = [jnp.zeros((24, 128), F32) for _ in range(SLOTS)]
        for k in range(ny):
            first = ((xi * ny + lax.rem(yi - k + ny, ny)) * 2).astype(F32)
            pair = r.ey[k].astype(F32)
            for t in range(2):
                for s in range(SLOTS):
                    sums[s] = sums[s] + jnp.where(
                        called[s : s + 1] == first + t, pair[t * 24 : t * 24 + 24], 0.0
                    )
        r.em[a] = jnp.concatenate(sums, axis=0).astype(BF16)
        return carry

    lax.fori_loop(0, nx, answer, 0)
    swap.wait_recv()
    r.ac[...] = r.vec[piece(core, half), :] + r.rc[...]
    r.ab[...] = r.ac[...].astype(BF16)
    over_x = [
        remote(r.ab.at[piece(x_at[k], rows_x)], r.rx.at[k], r.s_x.at[k], r.r_x.at[k], x_peer[k])
        for k in range(1, nx)
    ]
    err_x = [
        remote(r.em.at[nx - k], r.ex.at[k], r.s_ex.at[k], r.r_ex.at[k], x_peer[k])
        for k in range(1, nx)
    ]
    for copy in over_x:
        copy.start()
    for copy in over_x:
        copy.wait_recv()
    total = r.ac[piece(xi, rows_x), :]
    for k in range(1, nx):
        total = total + r.rx[k].astype(F32)

    def share(buf, at, peers, send, recv):
        return [
            remote(buf.at[at], buf.at[at], send.at[k], recv.at[k], peers[k])
            for k in range(1, len(peers))
        ]

    def gathered(buf, at, peers, send, recv):
        count = len(peers)
        for k in range(1, count):
            where = lax.rem(at - k + count, count)
            remote(buf.at[where], buf.at[where], send.at[k], recv.at[k], peers[k]).wait_recv()
        total = buf[0].astype(F32)
        for n in range(1, count):
            total = total + buf[n].astype(F32)
        return total

    part = rows_x // 2
    r.ya[yi] = total[0:part].astype(r.ya.dtype)
    y_first = share(r.ya, yi, y_peer, r.s_ya, r.r_ya)
    for copy in y_first:
        copy.start()
    r.za[zi] = total[part:].astype(r.za.dtype)
    z_first = share(r.za, zi, z_peer, r.s_za, r.r_za)
    for copy in z_first + err_x:
        copy.start()
    r.zb[zi] = gathered(r.ya, yi, y_peer, r.s_ya, r.r_ya).astype(r.zb.dtype)
    z_then = share(r.zb, zi, z_peer, r.s_zb, r.r_zb)
    for copy in z_then:
        copy.start()
    r.yb[yi] = gathered(r.za, zi, z_peer, r.s_za, r.r_za).astype(r.yb.dtype)
    y_then = share(r.yb, yi, y_peer, r.s_yb, r.r_yb)
    for copy in y_then:
        copy.start()
    r.gx[xi, 0:part] = gathered(r.zb, zi, z_peer, r.s_zb, r.r_zb).astype(BF16)
    r.gx[xi, part:] = gathered(r.yb, yi, y_peer, r.s_yb, r.r_yb).astype(BF16)
    back_x = [
        remote(r.gx.at[xi], r.gx.at[xi], r.s_gx.at[k], r.r_gx.at[k], x_peer[k])
        for k in range(1, nx)
    ]
    for copy in back_x:
        copy.start()
    for k in range(1, nx):
        at = lax.rem(xi - k + nx, nx)
        remote(r.gx.at[at], r.gx.at[at], r.s_gx.at[k], r.r_gx.at[k], x_peer[k]).wait_recv()
    back_c = remote(r.gx, r.gc, r.s_c.at[1], r.r_c.at[1], other)
    back_c.start()
    def store(buf, side, at):
        rows = lambda n: pl.ds(pl.multiple_of(side * half + n * rows_x, rows_x), rows_x)
        return [
            pltpu.make_async_copy(buf.at[n], r.out.at[rows(n)], r.stored.at[at, n])
            for n in range(nx)
        ]

    stores = store(r.gx, core, 0)
    for copy in stores:
        copy.start()
    for copy in err_x:
        copy.wait_recv()
    total = r.em[0].astype(F32)
    for k in range(1, nx):
        total = total + r.ex[k].astype(F32)
    r.tiles[...] = total.astype(BF16)
    back_c.wait_recv()
    last = store(r.gc, 1 - core, 1)
    for copy in last:
        copy.start()
    for copy in stores + last:
        copy.wait()
    sent = [swap, back_c] + name_x + img_x + tgt_x + img_n + tgt_n + err_y + err_x
    sent += [img_y(k) for k in range(1, ny)] + [tgt_y(k) for k in range(1, ny)]
    for copy in sent + over_x + y_first + z_first + z_then + y_then + back_x:
        copy.wait_send()


def whole(nx, ny, ng, operands):
    wide = 256
    nzc = ng // CORES
    half = ROWS // CORES
    rows_x = half // nx
    buffers = dict(
        list_v=((1, SLOTS), jnp.int32),
        count_v=((1, 1), jnp.int32),
        w_res_v=((9, 3, 32, 32), BF16),
        w_mid_v=((27, 64, 64), BF16),
        w_down_v=((8, 32, 64), BF16),
        w_up_v=((8, 32, 64), BF16),
        w_in_v=((27, 32), BF16),
        head_v=((3, 32), BF16),
        meta=((nx, 16, 128), BF16),
        xgi=((nx, 32, 128), BF16),
        xgt=((nx, 96, 128), BF16),
        pli=((ny, 16, 128), BF16),
        plt=((ny, 48, 128), BF16),
        yri=((ny, 16, 128), BF16),
        yrt=((ny, 48, 128), BF16),
        mi=((16, 128), BF16),
        mt=((48, 128), BF16),
        hri=((5, 3, 16, 128), BF16),
        hrt=((3, 3, 48, 128), BF16),
        w0=((256, 32), BF16),
        w1=((256, 1024), BF16),
        w1b=((256, 1024), BF16),
        wm=((64, 768), BF16),
        wmb=((64, 768), BF16),
        tcol=((176, wide), BF16),
        tgt=((6, 32, wide), F32),
        h0s=((10, 256, wide), BF16),
        c0=((20, 256, wide), BF16),
        h1s=((8, 256, wide), BF16),
        cd=((8, 256, wide), BF16),
        qs=((6, 64, wide), BF16),
        ss=((6, 256, wide), BF16),
        gls=((6, 32, wide), BF16),
        gss=((6, 256, wide), BF16),
        cg=((6, 256, wide), BF16),
        gds=((4, 64, wide), BF16),
        cr=((8, 256, wide), BF16),
        grs=((4, 256, wide), BF16),
        gas=((2, 256, 128), BF16),
        errs=((6, 32, wide), BF16),
        vec=((ROWS, 128), F32),
        err=((48, 128), BF16),
        rc=((half, 128), F32),
        ac=((half, 128), F32),
        rx=((nx, rows_x, 128), BF16),
        ab=((half, 128), BF16),
        ya=((ny, rows_x // 2, 128), BF16),
        za=((nzc, rows_x // 2, 128), BF16),
        yb=((ny, rows_x // 2, 128), BF16),
        zb=((nzc, rows_x // 2, 128), BF16),
        gx=((nx, rows_x, 128), BF16),
        gc=((nx, rows_x, 128), BF16),
        ey=((ny, 48, 128), BF16),
        em=((nx, 96, 128), BF16),
        ex=((nx, 96, 128), BF16),
    )
    sems = dict(loaded=10)
    for kind, count in (
        ("name", nx),
        ("ix", nx),
        ("tx", nx),
        ("iy", ny),
        ("ty", ny),
        ("in", 14),
        ("tn", 14),
        ("ey", ny),
        ("ex", nx),
        ("c", 2),
        ("x", nx),
        ("ya", ny),
        ("za", nzc),
        ("yb", ny),
        ("zb", nzc),
        ("gx", nx),
    ):
        sems["s_" + kind] = count
        sems["r_" + kind] = count
    names = list(operands) + ["out", "tiles"] + list(buffers) + list(sems) + ["stored"]
    return pl.pallas_call(
        functools.partial(whole_kernel, nx, ny, ng, names),
        out_shape=(
            jax.ShapeDtypeStruct((ROWS, 128), BF16),
            jax.ShapeDtypeStruct((96, 128), BF16),
        ),
        in_specs=[pl.BlockSpec(memory_space=pltpu.MemorySpace.HBM)] * len(operands),
        out_specs=(pl.BlockSpec(memory_space=pltpu.MemorySpace.HBM), VM),
        scratch_shapes=[pltpu.VMEM(shape, dtype) for shape, dtype in buffers.values()]
        + [pltpu.SemaphoreType.DMA((count,)) for count in sems.values()]
        + [pltpu.SemaphoreType.DMA((2, nx))],
        compiler_params=pltpu.CompilerParams(
            collective_id=0, has_side_effects=True, vmem_limit_bytes=56 << 20
        ),
        name="whole",
    )(*operands.values())


def unpack_kernel(
    sums, tiles, err, g_in, g_res, g_down, g_mid, g_up, g_head, lines, vec, sems
):
    ends = (RES, MID, DOWN, INP, USED + 8)
    loads = [
        pltpu.make_async_copy(sums.at[a:b], vec.at[a:b], sems.at[n])
        for n, (a, b) in enumerate(zip(ends[:-1], ends[1:]))
    ]
    load_err = pltpu.make_async_copy(tiles, err, sems.at[4])
    for copy in loads + [load_err]:
        copy.start()
    for t in range(27):
        if t // 3 % 3 != 1:
            g_mid[t] = jnp.zeros((64, 64), F32)
    loads[0].wait()
    for zy in range(9):
        strip = vec[RES + zy * 32 : RES + zy * 32 + 32, :].astype(F32)
        for c in range(3):
            part = strip if c == 0 else pltpu.roll(strip, 128 - 32 * c, 1)
            g_res[zy * 3 + c] = part[:, 0:32]
    loads[1].wait()
    for t in range(27):
        a, b, c = t // 9, t // 3 % 3, t % 3
        if b == 1:
            at = MID + (a * 2 + c // 2) * 64
            part = vec[at : at + 64, :].astype(F32)
            if c % 2:
                part = pltpu.roll(part, 64, 1)
            g_mid[t] = part[:, 0:64]
    loads[2].wait()
    loads[3].wait()
    for pos in range(8):
        quarter = pos & 3
        for at, grad in ((DOWN, g_down), (UP, g_up)):
            part = vec[at + quarter * 32 : at + quarter * 32 + 32, :].astype(F32)
            if pos >> 2:
                part = pltpu.roll(part, 64, 1)
            grad[tap_of(pos)] = part[:, 0:64]
        part = vec[INP + (pos >> 2) * 32 : INP + (pos >> 2) * 32 + 32, :].astype(F32)
        if quarter:
            part = pltpu.roll(part, 128 - 32 * quarter, 1)
        lines[pos] = part
    for t in range(27):
        dz, dy, dx = t // 9, t // 3 % 3, t % 3
        total = None
        for pos in range(8):
            xo, zo, yo = pos >> 2, pos >> 1 & 1, pos & 1
            if 0 <= yo + dy - 1 < 2:
                at = (zo + dz) * 8 + (xo + dx) * 2 + yo + dy - 1
                line = lines[pos, at : at + 1, :]
                total = line if total is None else total + line
        g_in[t : t + 1, :] = total[:, 0:32]
    g_head[...] = vec[HEAD : HEAD + 16, :].astype(F32)[0:3, 0:32]
    load_err.wait()


def unpack(vec, tiles):
    return pl.pallas_call(
        unpack_kernel,
        out_shape=(
            jax.ShapeDtypeStruct((96, 128), BF16),
            jax.ShapeDtypeStruct((27, 32), F32),
            jax.ShapeDtypeStruct((27, 32, 32), F32),
            jax.ShapeDtypeStruct((8, 32, 64), F32),
            jax.ShapeDtypeStruct((27, 64, 64), F32),
            jax.ShapeDtypeStruct((8, 32, 64), F32),
            jax.ShapeDtypeStruct((3, 32), F32),
        ),
        in_specs=[pl.BlockSpec(memory_space=pltpu.MemorySpace.HBM)] * 2,
        out_specs=(VM,) * 7,
        scratch_shapes=[
            pltpu.VMEM((8, 32, 128), F32),
            pltpu.VMEM((ROWS, 128), BF16),
            pltpu.SemaphoreType.DMA((5,)),
        ],
        compiler_params=pltpu.CompilerParams(vmem_limit_bytes=56 << 20),
        name="unpack",
    )(vec, tiles)


def local(
    tile_image, tile_target, owner_counts, tile_list, w_in, w_res, w_down, w_mid, w_up, head_weight
):
    ranks = lax.axis_size("xy")
    ng = lax.axis_size("gz")
    nx, ny = grid_of(ranks)
    operands = dict(
        img=tile_image.reshape(SLOTS * 8, 128),
        target=tile_target.reshape(SLOTS * 24, 128),
        counts=owner_counts,
        tile_list=tile_list.reshape(1, SLOTS),
        w_in=w_in,
        w_res=w_res.reshape(9, 3, 32, 32),
        w_down=jnp.transpose(w_down, (0, 2, 1)),
        w_mid=w_mid,
        w_up=w_up,
        head=head_weight,
    )
    sums, tiles = whole(nx, ny, ng, operands)
    tiles, g_in, g_res, g_down, g_mid, g_up, g_head = unpack(sums, tiles)
    tiles = tiles.reshape(1, 1, SLOTS, 3, 4, 2, 128)
    return (tiles, g_in, g_res, jnp.transpose(g_down, (0, 2, 1)), g_mid, g_up, g_head)


def solution(mesh):
    return jax.shard_map(
        local,
        mesh=mesh,
        in_specs=(
            P("gz", "xy", None, None, None, None),
            P("gz", "xy", None, None, None, None, None),
            P("gz", "xy"),
            P("gz", "xy", None),
            P(),
            P(),
            P(),
            P(),
            P(),
            P(),
        ),
        out_specs=(P("gz", "xy", None, None, None, None, None), P(), P(), P(), P(), P(), P()),
        check_vma=False,
    )
```
